32 devices in a mesh: dp: 16 (over z, y, x), sub: 2 (over core).
Axes of the slice: x: 2, y: 2, z: 4, core: 2. Of those that a mesh axis runs over, the one named last changes fastest.
Arguments:
- item_ids: int32 [16, 512], replicated, may hold values from 0 to 25087, as said below
- lengths: int32 [16], replicated, may hold values from 1 to 512, 6963 in all
- home_row: int32 [25088], replicated, may hold values from 0 to 25087, as said below
- log_freq: float32 [25088], replicated, may hold values from -3 to 0
- item_table: float32 [25088, 256], P('dp'), may hold values from -0.72 to 0.72
- table_first: float32 [25088, 256], P('dp')
- table_second: float32 [25088, 256], P('dp')
- pos_table: float32 [512, 256], P(None, ('dp', 'sub')), may hold values from -0.72 to 0.72
- pos_first: float32 [512, 256], P(None, ('dp', 'sub'))
- pos_second: float32 [512, 256], P(None, ('dp', 'sub'))
- qkv_weight: float32 [256, 768], P(None, ('dp', 'sub')), may hold values from -0.375 to 0.375
- qkv_first: float32 [256, 768], P(None, ('dp', 'sub'))
- qkv_second: float32 [256, 768], P(None, ('dp', 'sub'))
- merge_weight: float32 [256, 256], P(None, ('dp', 'sub')), may hold values from -1.5 to 1.5
- merge_first: float32 [256, 256], P(None, ('dp', 'sub'))
- merge_second: float32 [256, 256], P(None, ('dp', 'sub'))
- widen_weight: float32 [256, 1024], P(None, ('dp', 'sub')), may hold values from -0.375 to 0.375
- widen_first: float32 [256, 1024], P(None, ('dp', 'sub'))
- widen_second: float32 [256, 1024], P(None, ('dp', 'sub'))
- narrow_weight: float32 [1024, 256], P(None, ('dp', 'sub')), may hold values from -0.1875 to 0.1875
- narrow_first: float32 [1024, 256], P(None, ('dp', 'sub'))
- narrow_second: float32 [1024, 256], P(None, ('dp', 'sub'))
- norm_gains: float32 [3, 256], P(None, ('dp', 'sub')), may hold values from 0.5 to 1.5
- gains_first: float32 [3, 256], P(None, ('dp', 'sub'))
- gains_second: float32 [3, 256], P(None, ('dp', 'sub'))
Outputs:
- loss_sum: float32 [], replicated
- event_count: float32 [], replicated
- grad_norm: float32 [], replicated
- table_next: float32 [25088, 256], P('dp')
- table_first_next: float32 [25088, 256], P('dp')
- table_second_next: float32 [25088, 256], P('dp')
- pos_next: float32 [512, 256], P(None, ('dp', 'sub'))
- pos_first_next: float32 [512, 256], P(None, ('dp', 'sub'))
- pos_second_next: float32 [512, 256], P(None, ('dp', 'sub'))
- qkv_next: float32 [256, 768], P(None, ('dp', 'sub'))
- qkv_first_next: float32 [256, 768], P(None, ('dp', 'sub'))
- qkv_second_next: float32 [256, 768], P(None, ('dp', 'sub'))
- merge_next: float32 [256, 256], P(None, ('dp', 'sub'))
- merge_first_next: float32 [256, 256], P(None, ('dp', 'sub'))
- merge_second_next: float32 [256, 256], P(None, ('dp', 'sub'))
- widen_next: float32 [256, 1024], P(None, ('dp', 'sub'))
- widen_first_next: float32 [256, 1024], P(None, ('dp', 'sub'))
- widen_second_next: float32 [256, 1024], P(None, ('dp', 'sub'))
- narrow_next: float32 [1024, 256], P(None, ('dp', 'sub'))
- narrow_first_next: float32 [1024, 256], P(None, ('dp', 'sub'))
- narrow_second_next: float32 [1024, 256], P(None, ('dp', 'sub'))
- gains_next: float32 [3, 256], P(None, ('dp', 'sub'))
- gains_first_next: float32 [3, 256], P(None, ('dp', 'sub'))
- gains_second_next: float32 [3, 256], P(None, ('dp', 'sub'))
The draws below stay inside these ranges and needn't reach their ends.
Inputs may be any that keep to these rules, and one draw needn't show every extreme that they name: `item_ids`: of the slots of one device (the histories of one index of dp, the positions of one index of sub), at most 32 hold items whose table rows one index of dp holds, and some index of dp holds exactly 32 of them. A permutation: item i lives in row home_row[i] of item_table, held by the index home_row[i] // 1568 of dp. History h has its events in its first lengths[h] slots; some history fills all 512.
All inputs are finite; a program needn't handle non-finite values.
Results may differ from the reference program's by a relative error of at most 0.012.
The reference program's roundings to bfloat16 on the way count: a program that leaves them out, or rounds other values in their place, can miss the bound.
Values may be sent and summed in bfloat16 or wider, within the bound.
A program may use at most 384 MiB of HBM per device.

```python
import math
import jax
import jax.numpy as jnp
import numpy as np
from jax import lax

D = 256
HEADS = 8
FF = 1024
SEQ = 512
HIST_DEV = 1
ROWS_DEV = 1568
STEP = 10
ITEMS = 25088
HIST = 16
CAP = 32
N_DP = 16
N_SUB = 2


def grad_scale():
    total_params = ITEMS * D + SEQ * D + 4 * D * D + 2 * D * FF + 3 * D
    return 0.01 / math.sqrt(total_params)


def storage_order(key):
    return jax.random.permutation(jax.random.fold_in(key, 7), ITEMS).astype(jnp.int32)


def draw_home_row(key, part):
    return storage_order(key)


def draw_item_ids(key, part):
    storage = storage_order(key)
    inverse = jnp.argsort(storage, stable=True).astype(jnp.int32)
    tokens_dev = HIST_DEV * SEQ // N_SUB
    owner_pool = jnp.arange(N_DP * CAP, dtype=jnp.int32) // CAP

    def device_rows(dev_key):
        sub_keys = jax.random.split(dev_key, 3)
        shuffled = jax.random.permutation(sub_keys[0], owner_pool)
        chosen = shuffled[0]
        ordering = jnp.argsort((shuffled != chosen).astype(jnp.int32), stable=True)
        owners = jax.random.permutation(sub_keys[1], shuffled[ordering][:tokens_dev])
        row_pick = jax.random.randint(sub_keys[2], (tokens_dev,), 0, ROWS_DEV, dtype=jnp.int32)
        return owners * ROWS_DEV + row_pick
    dev_keys = jax.random.split(jax.random.fold_in(key, 11), N_DP * N_SUB)
    stored = jax.vmap(device_rows)(dev_keys)
    stored = stored.reshape(N_DP, N_SUB, HIST_DEV, SEQ // N_SUB).transpose(0, 2, 1, 3).reshape(HIST, SEQ)
    return inverse[stored]


def first_moment(key, shape, boost):
    return boost * grad_scale() * 0.1 / 0.9 * jax.random.normal(key, shape, jnp.float32)


def second_moment(key, shape, boost):
    base_level = (boost * grad_scale()) ** 2 * 0.001 / 0.999
    return base_level * jnp.exp(jax.random.uniform(key, shape, jnp.float32, math.log(0.5), math.log(8.0)))


def draw_table_first(key, part):
    return first_moment(key, (ITEMS, D), 1.0)


def draw_table_second(key, part):
    return second_moment(key, (ITEMS, D), 1.0)


def draw_pos_first(key, part):
    return first_moment(key, (SEQ, D), 2.0)


def draw_pos_second(key, part):
    return second_moment(key, (SEQ, D), 2.0)


def draw_qkv_first(key, part):
    return first_moment(key, (D, 3 * D), 3.0)


def draw_qkv_second(key, part):
    return second_moment(key, (D, 3 * D), 3.0)


def draw_merge_first(key, part):
    return first_moment(key, (D, D), 3.0)


def draw_merge_second(key, part):
    return second_moment(key, (D, D), 3.0)


def draw_widen_first(key, part):
    return first_moment(key, (D, FF), 3.0)


def draw_widen_second(key, part):
    return second_moment(key, (D, FF), 3.0)


def draw_narrow_first(key, part):
    return first_moment(key, (FF, D), 3.0)


def draw_narrow_second(key, part):
    return second_moment(key, (FF, D), 3.0)


def draw_gains_first(key, part):
    return first_moment(key, (3, D), 10.0)


def draw_gains_second(key, part):
    return second_moment(key, (3, D), 10.0)


def block_scale(stream_key, dims, cuts, least, top_value):
    def one(dim, blocks):
        steps = jax.random.uniform(jax.random.fold_in(jax.random.fold_in(stream_key, 6), dim), (blocks,), jnp.float32, least / len(cuts), top_value / len(cuts))
        return jnp.repeat(jnp.exp(steps), dims[dim] // blocks).reshape((-1,) + (1,) * (len(dims) - dim - 1))

    level = one(*cuts[0])
    for cut in cuts[1:]:
        level = level * one(*cut)
    return level


def length_profile(amount, total, most, skew):
    portions = [(1 << 20) // math.isqrt(rank ** skew) + 1 for rank in range(2, amount + 1)]
    spare, given = total - most - (amount - 1), [1] * (amount - 1)
    while spare > 0:
        movable = [i for i in range(amount - 1) if given[i] < most]
        whole, budget = sum([portions[i] for i in movable]), spare
        for i in movable:
            addition = min(most - given[i], max(1, budget * portions[i] // whole), spare)
            given[i] = given[i] + addition
            spare = spare - addition
    return np.array([most] + given)


def ragged_sizes(own_key, number_of, total, bound, skew):
    if number_of == 2:
        one = jax.random.randint(own_key, (), max(1, total - bound), min(bound, total - 1) + 1)
        return jnp.stack([one, total - one])
    tallies = jnp.asarray(length_profile(number_of, total, bound, skew), jnp.int32)
    pairs = (number_of - 1) // 2
    donor, receiver = tallies[1:1 + 2 * pairs:2], tallies[2:2 + 2 * pairs:2]
    room = jnp.minimum(donor - 1, bound - receiver)
    shifted = jax.random.randint(jax.random.fold_in(own_key, 1), (pairs,), 0, 1 << 20) % (room + 1)
    tallies = tallies.at[1:1 + 2 * pairs:2].set(donor - shifted).at[2:2 + 2 * pairs:2].set(receiver + shifted)
    return tallies[jax.random.permutation(jax.random.fold_in(own_key, 2), number_of)]


def centred(rng, shape, width, bound, cuts=(), kind=jnp.bfloat16):
    entries = jax.random.normal(rng, shape, jnp.float32) * width
    if len(cuts) > 0:
        entries = block_scale(rng, shape, cuts, -0.22, 0.18) * entries
    return jnp.clip(entries, min=-bound, max=bound).astype(kind)


def setup_inputs(seed: int = 0) -> dict:
    keys = jax.random.split(jax.random.key(seed), 26)
    item_ids = draw_item_ids(jax.random.fold_in(keys[25], 71), 0)
    lengths = ragged_sizes(keys[1], HIST, HIST * SEQ * 85 // 100, SEQ, 2).astype(jnp.int32)
    home_row = draw_home_row(jax.random.fold_in(keys[25], 71), 0)
    log_freq = jnp.clip(jax.random.uniform(keys[3], (ITEMS,), jnp.float32, -3.0, 0.0), -3.0, 0.0)
    item_table = centred(keys[4], (ITEMS, D), 0.12, 0.72, ((0, 16),), jnp.float32)
    table_first = draw_table_first(jax.random.fold_in(keys[25], 71), 0)
    table_second = draw_table_second(jax.random.fold_in(keys[25], 71), 0)
    pos_table = centred(keys[7], (SEQ, D), 0.12, 0.72, ((1, 32),), jnp.float32)
    pos_first = draw_pos_first(jax.random.fold_in(keys[25], 71), 0)
    pos_second = draw_pos_second(jax.random.fold_in(keys[25], 71), 0)
    qkv_weight = centred(keys[10], (D, 3 * D), D ** -0.5, 0.375, ((1, 32),), jnp.float32)
    qkv_first = draw_qkv_first(jax.random.fold_in(keys[25], 71), 0)
    qkv_second = draw_qkv_second(jax.random.fold_in(keys[25], 71), 0)
    merge_weight = centred(keys[13], (D, D), (D // 16) ** -0.5, 1.5, ((1, 32),), jnp.float32)
    merge_first = draw_merge_first(jax.random.fold_in(keys[25], 71), 0)
    merge_second = draw_merge_second(jax.random.fold_in(keys[25], 71), 0)
    widen_weight = centred(keys[16], (D, FF), D ** -0.5, 0.375, ((1, 32),), jnp.float32)
    widen_first = draw_widen_first(jax.random.fold_in(keys[25], 71), 0)
    widen_second = draw_widen_second(jax.random.fold_in(keys[25], 71), 0)
    narrow_weight = centred(keys[19], (FF, D), FF ** -0.5, 0.1875, ((1, 32),), jnp.float32)
    narrow_first = draw_narrow_first(jax.random.fold_in(keys[25], 71), 0)
    narrow_second = draw_narrow_second(jax.random.fold_in(keys[25], 71), 0)
    norm_gains = jnp.clip(1.0 + 0.1 * jax.random.normal(keys[22], (3, D), jnp.float32), 0.5, 1.5)
    gains_first = draw_gains_first(jax.random.fold_in(keys[25], 71), 0)
    gains_second = draw_gains_second(jax.random.fold_in(keys[25], 71), 0)
    return dict(item_ids=item_ids, lengths=lengths, home_row=home_row, log_freq=log_freq, item_table=item_table, table_first=table_first, table_second=table_second, pos_table=pos_table, pos_first=pos_first, pos_second=pos_second, qkv_weight=qkv_weight, qkv_first=qkv_first, qkv_second=qkv_second, merge_weight=merge_weight, merge_first=merge_first, merge_second=merge_second, widen_weight=widen_weight, widen_first=widen_first, widen_second=widen_second, narrow_weight=narrow_weight, narrow_first=narrow_first, narrow_second=narrow_second, norm_gains=norm_gains, gains_first=gains_first, gains_second=gains_second)


@jax.custom_vjp
def low(v):
    return lax.optimization_barrier(v.astype(jnp.bfloat16)).astype(jnp.float32)

@jax.custom_vjp
def low_back(v):
    return v

def low_keep(v):
    return (low(v), None)

def low_pass(kept, grad):
    return (grad,)

def back_keep(v):
    return (v, None)

def back_low(kept, grad):
    return (low(grad),)
low.defvjp(low_keep, low_pass)
low_back.defvjp(back_keep, back_low)
precise = lax.Precision.HIGHEST
norm_eps = 1e-06
beta_one = 0.9
beta_two = 0.999
adam_eps = 1e-08
decay_rate = 0.01
learn_rate = 0.1
gain_rate = 0.5
clip_limit = 0.01
big_negative = -1e+30

def rms_scale(values, gain_row):
    inverse = lax.rsqrt(lax.optimization_barrier(jnp.mean(values * values, axis=-1, keepdims=True)) + norm_eps)
    return values * inverse * gain_row

def history_group(embedded, dense_w):
    pos_low, qkv_low, merge_low, widen_low, narrow_low, gains_low = dense_w
    group_size, seq_len, model_width = embedded.shape
    head_dim = model_width // HEADS
    resid_zero = embedded + pos_low[None]
    input_one = low(rms_scale(resid_zero, gains_low[0]))
    qkv_all = low_back(low(jnp.einsum('gtd,de->gte', input_one, qkv_low, precision=precise)))
    qkv_parts = qkv_all.reshape(group_size, seq_len, 3, HEADS, head_dim)
    queries, keys_all, values_all = (qkv_parts[:, :, 0], qkv_parts[:, :, 1], qkv_parts[:, :, 2])
    scores = low_back(jnp.einsum('gqhe,gkhe->ghqk', queries, keys_all, precision=precise) * head_dim ** (-0.5))
    allowed = jnp.arange(seq_len)[None, :] <= jnp.arange(seq_len)[:, None]
    scores = jnp.where(allowed, scores, big_negative)
    attn_prob = low(jax.nn.softmax(scores, axis=-1))
    attended = jnp.einsum('ghqk,gkhe->gqhe', attn_prob, values_all, precision=precise)
    attended = low_back(low(attended)).reshape(group_size, seq_len, model_width)
    resid_one = resid_zero + low_back(jnp.einsum('gtd,de->gte', attended, merge_low, precision=precise))
    input_two = low(rms_scale(resid_one, gains_low[1]))
    hidden_pre = low_back(jnp.einsum('gtd,df->gtf', input_two, widen_low, precision=precise))
    hidden_act = low(jax.nn.gelu(hidden_pre))
    resid_two = resid_one + low_back(jnp.einsum('gtf,fd->gtd', hidden_act, narrow_low, precision=precise))
    return low(rms_scale(resid_two, gains_low[2]))

def step_loss(item_table, pos_table, qkv_weight, merge_weight, widen_weight, narrow_weight, norm_gains, item_ids, lengths, home_row, log_freq):
    dense_w = (low(pos_table), low(qkv_weight), low(merge_weight), low(widen_weight), low(narrow_weight), low(norm_gains))
    embedded = low(item_table[home_row[item_ids]])
    hist_all, seq_len, model_width = embedded.shape
    all_rows = hist_all * seq_len
    groups = embedded.reshape(hist_all // 8, 8, seq_len, model_width)
    user_vecs = lax.map(jax.checkpoint(lambda block_in: history_group(block_in, dense_w)), groups).reshape(all_rows, model_width)
    candidates = embedded.reshape(all_rows, model_width)
    position = jnp.arange(seq_len)[None, :]
    span = lengths[:, None]
    valid_cand = ((position >= 1) & (position < span)).reshape(-1)
    event_mask = (position + 1 < span).astype(jnp.float32).reshape(-1)
    targets = jnp.minimum(jnp.arange(all_rows) + 1, all_rows - 1).astype(jnp.int32)
    correction = log_freq[item_ids].reshape(-1)
    block_rows = min(2048, all_rows)

    def block_loss(inputs):
        user_rows, mask_rows, target_rows = inputs
        logits = low_back(jnp.dot(user_rows, candidates.T, precision=precise)) - correction[None, :]
        logits = jnp.where(valid_cand[None, :], logits, big_negative)
        row_peak = lax.optimization_barrier(jnp.max(logits, axis=1, keepdims=True))
        log_total = row_peak[:, 0] + jnp.log(lax.optimization_barrier(jnp.sum(jnp.exp(logits - row_peak), axis=1)))
        target_hit = jnp.take_along_axis(logits, target_rows[:, None], axis=1)[:, 0]
        return jnp.sum(mask_rows * (log_total - target_hit))
    partial_sums = lax.map(jax.checkpoint(block_loss), (user_vecs.reshape(-1, block_rows, model_width), event_mask.reshape(-1, block_rows), targets.reshape(-1, block_rows)))
    loss_total = jnp.sum(partial_sums)
    event_count = jnp.sum(lengths - 1).astype(jnp.float32)
    return (loss_total / event_count, (loss_total, event_count))

def adamw(weight, moment_one, moment_two, gradient, rate):
    moment_one = beta_one * moment_one + (1.0 - beta_one) * gradient
    moment_two = beta_two * moment_two + (1.0 - beta_two) * gradient * gradient
    fix_one = 1.0 - beta_one ** STEP
    fix_two = 1.0 - beta_two ** STEP
    update = moment_one / fix_one / (jnp.sqrt(moment_two / fix_two) + adam_eps) + decay_rate * weight
    return (weight - rate * update, moment_one, moment_two)

def reference(item_ids, lengths, home_row, log_freq, item_table, table_first, table_second, pos_table, pos_first, pos_second, qkv_weight, qkv_first, qkv_second, merge_weight, merge_first, merge_second, widen_weight, widen_first, widen_second, narrow_weight, narrow_first, narrow_second, norm_gains, gains_first, gains_second):
    params = (item_table, pos_table, qkv_weight, merge_weight, widen_weight, narrow_weight, norm_gains)

    def objective(*weights):
        return step_loss(*weights, item_ids, lengths, home_row, log_freq)
    mean_loss, pull_back, extras = jax.vjp(objective, *params, has_aux=True)
    loss_total, event_count = extras
    grads = pull_back(jnp.ones_like(mean_loss))
    square_sum = sum((jnp.sum(gradient * gradient) for gradient in grads))
    grad_norm = jnp.sqrt(square_sum)
    factor = jnp.minimum(1.0, clip_limit / grad_norm)
    firsts = (table_first, pos_first, qkv_first, merge_first, widen_first, narrow_first, gains_first)
    seconds = (table_second, pos_second, qkv_second, merge_second, widen_second, narrow_second, gains_second)
    rates = (learn_rate,) * 6 + (gain_rate,)
    results = [loss_total, event_count, grad_norm]
    for weight, moment_one, moment_two, gradient, rate in zip(params, firsts, seconds, grads, rates):
        results.extend(adamw(weight, moment_one, moment_two, gradient * factor, rate))
    return tuple(results)
```

```python
import functools
import math
import types

import jax
import jax.numpy as jnp
from jax import lax
from jax.experimental import pallas as pl
from jax.experimental.pallas import tpu as pltpu
from jax.sharding import PartitionSpec as P

HEADS = 8
STEP = 10


norm_eps = 1e-06
beta_one = 0.9
beta_two = 0.999
adam_eps = 1e-08
decay_rate = 0.01
learn_rate = 0.1
gain_rate = 0.5
clip_limit = 0.01
big_negative = -1e30
block_cols = 4096


def dot_plain(left_mat, right_mat):
    return jnp.dot(left_mat, right_mat, preferred_element_type=jnp.float32)


def dot_left_t(left_mat, right_mat):
    return lax.dot_general(
        left_mat, right_mat, (((0,), (0,)), ((), ())), preferred_element_type=jnp.float32
    )


def dot_right_t(left_mat, right_mat):
    return lax.dot_general(
        left_mat, right_mat, (((1,), (1,)), ((), ())), preferred_element_type=jnp.float32
    )


def rms_forward(values, gain_row):
    inverse = lax.rsqrt(jnp.mean(values * values, axis=-1, keepdims=True) + norm_eps)
    return (values * inverse * gain_row, inverse)


def rms_backward(upstream, values, inverse, gain_row):
    unit_vals = values * inverse
    gain_grad = jnp.sum(upstream * unit_vals, axis=0)
    scaled = upstream * gain_row
    inner_mean = jnp.mean(scaled * unit_vals, axis=-1, keepdims=True)
    return (inverse * (scaled - unit_vals * inner_mean), gain_grad)


def head_scores(queries, keys_all, allowed):
    scaling = queries.shape[-1] ** (-0.5)
    plain_scores = (
        jnp.einsum("bqhe,bkhe->bhqk", queries, keys_all, preferred_element_type=jnp.float32)
        * scaling
    )
    return jnp.where(allowed, plain_scores, big_negative)


def target_of(indices, slice_len, tokens_dev):
    within = indices % slice_len
    return jnp.where(within + 1 < slice_len, indices + 1, indices - within + tokens_dev)


def logits_for(user_rows, cand_rows, corr_rows, valid_rows):
    logits = dot_right_t(user_rows, cand_rows) - corr_rows[None, :]
    return jnp.where(valid_rows[None, :], logits, big_negative)


def coefficient(logits, log_total, weights, columns, targets):
    hits = (columns[None, :] == targets[:, None]).astype(jnp.float32)
    return (weights[:, None] * (jnp.exp(logits - log_total[:, None]) - hits)).astype(jnp.bfloat16)


def block_forward(resid_zero, dense_w, allowed, hist_local):
    qkv_full, merge_full, widen_full, narrow_full, gains_full = dense_w
    gain_float = gains_full.astype(jnp.float32)
    tokens_dev, model_width = resid_zero.shape
    normed_one, inverse_one = rms_forward(resid_zero, gain_float[0])
    input_one = normed_one.astype(jnp.bfloat16)
    qkv_parts = (
        dot_plain(input_one, qkv_full)
        .astype(jnp.bfloat16)
        .reshape(hist_local, -1, 3, HEADS, model_width // HEADS)
    )
    queries = qkv_parts[:, :, 0]
    keys_all, values_all = (
        lax.all_gather(qkv_parts[:, :, 1], "sub", axis=1, tiled=True),
        lax.all_gather(qkv_parts[:, :, 2], "sub", axis=1, tiled=True),
    )
    scores = head_scores(queries, keys_all, allowed)
    row_peak = jnp.max(scores, axis=-1, keepdims=True)
    expo_vals = jnp.exp(scores - row_peak)
    row_total = jnp.sum(expo_vals, axis=-1, keepdims=True)
    log_total = row_peak + jnp.log(row_total)
    attn_prob = (expo_vals / row_total).astype(jnp.bfloat16)
    attended = jnp.einsum(
        "bhqk,bkhe->bqhe", attn_prob, values_all, preferred_element_type=jnp.float32
    )
    attended = attended.astype(jnp.bfloat16).reshape(tokens_dev, model_width)
    resid_one = resid_zero + dot_plain(attended, merge_full)
    normed_two, inverse_two = rms_forward(resid_one, gain_float[1])
    input_two = normed_two.astype(jnp.bfloat16)
    hidden_pre = dot_plain(input_two, widen_full)
    hidden_act = jax.nn.gelu(hidden_pre).astype(jnp.bfloat16)
    resid_two = resid_one + dot_plain(hidden_act, narrow_full)
    normed_three, inverse_three = rms_forward(resid_two, gain_float[2])
    kept = (
        resid_zero,
        inverse_one,
        input_one,
        queries,
        keys_all,
        values_all,
        log_total,
        attended,
        resid_one,
        inverse_two,
        input_two,
        hidden_pre,
        hidden_act,
        resid_two,
        inverse_three,
    )
    return (normed_three.astype(jnp.bfloat16), kept)


def block_backward(user_grad, kept, dense_w, allowed):
    (
        resid_zero,
        inverse_one,
        input_one,
        queries,
        keys_all,
        values_all,
        log_total,
        attended,
        resid_one,
        inverse_two,
        input_two,
        hidden_pre,
        hidden_act,
        resid_two,
        inverse_three,
    ) = kept
    qkv_full, merge_full, widen_full, narrow_full, gains_full = dense_w
    gain_float = gains_full.astype(jnp.float32)
    tokens_dev, model_width = resid_zero.shape
    head_dim = queries.shape[-1]
    grad_two, gain_three = rms_backward(user_grad, resid_two, inverse_three, gain_float[2])
    branch_two = grad_two.astype(jnp.bfloat16)
    narrow_grad = dot_left_t(hidden_act, branch_two)
    hidden_grad = dot_right_t(branch_two, narrow_full)
    pre_grad = jax.vjp(jax.nn.gelu, hidden_pre)[1](hidden_grad)[0].astype(jnp.bfloat16)
    widen_grad = dot_left_t(input_two, pre_grad)
    from_two, gain_two = rms_backward(
        dot_right_t(pre_grad, widen_full), resid_one, inverse_two, gain_float[1]
    )
    grad_one = grad_two + from_two
    branch_one = grad_one.astype(jnp.bfloat16)
    merge_grad = dot_left_t(attended, branch_one)
    mixed_grad = dot_right_t(branch_one, merge_full).astype(jnp.bfloat16).reshape(queries.shape)
    scores = head_scores(queries, keys_all, allowed)
    attn_prob = jnp.exp(scores - log_total)
    prob_grad = jnp.einsum(
        "bqhe,bkhe->bhqk", mixed_grad, values_all, preferred_element_type=jnp.float32
    )
    score_grad = attn_prob * (prob_grad - jnp.sum(attn_prob * prob_grad, axis=-1, keepdims=True))
    score_grad = score_grad.astype(jnp.bfloat16)
    scaling = head_dim ** (-0.5)
    query_grad = (
        jnp.einsum("bhqk,bkhe->bqhe", score_grad, keys_all, preferred_element_type=jnp.float32)
        * scaling
    )
    keys_grad = (
        jnp.einsum("bhqk,bqhe->bkhe", score_grad, queries, preferred_element_type=jnp.float32)
        * scaling
    )
    values_grad = jnp.einsum(
        "bhqk,bqhe->bkhe",
        attn_prob.astype(jnp.bfloat16),
        mixed_grad,
        preferred_element_type=jnp.float32,
    )
    key_own, value_own = (
        lax.psum_scatter(
            keys_grad.astype(jnp.bfloat16), "sub", scatter_dimension=1, tiled=True
        ).astype(jnp.float32),
        lax.psum_scatter(
            values_grad.astype(jnp.bfloat16), "sub", scatter_dimension=1, tiled=True
        ).astype(jnp.float32),
    )
    qkv_grad = (
        jnp.stack([query_grad, key_own, value_own], axis=2)
        .astype(jnp.bfloat16)
        .reshape(tokens_dev, 3 * model_width)
    )
    qkv_wgrad = dot_left_t(input_one, qkv_grad)
    from_one, gain_one = rms_backward(
        dot_right_t(qkv_grad, qkv_full), resid_zero, inverse_one, gain_float[0]
    )
    gain_grads = jnp.stack([gain_one, gain_two, gain_three])
    return (grad_one + from_one, (qkv_wgrad, merge_grad, widen_grad, narrow_grad, gain_grads))


def adamw(weight, moment_one, moment_two, gradient, rate):
    moment_one = beta_one * moment_one + (1.0 - beta_one) * gradient
    moment_two = beta_two * moment_two + (1.0 - beta_two) * gradient * gradient
    fix_one = 1.0 - beta_one**STEP
    fix_two = 1.0 - beta_two**STEP
    update = (
        moment_one / fix_one / (jnp.sqrt(moment_two / fix_two) + adam_eps) + decay_rate * weight
    )
    return (weight - rate * update, moment_one, moment_two)


def body(
    item_ids,
    lengths,
    home_row,
    log_freq,
    item_table,
    table_first,
    table_second,
    pos_table,
    pos_first,
    pos_second,
    qkv_weight,
    qkv_first,
    qkv_second,
    merge_weight,
    merge_first,
    merge_second,
    widen_weight,
    widen_first,
    widen_second,
    narrow_weight,
    narrow_first,
    narrow_second,
    norm_gains,
    gains_first,
    gains_second,
):
    dp_count = lax.axis_size("dp")
    sub_count = lax.axis_size("sub")
    dp_index = lax.axis_index("dp")
    sub_index = lax.axis_index("sub")
    rows_dev, model_width = item_table.shape
    hist_local = item_ids.shape[0] // dp_count
    seq_len = item_ids.shape[1]
    slice_len = seq_len // sub_count
    tokens_dev = hist_local * slice_len
    capacity = max(2, (2 * tokens_dev + dp_count - 1) // dp_count)
    all_tokens = dp_count * sub_count * tokens_dev
    pos_full, qkv_full, merge_full, widen_full, narrow_full, gains_full = (
        lax.all_gather(pos_table.astype(jnp.bfloat16), ("dp", "sub"), axis=1, tiled=True),
        lax.all_gather(qkv_weight.astype(jnp.bfloat16), ("dp", "sub"), axis=1, tiled=True),
        lax.all_gather(merge_weight.astype(jnp.bfloat16), ("dp", "sub"), axis=1, tiled=True),
        lax.all_gather(widen_weight.astype(jnp.bfloat16), ("dp", "sub"), axis=1, tiled=True),
        lax.all_gather(narrow_weight.astype(jnp.bfloat16), ("dp", "sub"), axis=1, tiled=True),
        lax.all_gather(norm_gains.astype(jnp.bfloat16), ("dp", "sub"), axis=1, tiled=True),
    )
    dense_w = (qkv_full, merge_full, widen_full, narrow_full, gains_full)
    own_items = lax.dynamic_slice(
        item_ids, (dp_index * hist_local, sub_index * slice_len), (hist_local, slice_len)
    ).reshape(tokens_dev)
    stored_at = home_row[own_items]
    owner_dev = stored_at // rows_dev
    local_row = stored_at % rows_dev
    owner_hot = (owner_dev[:, None] == jnp.arange(dp_count, dtype=jnp.int32)[None, :]).astype(
        jnp.int32
    )
    owner_rank = jnp.sum(jnp.cumsum(owner_hot, axis=0) * owner_hot, axis=1) - 1
    slot_index = owner_dev * capacity + owner_rank
    request = (
        jnp.zeros((dp_count * capacity,), jnp.int32)
        .at[slot_index]
        .set(local_row)
        .reshape(dp_count, capacity)
    )
    arrived = lax.all_to_all(request, "dp", split_axis=0, concat_axis=0, tiled=True)
    found_rows = item_table[arrived].astype(jnp.bfloat16)
    arrived_rows = lax.all_to_all(found_rows, "dp", split_axis=0, concat_axis=0, tiled=True)
    embedded = arrived_rows.reshape(dp_count * capacity, model_width)[slot_index]
    pos_rows = lax.dynamic_slice_in_dim(pos_full, sub_index * slice_len, slice_len, 0).astype(
        jnp.float32
    )
    resid_zero = (
        embedded.astype(jnp.float32).reshape(hist_local, slice_len, model_width) + pos_rows[None]
    ).reshape(tokens_dev, model_width)
    query_pos = sub_index * slice_len + jnp.arange(slice_len)
    allowed = jnp.arange(seq_len)[None, :] <= query_pos[:, None]
    user_vecs, kept = block_forward(resid_zero, dense_w, allowed, hist_local)
    candidates = lax.all_gather(embedded, ("dp", "sub"), axis=0, tiled=True)
    layout = (dp_count, hist_local, sub_count, slice_len)

    def by_device(values):
        return values.reshape(layout).transpose(0, 2, 1, 3).reshape(all_tokens)

    all_items = by_device(item_ids)
    all_pos = by_device(
        jnp.broadcast_to(jnp.arange(seq_len, dtype=jnp.int32)[None, :], item_ids.shape)
    )
    all_len = by_device(jnp.broadcast_to(lengths[:, None], item_ids.shape))
    valid_all = (all_pos >= 1) & (all_pos < all_len)
    correction = log_freq[all_items]
    base_index = (dp_index * sub_count + sub_index) * tokens_dev
    own_index = base_index + jnp.arange(tokens_dev)
    own_pos = lax.dynamic_slice_in_dim(all_pos, base_index, tokens_dev)
    own_len = lax.dynamic_slice_in_dim(all_len, base_index, tokens_dev)
    event_count = jnp.sum(lengths - 1).astype(jnp.float32)
    valid_rows = (own_pos + 1 < own_len).astype(jnp.float32)
    row_weight = valid_rows / event_count
    targets = target_of(own_index, slice_len, tokens_dev)
    col_block = min(block_cols, all_tokens)
    starts = jnp.arange(all_tokens // col_block) * col_block

    def block_logits(block_start):
        cand_rows = lax.dynamic_slice_in_dim(candidates, block_start, col_block, 0)
        corr_rows = lax.dynamic_slice_in_dim(correction, block_start, col_block)
        valid_cols = lax.dynamic_slice_in_dim(valid_all, block_start, col_block)
        return (
            cand_rows,
            logits_for(user_vecs, cand_rows, corr_rows, valid_cols),
            block_start + jnp.arange(col_block),
        )

    def forward_block(running, block_start):
        row_peak, row_total, target_logit = running
        cand_rows, logits, columns = block_logits(block_start)
        new_peak = jnp.maximum(row_peak, jnp.max(logits, axis=1))
        row_total = row_total * jnp.exp(row_peak - new_peak) + jnp.sum(
            jnp.exp(logits - new_peak[:, None]), axis=1
        )
        target_logit = target_logit + jnp.sum(
            jnp.where(columns[None, :] == targets[:, None], logits, 0.0), axis=1
        )
        return ((new_peak, row_total, target_logit), None)

    start_state = (
        jnp.full((tokens_dev,), big_negative, jnp.float32),
        jnp.zeros((tokens_dev,), jnp.float32),
        jnp.zeros((tokens_dev,), jnp.float32),
    )
    (row_peak, row_total, target_logit), _ = lax.scan(forward_block, start_state, starts)
    log_total = row_peak + jnp.log(row_total)
    loss_local = jnp.sum(valid_rows * (log_total - target_logit))

    def user_block(running, block_start):
        cand_rows, logits, columns = block_logits(block_start)
        coeffs = coefficient(logits, log_total, row_weight, columns, targets)
        return (running + dot_plain(coeffs, cand_rows), None)

    user_grad, _ = lax.scan(user_block, jnp.zeros((tokens_dev, model_width), jnp.float32), starts)
    step_rows = math.gcd(tokens_dev * lax.axis_size(("dp", "sub")), max(block_cols, tokens_dev))

    def one_block(offset):
        cand_rows = lax.dynamic_slice_in_dim(candidates, offset, step_rows, 0)
        corr_rows = lax.dynamic_slice_in_dim(correction, offset, step_rows)
        valid_cols = lax.dynamic_slice_in_dim(valid_all, offset, step_rows)
        logits = logits_for(user_vecs, cand_rows, corr_rows, valid_cols)
        coeffs = coefficient(logits, log_total, row_weight, offset + jnp.arange(step_rows), targets)
        return dot_left_t(coeffs, user_vecs)

    pieces = lax.map(
        one_block, jnp.arange(tokens_dev * lax.axis_size(("dp", "sub")) // step_rows) * step_rows
    )
    cand_grad = lax.psum_scatter(
        pieces.reshape(tokens_dev * lax.axis_size(("dp", "sub")), model_width),
        ("dp", "sub"),
        scatter_dimension=0,
        tiled=True,
    )
    resid_grad, weight_grads = block_backward(user_grad, kept, dense_w, allowed)
    qkv_wgrad, merge_grad, widen_grad, narrow_grad, gain_grads = weight_grads
    emb_grad = resid_grad + cand_grad
    pos_rows_grad = jnp.sum(resid_grad.reshape(hist_local, slice_len, model_width), axis=0)
    pos_grad = lax.dynamic_update_slice_in_dim(
        jnp.zeros((seq_len, model_width), jnp.float32), pos_rows_grad, sub_index * slice_len, 0
    )
    outgoing = (
        jnp.zeros((dp_count * capacity, model_width), jnp.float32).at[slot_index].set(emb_grad)
    )
    incoming = lax.all_to_all(
        outgoing.reshape(dp_count, capacity, model_width),
        "dp",
        split_axis=0,
        concat_axis=0,
        tiled=True,
    )
    incoming_rows = incoming.reshape(-1, model_width)
    arrived_flat = arrived.reshape(-1)
    plane_grad = jnp.zeros((rows_dev, model_width), jnp.float32).at[arrived_flat].add(incoming_rows)
    table_grad = lax.psum(plane_grad, "sub")
    shard_grads = (
        lax.psum_scatter(pos_grad, ("dp", "sub"), scatter_dimension=1, tiled=True),
        lax.psum_scatter(qkv_wgrad, ("dp", "sub"), scatter_dimension=1, tiled=True),
        lax.psum_scatter(merge_grad, ("dp", "sub"), scatter_dimension=1, tiled=True),
        lax.psum_scatter(widen_grad, ("dp", "sub"), scatter_dimension=1, tiled=True),
        lax.psum_scatter(narrow_grad, ("dp", "sub"), scatter_dimension=1, tiled=True),
        lax.psum_scatter(gain_grads, ("dp", "sub"), scatter_dimension=1, tiled=True),
    )
    square_part = sum((jnp.sum(gradient * gradient) for gradient in shard_grads))
    square_part = square_part + jnp.where(sub_index == 0, jnp.sum(table_grad * table_grad), 0.0)
    loss_sum, square_sum = lax.psum((loss_local, square_part), ("dp", "sub"))
    grad_norm = jnp.sqrt(square_sum)
    factor = jnp.minimum(1.0, clip_limit / grad_norm)
    masters = (
        item_table,
        pos_table,
        qkv_weight,
        merge_weight,
        widen_weight,
        narrow_weight,
        norm_gains,
    )
    firsts = (
        table_first,
        pos_first,
        qkv_first,
        merge_first,
        widen_first,
        narrow_first,
        gains_first,
    )
    seconds = (
        table_second,
        pos_second,
        qkv_second,
        merge_second,
        widen_second,
        narrow_second,
        gains_second,
    )
    rates = (learn_rate,) * 6 + (gain_rate,)
    all_grads = (table_grad,) + tuple(shard_grads)
    results = [loss_sum, event_count, grad_norm]
    for weight, moment_one, moment_two, gradient, rate in zip(
        masters, firsts, seconds, all_grads, rates
    ):
        results.extend(adamw(weight, moment_one, moment_two, gradient * factor, rate))
    return tuple(results)


MESH_ID = pl.DeviceIdType.MESH
FF_CHUNK = 256


def dot_nn(left, right):
    return lax.dot_general(
        left, right, (((1,), (0,)), ((), ())), preferred_element_type=jnp.float32
    )


def dot_nt(left, right):
    return lax.dot_general(
        left, right, (((1,), (1,)), ((), ())), preferred_element_type=jnp.float32
    )


def dot_tn(left, right):
    return lax.dot_general(
        left, right, (((0,), (0,)), ((), ())), preferred_element_type=jnp.float32
    )


def low(values):
    return values.astype(jnp.bfloat16)


def wide(values):
    return values.astype(jnp.float32)


def iota_of(shape, axis):
    return lax.broadcasted_iota(jnp.int32, shape, axis)


def flip(index, bits):
    total = 0
    for power in (1, 2, 4, 8):
        a = lax.rem(lax.div(index, power), 2)
        b = (bits // power) % 2 if isinstance(bits, int) else lax.rem(lax.div(bits, power), 2)
        total = total + power * (a + b - 2 * a * b)
    return total


def arrival_order(levels):
    above = range(1, levels)
    return (
        [(0, 0), (0, 1), (0, 2)]
        + [(level, 0) for level in above]
        + [(0, 3)]
        + [(level, corner) for level in above for corner in (1, 2)]
        + [(level, 3) for level in above]
    )


class Place:
    def __init__(self, chips):
        self.chips = chips
        self.chip = lax.axis_index("dp")
        self.core = lax.axis_index("sub")
        self.level = lax.div(self.chip, 4)
        self.corner = lax.rem(self.chip, 4)
        self.near_x = self.level * 4 + flip(self.corner, 1)
        self.near_y = self.level * 4 + flip(self.corner, 2)

    def way(self, step):
        order = arrival_order(self.chips // 4)
        if isinstance(step, int):
            return order[step]
        return tuple(
            sum(jnp.where(step == i, place[axis], 0) for i, place in enumerate(order) if place[axis])
            for axis in range(2)
        )

    def relative(self, step):
        level, corner = self.way(step)
        return flip(self.level, level) * 4 + flip(self.corner, corner)


def remote(src, dst, send, recv, chip, core):
    return pltpu.make_async_remote_copy(
        src_ref=src,
        dst_ref=dst,
        send_sem=send,
        recv_sem=recv,
        device_id=(chip, core),
        device_id_type=MESH_ID,
    )


class Gather:
    def __init__(self, place, buf, send, recv):
        self.place, self.buf, self.send, self.recv = place, buf, send, recv
        self.levels = place.chips // 4
        self.passed = 1

    def copy(self, block, sem, chip, core):
        return remote(
            self.buf.at[block], self.buf.at[block], self.send.at[sem], self.recv.at[block], chip, core
        )

    def block(self, step, other=False):
        place = self.place
        return place.relative(step) * 2 + (1 - place.core if other else place.core)

    def send_on(self, step, action):
        place = self.place
        block = self.block(step)
        action(self.copy(block, step * 3, place.chip, 1 - place.core))

        def to_x():
            action(self.copy(block, step * 3 + 1, place.near_x, place.core))

        def to_y():
            action(self.copy(block, step * 3 + 2, place.near_y, place.core))

        level, corner = place.way(step)
        if corner == 0:
            to_x()
            to_y()
        elif corner == 1 and level % 2 == 0:
            to_y()
        elif corner == 2 and level % 2 == 1:
            to_x()

    def along_z(self, action):
        place = self.place
        block = self.block(0)
        for step in range(1, self.levels):
            chip = flip(place.level, step) * 4 + place.corner
            action(self.copy(block, place.chips * 3 + step - 1, chip, place.core))

    def start(self):
        self.along_z(lambda copy: copy.start())
        self.send_on(0, lambda copy: copy.start())

    def arrived(self, step, other=False):
        place = self.place
        self.copy(self.block(step, other), 0, place.chip, 1 - place.core).wait_recv()

    def pass_on(self, step):
        self.arrived(step)
        self.send_on(step, lambda copy: copy.start())

    def advance(self, count):
        for _ in range(min(count, self.place.chips - self.passed)):
            self.pass_on(self.passed)
            self.passed += 1

    def complete(self):
        self.advance(self.place.chips)
        for step in range(self.place.chips):
            self.arrived(step, other=True)

    def sent(self):
        self.along_z(lambda copy: copy.wait_send())
        for step in range(self.place.chips):
            self.send_on(step, lambda copy: copy.wait_send())

    @staticmethod
    def sends(chips):
        return chips * 3 + chips // 4 - 1


class Spread:
    def __init__(self, place, buf, send, recv):
        self.place, self.buf, self.send, self.recv = place, buf, send, recv
        self.me, self.count = place.chip * 2 + place.core, place.chips * 2

    def copy(self, other, at):
        return remote(
            self.buf.at[at], self.buf.at[at], self.send.at[other], self.recv.at[at],
            lax.div(other, 2), lax.rem(other, 2),
        )

    def each(self, action):
        def step(index, carry):
            action(lax.rem(self.me + index, self.count))
            return carry

        lax.fori_loop(1, self.count, step, 0)

    def start(self):
        self.each(lambda other: self.copy(other, self.me).start())

    def arrived(self):
        self.each(lambda other: self.copy(other, other).wait_recv())

    def sent(self):
        self.each(lambda other: self.copy(other, self.me).wait_send())


class Scatter:
    def __init__(self, place, src, dst, send, recv):
        self.place, self.src, self.dst, self.send, self.recv = place, src, dst, send, recv

    def copy(self, to, at):
        place = self.place
        return remote(
            self.src.at[to] if self.src is not None else self.dst.at[place.chip],
            self.dst.at[at],
            self.send.at[to],
            self.recv.at[at],
            to,
            place.core,
        )

    def each(self, action):
        place = self.place

        def step(index, carry):
            action(lax.rem(place.chip + index, place.chips))
            return carry

        lax.fori_loop(1, place.chips, step, 0)

    def start(self):
        self.each(lambda chip: self.copy(chip, self.place.chip).start())

    def arrived(self):
        self.each(lambda chip: self.copy(chip, chip).wait_recv())

    def sent(self):
        self.each(lambda chip: self.copy(chip, self.place.chip).wait_send())


class Reduce:
    def __init__(self, place, pack, pair, summed, plane, part, line, sems):
        self.place, self.pack, self.pair, self.summed = place, pack, pair, summed
        self.plane, self.part, self.line, self.sems = plane, part, line, sems
        self.levels = place.chips // 4

    def pair_copy(self):
        place = self.place
        return remote(
            self.pack.at[1 - place.core], self.pair, self.sems.at[0], self.sems.at[1], place.chip, 1 - place.core
        )

    def plane_copy(self, way, coming=False):
        place = self.place
        corner = flip(place.corner, way)
        return remote(
            self.summed.at[corner], self.plane.at[corner if coming else place.corner],
            self.sems.at[2 + way], self.sems.at[6 + way], place.level * 4 + corner, place.core,
        )

    def line_copy(self, way, coming=False):
        place = self.place
        level = flip(place.level, way)
        return remote(
            self.part.at[level], self.line.at[level if coming else place.level],
            self.sems.at[10 + way], self.sems.at[10 + self.levels + way], level * 4 + place.corner, place.core,
        )

    def to_pair(self):
        self.pair_copy().start()

    def to_plane(self):
        self.pair_copy().wait_recv()
        place = self.place
        for way in (3, 1, 2, 0):
            corner = flip(place.corner, way)
            for level in range(self.levels):
                self.summed[corner, level] = low(
                    wide(self.pack[place.core, corner, level]) + wide(self.pair[corner, level])
                )
            if way:
                self.plane_copy(way).start()

    def to_line(self):
        place = self.place
        corners = [flip(place.corner, way) for way in (1, 2, 3)]
        for way in (1, 2, 3):
            self.plane_copy(way, True).wait_recv()
        for way in [*range(1, self.levels), 0]:
            level = flip(place.level, way)
            total = wide(self.summed[place.corner, level])
            for corner in corners:
                total = total + wide(self.plane[corner, level])
            self.part[level] = low(total)
            if way:
                self.line_copy(way).start()

    def total(self):
        place = self.place
        total = wide(self.part[place.level])
        for way in range(1, self.levels):
            self.line_copy(way, True).wait_recv()
            total = total + wide(self.line[flip(place.level, way)])
        return total

    def sent(self):
        self.pair_copy().wait_send()
        for way in (1, 2, 3):
            self.plane_copy(way).wait_send()
        for way in range(1, self.levels):
            self.line_copy(way).wait_send()


def rms_apply(values, gain_row):
    inverse = lax.rsqrt(jnp.mean(values * values, axis=-1, keepdims=True) + norm_eps)
    return values * inverse * gain_row, inverse


def rms_back(upstream, values, inverse, gain_row):
    unit = values * inverse
    gain_grad = jnp.sum(upstream * unit, axis=0, keepdims=True)
    scaled = upstream * gain_row
    inner = jnp.mean(scaled * unit, axis=-1, keepdims=True)
    return inverse * (scaled - unit * inner), gain_grad


GELU_A = math.sqrt(2.0 / math.pi)
GELU_B = 0.044715


def gelu_both(x):
    square = x * x
    curve = jnp.tanh(GELU_A * x * (1.0 + GELU_B * square))
    half = 0.5 * (1.0 + curve)
    slope = half + 0.5 * x * (1.0 - curve * curve) * (GELU_A * (1.0 + 3.0 * GELU_B * square))
    return x * half, slope


def pieces_of(values):
    first = wide(low(values))
    second = wide(low(values - first))
    return first, second, values - first - second


def step_kernel(sizes, *refs):
    (chips, rows_dev, seq_len, width, hidden, capacity, half_slots, key_rows) = sizes
    refs = list(refs)
    names = list(dict(ENDS)) + list(scratch_of(sizes))
    r = types.SimpleNamespace(**dict(zip(names, refs, strict=True)))
    place = Place(chips)
    chip, core = place.chip, place.core
    me = chip * 2 + core
    tokens = half_slots
    wa, wb, cand_buf, user_buf = r.wa, r.wb, r.cand, r.user
    gather_a = Gather(place, wa, r.wa_send, r.wa_recv)
    gather_b = Gather(place, wb, r.wb_send, r.wb_recv)
    gather_c = Gather(place, cand_buf, r.cand_send, r.cand_recv)
    gather_u = Gather(place, user_buf, r.user_send, r.user_recv)
    spread_corr = Spread(place, r.corr, r.corr_send, r.corr_recv)
    spread_norm = Spread(place, r.norm, r.norm_send, r.norm_recv)
    spread_sums = Spread(place, r.scalar_buf, r.scalar_send, r.scalar_recv)

    barrier = pltpu.get_barrier_semaphore()

    def greet(index, carry):
        other = lax.rem(me + index, 2 * chips)
        pl.semaphore_signal(
            barrier, inc=1, device_id=(lax.div(other, 2), lax.rem(other, 2)), device_id_type=MESH_ID
        )
        return carry

    lax.fori_loop(1, 2 * chips, greet, 0)

    pos_t = r.pos[...]
    wa[me] = low(
        jnp.concatenate([r.qkv[...], r.gains[...], pos_t[:, :width], pos_t[:, width:]], axis=0)
    )
    narrow_t = r.narrow[...]
    wb[me] = low(
        jnp.concatenate(
            [r.merge[...], r.widen[...]]
            + [narrow_t[:, i * width : (i + 1) * width] for i in range(hidden // width)]
            + [jnp.zeros((8, width), jnp.float32)],
            axis=0,
        )
    )

    low_table = r.low_table
    low_table[pl.ds(0, rows_dev), :] = low(r.table[...])
    pad_rows = low_table.shape[0] - rows_dev
    low_table[pl.ds(rows_dev, pad_rows), :] = jnp.zeros((pad_rows, width), jnp.bfloat16)
    keys = r.keys
    keys[...] = jnp.zeros_like(keys)
    home = r.home[...]
    used = home.shape[0]
    keys[pl.ds(0, used), pl.ds(0, 128)] = wide(lax.div(home, 256))
    keys[pl.ds(0, used), pl.ds(128, 128)] = wide(lax.rem(home, 256))
    home_look = low(jnp.transpose(keys[:, 0:256]))
    ids_all = r.ids[:, pl.ds(pl.multiple_of(core * tokens, tokens), tokens)]
    lane_of = iota_of((128, tokens), 0)
    key_of = iota_of((key_rows, tokens), 0)

    def look(table_t, ids_row, parts):
        hot = low(wide(key_of == lax.div(ids_row, 128)))
        picked = dot_nn(table_t, hot)
        mask = lane_of == lax.rem(ids_row, 128)
        return [
            jnp.sum(jnp.where(mask, picked[128 * i : 128 * i + 128], 0.0), axis=0, keepdims=True)
            for i in range(parts)
        ]

    home_rows = []
    for d in range(chips):
        top, bottom = look(home_look, ids_all[d : d + 1, :], 2)
        home_rows.append(top * 256.0 + bottom)
    home_all = jnp.concatenate(home_rows, axis=0)
    r.home_all[...] = home_all

    pl.semaphore_wait(barrier, 2 * chips - 1)
    gather_a.start()

    upper = low(wide(iota_of((tokens, tokens), 0) <= iota_of((tokens, tokens), 1)))
    first_row = wide(chip * rows_dev)
    local_all = home_all - first_row
    owned = (local_all >= 0.0) & (local_all < float(rows_dev))
    rank = dot_nn(low(wide(owned)), upper) - 1.0
    slot_rank = wide(iota_of((capacity, tokens), 0))
    wanted = []
    for d in range(chips):
        chosen = (rank[d : d + 1, :] == slot_rank) & owned[d : d + 1, :]
        wanted.append(
            jnp.sum(jnp.where(chosen, local_all[d : d + 1, :] + 1.0, 0.0), axis=1, keepdims=True) - 1.0
        )
    wanted = jnp.concatenate(wanted, axis=0)
    asked = chips * capacity
    lanes = low_table.shape[0]
    hot_rows = low(wide(iota_of((asked, lanes), 1) == wanted.astype(jnp.int32)))
    out_rows = low(dot_nn(hot_rows, low_table[...])).reshape(chips, capacity, width)
    r.row_out[...] = out_rows
    r.row_in[chip] = r.row_out[chip]
    rows_there = Scatter(place, r.row_out, r.row_in, r.row_send, r.row_recv)
    rows_there.start()
    gather_b.start()
    wanted_row = jnp.transpose(jnp.broadcast_to(wanted, (asked, 128)))[0:1, :]
    r.asked[core] = wanted_row
    asked_copy = remote(
        r.asked.at[core], r.asked.at[core], r.asked_send, r.asked_recv, chip, 1 - core
    )
    asked_copy.start()

    own_home = r.home_all[pl.ds(chip, 1), :]
    owner_first = wide(iota_of((chips, tokens), 0) * rows_dev)
    at_owner = (own_home >= owner_first) & (own_home < owner_first + float(rows_dev))
    own_rank = dot_nn(low(wide(at_owner)), upper) - 1.0
    spread = jnp.concatenate(
        [
            wide((own_rank[o : o + 1, :] == slot_rank) & at_owner[o : o + 1, :])
            for o in range(chips)
        ],
        axis=0,
    )
    r.spread[...] = low(spread)

    freq = r.freq[...]
    for i, piece in enumerate(pieces_of(freq)):
        keys[pl.ds(0, used), pl.ds(128 * i, 128)] = piece
    freq_look = low(jnp.transpose(keys[...]))
    own_ids = r.ids[pl.ds(chip, 1), pl.ds(pl.multiple_of(core * tokens, tokens), tokens)]
    fa, fb, fc = look(freq_look, own_ids, 3)
    own_length = r.lengths[chip]
    row_pos = core * tokens + iota_of((1, tokens), 1)
    is_cand = (row_pos >= 1) & (row_pos < own_length)
    own_corr = jnp.where(is_cand, fa + fb + fc, -big_negative)
    r.corr[me] = own_corr
    spread_corr.start()

    def turned(row):
        return jnp.transpose(jnp.broadcast_to(row, (128, tokens)))[:, 0:1]

    corr_col = turned(own_corr)
    r.corr_col[...] = jnp.broadcast_to(corr_col, (tokens, 128))

    total_events = jnp.float32(0.0)
    for d in range(chips):
        total_events = total_events + wide(r.lengths[d] - 1)
    col_pos = core * tokens + iota_of((tokens, 1), 0)
    is_event = col_pos + 1 < own_length

    gather_a.advance(3)
    rows_there.arrived()
    embedded = low(dot_tn(r.spread[...], r.row_in[...].reshape(asked, width)))
    cand_buf[me] = embedded
    gather_c.start()
    gather_a.advance(3)
    gather_b.advance(3)
    gather_a.complete()
    qkv_w, pos_w, gain_w = r.qkv_w, r.pos_w, r.gain_w

    def unpack_a(index, carry):
        one, two = wide(wa[2 * index]), wide(wa[2 * index + 1])
        qkv_w[pl.ds(pl.multiple_of(index * 48, 16), 48), :] = low(jnp.concatenate([one[0:24], two[0:24]], axis=0))
        gain_w[pl.ds(pl.multiple_of(index * 16, 16), 16), :] = jnp.concatenate([one[24:32], two[24:32]], axis=0)[:, 0:128]
        early = jnp.concatenate([one[32:40], two[32:40]], axis=0)
        late = jnp.concatenate([one[40:48], two[40:48]], axis=0)
        pos_w[pl.ds(pl.multiple_of(index * 16, 16), 16), :] = jnp.where(core == 0, early, late)
        return carry

    lax.fori_loop(0, chips, unpack_a, 0)
    gain_rows = jnp.transpose(gain_w[...])[0:8, :]
    r.gain_rows[...] = gain_rows
    gain_one, gain_two, gain_three = (r.gain_rows[i : i + 1, :] for i in range(3))

    resid_zero = wide(cand_buf[me]) + jnp.transpose(pos_w[...])
    r.resid_zero[...] = resid_zero
    normed, _ = rms_apply(resid_zero, gain_one)
    r.input_one[...] = low(normed)
    qkv_own = low(dot_nt(r.input_one[...], qkv_w[...]))
    r.query[...] = qkv_own[:, 0:width]
    kv = r.kv
    kv[0] = qkv_own[:, width : 3 * width]
    kv_copy = remote(kv.at[0], kv.at[1], r.kv_send, r.kv_recv, chip, 1 - core)
    kv_copy.start()

    gather_b.advance(3)
    kv_copy.wait_recv()

    head_dim = width // HEADS
    scaling = head_dim ** (-0.5)
    causal = iota_of((tokens, tokens), 1) <= iota_of((tokens, tokens), 0)
    other_bias = jnp.where(core == 0, big_negative, 0.0)
    head_lane = lax.div(iota_of((1, width), 1), head_dim)
    prob = r.prob
    mixed_sum = r.acc
    mixed_sum[...] = jnp.zeros_like(mixed_sum)
    zero_low = jnp.zeros((), jnp.bfloat16)

    def of_head(values, head):
        return jnp.where(head_lane == head, values, zero_low)

    def attend(head):
        query = of_head(r.query[...], head)
        own = dot_nt(query, kv[0, :, 0:width]) * scaling
        own = jnp.where(causal, own, big_negative)
        other = dot_nt(query, kv[1, :, 0:width]) * scaling + other_bias
        peak = jnp.maximum(
            jnp.max(own, axis=-1, keepdims=True), jnp.max(other, axis=-1, keepdims=True)
        )
        own = jnp.exp(own - peak)
        other = jnp.exp(other - peak)
        total = jnp.sum(own, axis=-1, keepdims=True) + jnp.sum(other, axis=-1, keepdims=True)
        share = 1.0 / total
        own = own * share
        other = other * share
        prob[head, :, 0:tokens] = own
        prob[head, :, tokens : 2 * tokens] = other
        mixed_sum[...] += dot_nn(low(own), of_head(kv[0, :, width : 2 * width], head)) + dot_nn(
            low(other), of_head(kv[1, :, width : 2 * width], head)
        )

    for head in range(HEADS):
        attend(head)
        if head % 2:
            gather_b.advance(2)
            gather_c.advance(1)
    gather_b.complete()
    merge_w, widen_w, narrow_w = r.merge_w, r.widen_w, r.narrow_w

    def unpack_b(index, carry):
        one, two = wide(wb[2 * index]), wide(wb[2 * index + 1])
        at16 = pl.ds(pl.multiple_of(index * 16, 16), 16)
        merge_w[at16, :] = low(jnp.concatenate([one[0:8], two[0:8]], axis=0))
        widen_w[pl.ds(pl.multiple_of(index * 64, 16), 64), :] = low(jnp.concatenate([one[8:40], two[8:40]], axis=0))
        for i in range(hidden // width):
            top = 40 + 8 * i
            narrow_w[at16, pl.ds(i * width, width)] = low(
                jnp.concatenate([one[top : top + 8], two[top : top + 8]], axis=0)
            )
        return carry

    lax.fori_loop(0, chips, unpack_b, 0)
    r.attended[...] = low(mixed_sum[...])
    resid_one = r.resid_zero[...] + dot_nt(r.attended[...], merge_w[...])
    r.resid_one[...] = resid_one
    normed, _ = rms_apply(resid_one, gain_two)
    r.input_two[...] = low(normed)
    r.resid_two[...] = resid_one
    for i in range(hidden // FF_CHUNK):
        part = slice(i * FF_CHUNK, (i + 1) * FF_CHUNK)
        act, slope = gelu_both(dot_nt(r.input_two[...], widen_w[part, :]))
        r.act[:, part] = low(act)
        r.slope[:, part] = slope
        gather_c.advance(1)
    r.resid_two[...] += dot_nt(r.act[...], narrow_w[...])
    normed, _ = rms_apply(r.resid_two[...], gain_three)
    user_buf[me] = low(normed)
    gather_u.start()

    users = user_buf[me]
    gather_c.advance(2)
    gather_c.arrived(0, other=True)
    spread_corr.arrived()
    shifted = jnp.concatenate([wide(cand_buf[me])[1:, :], wide(cand_buf[chip * 2 + 1, pl.ds(0, 16), :])[0:1, :]], axis=0)
    target_corr = jnp.concatenate([corr_col[1:, :], r.corr[chip * 2 + 1][:, 0:1]], axis=0)
    target_logit = jnp.sum(wide(users) * shifted, axis=-1, keepdims=True) - target_corr
    target_logit = jnp.where(is_event, target_logit, 0.0)
    logit_buf, peaks, totals, acc = r.logit, r.peaks, r.totals, r.acc
    totals[...] = jnp.zeros_like(totals)
    acc[...] = jnp.zeros_like(acc)
    both = 2 * tokens
    group = chips // CHUNKS
    chip_row = core * tokens + iota_of((tokens, both), 0)
    chip_col = iota_of((tokens, both), 1)

    def pair_rows(buf, there):
        return buf[pl.ds(2 * there, 2)].reshape(both, width)

    def pair_row(buf, there):
        return jnp.concatenate([buf[2 * there], buf[2 * there + 1]], axis=1)

    def fold(values, how):
        parts = [values[:, i : i + 128] for i in range(0, values.shape[1], 128)]
        return functools.reduce(how, parts)

    peak = jnp.full((tokens, 1), big_negative, jnp.float32)
    for chunk in range(CHUNKS):
        gather_c.advance(group * (chunk + 1) - gather_c.passed)
        peaks[...] = jnp.broadcast_to(peak, peaks.shape)

        def logit_step(index, carry):
            step = chunk * group + index

            @pl.when(step > 0)
            def _():
                gather_c.arrived(step, other=True)

            there = place.relative(step)
            logits = dot_nt(users, pair_rows(cand_buf, there)) - pair_row(r.corr, there)
            logit_buf[index] = logits
            peaks[...] = jnp.maximum(peaks[...], fold(logits, jnp.maximum))
            return carry

        lax.fori_loop(0, group, logit_step, 0)
        before, peak = peak, jnp.max(peaks[...], axis=-1, keepdims=True)
        scale = jnp.exp(before - peak)
        totals[...] *= scale
        acc[...] *= scale
        if chunk > 0:
            gather_u.advance(2)

        def expo_step(index, carry):
            there = place.relative(chunk * group + index)
            expo = jnp.exp(logit_buf[index] - peak)
            totals[...] += fold(expo, jnp.add)
            if chunk == 0:
                expo = jnp.where((chip_col == chip_row + 1) & (index == 0), 0.0, expo)
            acc[...] += dot_nn(low(expo), pair_rows(cand_buf, there))
            return carry

        lax.fori_loop(0, group, expo_step, 0)
    total = jnp.sum(totals[...], axis=-1, keepdims=True)
    log_total = peak + jnp.log(total)
    loss_own = jnp.sum(jnp.where(is_event, log_total - target_logit, 0.0), axis=0, keepdims=True)
    weight = jnp.where(is_event, 1.0 / total_events, 0.0)
    target_coef = wide(low(weight * (jnp.exp(target_logit - log_total) - 1.0)))
    user_grad = acc[...] * (weight / total) + target_coef * shifted
    shift_col = jnp.where(is_event, log_total + jnp.log(total_events), -big_negative)
    norm_buf = r.norm
    norm_buf[me] = jnp.transpose(jnp.broadcast_to(shift_col, (tokens, 128)))[0:1, :]
    spread_norm.start()
    grad_two, gain_grad_three = rms_back(
        user_grad, r.resid_two[...],
        lax.rsqrt(jnp.mean(r.resid_two[...] * r.resid_two[...], axis=-1, keepdims=True) + norm_eps),
        gain_three,
    )
    branch_two = low(grad_two)
    narrow_grad = dot_tn(branch_two, r.act[...])
    r.pre[...] = low(dot_nn(branch_two, narrow_w[...]) * r.slope[...])
    widen_grad = dot_tn(r.pre[...], r.input_two[...])
    resid_one = r.resid_one[...]
    inverse_two = lax.rsqrt(jnp.mean(resid_one * resid_one, axis=-1, keepdims=True) + norm_eps)
    from_two, gain_grad_two = rms_back(dot_nn(r.pre[...], widen_w[...]), resid_one, inverse_two, gain_two)
    grad_one = grad_two + from_two
    r.grad_one[...] = grad_one
    branch_one = low(grad_one)
    merge_grad = dot_tn(branch_one, r.attended[...])
    r.mixed[...] = low(dot_nn(branch_one, merge_w[...]))

    tail, head_pack = r.tail_pack, r.head_pack
    for d in range(2 * chips):
        at = (d % 2, d // 2 % 4, d // 8)
        tail[*at, pl.ds(0, 32), :] = low(widen_grad[32 * d : 32 * d + 32])
        tail[*at, pl.ds(32, 32), :] = low(
            jnp.concatenate(
                [
                    narrow_grad[8 * d : 8 * d + 8, i * width : (i + 1) * width]
                    for i in range(hidden // width)
                ],
                axis=0,
            )
        )
    reduce_tail = Reduce(place, tail, r.tail_pair, r.tail_sum, r.tail_plane, r.tail_part, r.tail_line, r.tail_sems)
    reduce_head = Reduce(place, head_pack, r.head_pair, r.head_sum, r.head_plane, r.head_part, r.head_line, r.head_sems)
    reduce_tail.to_pair()
    dq, dkv = r.dq, r.dkv
    dq[...] = jnp.zeros_like(dq)
    dkv[...] = jnp.zeros_like(dkv)

    def attend_back(head):
        mixed = of_head(r.mixed[...], head)
        query = of_head(r.query[...], head)
        own, other = prob[head, :, 0:tokens], prob[head, :, tokens : 2 * tokens]
        own_grad = dot_nt(mixed, kv[0, :, width : 2 * width])
        other_grad = dot_nt(mixed, kv[1, :, width : 2 * width])
        inner = jnp.sum(own * own_grad, axis=-1, keepdims=True) + jnp.sum(
            other * other_grad, axis=-1, keepdims=True
        )
        own_score = low(own * (own_grad - inner))
        other_score = low(other * (other_grad - inner))
        dq[...] += dot_nn(own_score, of_head(kv[0, :, 0:width], head)) + dot_nn(
            other_score, of_head(kv[1, :, 0:width], head)
        )
        dkv[0, :, 0:width] += dot_tn(own_score, query)
        dkv[1, :, 0:width] += dot_tn(other_score, query)
        dkv[0, :, width : 2 * width] += dot_tn(low(own), mixed)
        dkv[1, :, width : 2 * width] += dot_tn(low(other), mixed)

    for head in range(HEADS):
        attend_back(head)
        if head % 2:
            gather_u.advance(2)
        if head == 3:
            reduce_tail.to_plane()
    back = r.back
    back[0, :, 0:width] = low(dkv[1, :, 0:width] * scaling)
    back[0, :, width : 2 * width] = low(dkv[1, :, width : 2 * width])
    back_copy = remote(back.at[0], back.at[1], r.back_send, r.back_recv, chip, 1 - core)
    back_copy.start()
    back_copy.wait_recv()
    qkv_grad = r.qkv_grad
    qkv_grad[:, 0:width] = low(dq[...] * scaling)
    qkv_grad[:, width : 2 * width] = low(dkv[0, :, 0:width] * scaling + wide(back[1, :, 0:width]))
    qkv_grad[:, 2 * width : 3 * width] = low(dkv[0, :, width : 2 * width] + wide(back[1, :, width : 2 * width]))
    qkv_wgrad = dot_tn(qkv_grad[...], r.input_one[...])
    resid_zero = r.resid_zero[...]
    inverse_one = lax.rsqrt(jnp.mean(resid_zero * resid_zero, axis=-1, keepdims=True) + norm_eps)
    from_one, gain_grad_one = rms_back(dot_nn(qkv_grad[...], qkv_w[...]), resid_zero, inverse_one, gain_one)
    resid_grad = r.grad_one[...] + from_one
    r.resid_grad[...] = resid_grad
    pos_grad = jnp.transpose(resid_grad)
    nothing = jnp.zeros((8, width), jnp.float32)
    for d in range(2 * chips):
        at = (d % 2, d // 2 % 4, d // 8)
        head_pack[*at, pl.ds(0, 32), :] = low(
            jnp.concatenate([qkv_wgrad[24 * d : 24 * d + 24], merge_grad[8 * d : 8 * d + 8]], axis=0)
        )
        pos_piece = pos_grad[8 * d : 8 * d + 8]
        head_pack[*at, pl.ds(32, 16), :] = low(
            jnp.concatenate(
                [jnp.where(core == 0, pos_piece, nothing), jnp.where(core == 0, nothing, pos_piece)], axis=0
            )
        )
    reduce_head.to_pair()
    gain_buf = r.gain_buf
    gain_buf[chip] = jnp.concatenate([gain_grad_one, gain_grad_two, gain_grad_three], axis=1)
    gain_there = Scatter(place, None, gain_buf, r.gain_send, r.gain_recv)
    gain_there.start()
    reduce_tail.to_line()
    gather_u.advance(chips)
    reduce_head.to_plane()
    gather_u.arrived(0, other=True)
    spread_norm.arrived()
    cand_grad = r.acc
    cand_grad[...] = jnp.zeros_like(cand_grad)
    corr_col = r.corr_col[:, 0:1]
    own_cand = cand_buf[me]
    event_row = jnp.where(iota_of((1, both), 1) + 1 < own_length, 1.0 / total_events, 0.0)

    def give_block(there, own):
        block_rows = pair_rows(user_buf, there)
        coef = jnp.exp((dot_nt(own_cand, block_rows) - corr_col) - pair_row(norm_buf, there))
        if own:
            coef = coef - jnp.where((chip_row == chip_col + 1) & (corr_col < 1e29), event_row, 0.0)
        cand_grad[...] += dot_nn(low(coef), block_rows)

    def grad_step(step, carry):
        gather_u.arrived(step, other=True)
        give_block(place.relative(step), False)
        return carry

    give_block(chip, True)
    lax.fori_loop(1, chips // 2, grad_step, 0)
    reduce_head.to_line()
    lax.fori_loop(chips // 2, chips, grad_step, 0)

    emb_grad = low(r.resid_grad[...] + cand_grad[...])
    back_out, back_in = r.back_out, r.back_in
    back_out[...] = low(dot_nn(r.spread[...], emb_grad)).reshape(chips, capacity, width)
    back_in[core, chip] = back_out[chip]
    rows_back = Scatter(place, back_out, back_in.at[core], r.rows_send, r.rows_recv)
    rows_back.start()

    shard = r.shard_grad
    shard[0:64] = reduce_tail.total()
    shard[64:112] = reduce_head.total()
    total = shard[...]
    gain_there.arrived()
    gain_total = gain_buf[0]
    for step in range(1, chips):
        gain_total = gain_total + gain_buf[step]
    gain_pair = r.gain_pair
    gain_pair[core] = gain_total
    gain_copy = remote(gain_pair.at[core], gain_pair.at[core], r.gp_send, r.gp_recv, chip, 1 - core)
    gain_copy.start()
    gain_copy.wait_recv()
    gain_total = gain_pair[0] + gain_pair[1]
    r.gain_grad[...] = gain_total
    gain_lane = iota_of((1, 3 * width), 1)
    gain_mine = lax.div(lax.rem(gain_lane, width), 8) == me
    square = jnp.sum(total * total, axis=0, keepdims=True)
    square = jnp.sum(square, axis=1, keepdims=True)
    square = square + jnp.sum(jnp.where(gain_mine, gain_total * gain_total, 0.0), axis=1, keepdims=True)

    rows_back.arrived()
    rows_pair = remote(back_in.at[core], back_in.at[core], r.rp_send, r.rp_recv, chip, 1 - core)
    rows_pair.start()
    asked_copy.wait_recv()
    asked_all = jnp.concatenate([r.asked[0], r.asked[1]], axis=1).astype(jnp.int32)
    rows_pair.wait_recv()
    table_grad = r.table_grad
    part_rows = TABLE_PART if rows_dev % TABLE_PART == 0 else 8
    incoming = back_in[...].reshape(2 * asked, width)
    r.square[...] = jnp.zeros_like(r.square)

    def table_part(index, carry):
        first = pl.multiple_of(index * part_rows, 8)
        hot = low(wide(iota_of((part_rows, 2 * asked), 0) + first == asked_all))
        grads = dot_nn(hot, incoming)
        table_grad[pl.ds(first, part_rows), :] = grads
        r.square[...] += jnp.sum(grads * grads, axis=0, keepdims=True)
        return carry

    lax.fori_loop(0, rows_dev // part_rows, table_part, 0)
    square = square + 0.5 * jnp.sum(r.square[...], axis=1, keepdims=True)

    scalar_buf = r.scalar_buf
    lane = iota_of((1, 128), 1)
    scalar_buf[me] = jnp.where(lane == 0, square, jnp.where(lane == 1, loss_own, 0.0))
    spread_sums.start()
    gather_a.sent()
    gather_b.sent()
    gather_c.sent()
    gather_u.sent()
    rows_there.sent()
    rows_back.sent()
    gain_there.sent()
    spread_corr.sent()
    spread_norm.sent()
    reduce_tail.sent()
    reduce_head.sent()
    for copy in (asked_copy, kv_copy, back_copy, gain_copy, rows_pair):
        copy.wait_send()
    spread_sums.arrived()
    sums = scalar_buf[0]
    for d in range(1, 2 * chips):
        sums = sums + scalar_buf[d]
    r.sums[...] = jnp.where(lane == 2, total_events, sums)
    spread_sums.sent()


TABLE_PART = 224
CHUNKS = 4
ENDS = dict(
    ids=0, lengths=0, home=0, freq=0, table=0, pos=0, qkv=0, merge=0, widen=0, narrow=0, gains=0,
    table_grad=1, shard_grad=1, gain_grad=1, sums=1,
)


def scratch_of(sizes):
    (chips, rows_dev, seq_len, width, hidden, capacity, tokens, key_rows) = sizes
    f32, b16 = jnp.float32, jnp.bfloat16
    devices, levels = 2 * chips, chips // 4
    dma = pltpu.SemaphoreType.DMA
    lanes = -(-rows_dev // 128) * 128
    if lanes == rows_dev:
        lanes += 128
    sends = Gather.sends(chips)
    shapes = dict(
        wa=pltpu.VMEM((devices, 48, width), b16),
        wb=pltpu.VMEM((devices, 80, width), b16),
        cand=pltpu.VMEM((devices, tokens, width), b16),
        corr=pltpu.VMEM((devices, 1, tokens), f32),
        logit=pltpu.VMEM((chips // CHUNKS, tokens, 2 * tokens), f32),
        user=pltpu.VMEM((devices, tokens, width), b16),
        low_table=pltpu.VMEM((lanes, width), b16),
        keys=pltpu.VMEM((key_rows, 384), f32),
        home_all=pltpu.VMEM((chips, tokens), f32),
        row_out=pltpu.VMEM((chips, capacity, width), b16),
        row_in=pltpu.VMEM((chips, capacity, width), b16),
        asked=pltpu.VMEM((2, 1, chips * capacity), f32),
        spread=pltpu.VMEM((chips * capacity, tokens), b16),
        corr_col=pltpu.VMEM((tokens, 128), f32),
        qkv_w=pltpu.VMEM((3 * width, width), b16),
        pos_w=pltpu.VMEM((width, tokens), f32),
        gain_w=pltpu.VMEM((width, 128), f32),
        gain_rows=pltpu.VMEM((8, width), f32),
        merge_w=pltpu.VMEM((width, width), b16),
        widen_w=pltpu.VMEM((hidden, width), b16),
        narrow_w=pltpu.VMEM((width, hidden), b16),
        resid_zero=pltpu.VMEM((tokens, width), f32),
        resid_one=pltpu.VMEM((tokens, width), f32),
        resid_two=pltpu.VMEM((tokens, width), f32),
        input_one=pltpu.VMEM((tokens, width), b16),
        input_two=pltpu.VMEM((tokens, width), b16),
        query=pltpu.VMEM((tokens, width), b16),
        kv=pltpu.VMEM((2, tokens, 2 * width), b16),
        prob=pltpu.VMEM((HEADS, tokens, 2 * tokens), f32),
        acc=pltpu.VMEM((tokens, width), f32),
        attended=pltpu.VMEM((tokens, width), b16),
        act=pltpu.VMEM((tokens, hidden), b16),
        slope=pltpu.VMEM((tokens, hidden), f32),
        pre=pltpu.VMEM((tokens, hidden), b16),
        peaks=pltpu.VMEM((tokens, 128), f32),
        totals=pltpu.VMEM((tokens, 128), f32),
        norm=pltpu.VMEM((devices, 1, tokens), f32),
        grad_one=pltpu.VMEM((tokens, width), f32),
        mixed=pltpu.VMEM((tokens, width), b16),
        tail_pack=pltpu.VMEM((2, 4, levels, 64, width), b16),
        tail_pair=pltpu.VMEM((4, levels, 64, width), b16),
        tail_sum=pltpu.VMEM((4, levels, 64, width), b16),
        tail_plane=pltpu.VMEM((4, levels, 64, width), b16),
        tail_part=pltpu.VMEM((levels, 64, width), b16),
        tail_line=pltpu.VMEM((levels, 64, width), b16),
        tail_sems=dma((10 + 2 * levels,)),
        head_pack=pltpu.VMEM((2, 4, levels, 48, width), b16),
        head_pair=pltpu.VMEM((4, levels, 48, width), b16),
        head_sum=pltpu.VMEM((4, levels, 48, width), b16),
        head_plane=pltpu.VMEM((4, levels, 48, width), b16),
        head_part=pltpu.VMEM((levels, 48, width), b16),
        head_line=pltpu.VMEM((levels, 48, width), b16),
        head_sems=dma((10 + 2 * levels,)),
        dq=pltpu.VMEM((tokens, width), f32),
        dkv=pltpu.VMEM((2, tokens, 2 * width), f32),
        back=pltpu.VMEM((2, tokens, 2 * width), b16),
        qkv_grad=pltpu.VMEM((tokens, 3 * width), b16),
        resid_grad=pltpu.VMEM((tokens, width), f32),
        gain_buf=pltpu.VMEM((chips, 1, 3 * width), f32),
        gain_pair=pltpu.VMEM((2, 1, 3 * width), f32),
        back_out=pltpu.VMEM((chips, capacity, width), b16),
        back_in=pltpu.VMEM((2, chips, capacity, width), b16),
        square=pltpu.VMEM((1, width), f32),
        scalar_buf=pltpu.VMEM((devices, 1, 128), f32),
        wa_send=dma((sends,)), wa_recv=dma((devices,)),
        wb_send=dma((sends,)), wb_recv=dma((devices,)),
        cand_send=dma((sends,)), cand_recv=dma((devices,)),
        user_send=dma((sends,)), user_recv=dma((devices,)),
        row_send=dma((chips,)), row_recv=dma((chips,)),
        rows_send=dma((chips,)), rows_recv=dma((chips,)),
        gain_send=dma((chips,)), gain_recv=dma((chips,)),
        norm_send=dma((devices,)), norm_recv=dma((devices,)),
        corr_send=dma((devices,)), corr_recv=dma((devices,)),
        scalar_send=dma((devices,)), scalar_recv=dma((devices,)),
        asked_send=dma, asked_recv=dma,
        kv_send=dma, kv_recv=dma,
        back_send=dma, back_recv=dma,
        gp_send=dma, gp_recv=dma,
        rp_send=dma, rp_recv=dma,
    )
    return shapes


def adam(weight, first, second, grad, rate):
    first = beta_one * first + (1.0 - beta_one) * grad
    second = beta_two * second + (1.0 - beta_two) * grad * grad
    fix_one = 1.0 - beta_one**STEP
    fix_two = 1.0 - beta_two**STEP
    update = first / fix_one / (jnp.sqrt(second / fix_two) + adam_eps) + decay_rate * weight
    return weight - rate * update, first, second


def update_kernel(width, *refs):
    (table_grad, shard, gain_grad, sums), refs = refs[:4], refs[4:]
    ins, outs = refs[:21], refs[21:]
    square = sums[0:1, 0:1]
    norm = jnp.sqrt(square)
    factor = jnp.minimum(1.0, clip_limit / norm)

    def update(index, grad, rate):
        new = adam(*(ref[...] for ref in ins[3 * index : 3 * index + 3]), grad * factor, rate)
        for ref, value in zip(outs[3 + 3 * index : 6 + 3 * index], new):
            ref[...] = value

    update(0, table_grad[...], learn_rate)

    @pl.when(pl.program_id(0) == 0)
    def _():
        outs[0][...] = sums[0:1, 1:2]
        outs[1][...] = sums[0:1, 2:3]
        outs[2][...] = norm
        update(1, jnp.concatenate([shard[96:104, :], shard[104:112, :]], axis=1), learn_rate)
        update(2, shard[64:88, :], learn_rate)
        update(3, shard[88:96, :], learn_rate)
        update(4, shard[0:32, :], learn_rate)
        update(5, jnp.concatenate([shard[32 + 8 * i : 40 + 8 * i, :] for i in range(4)], axis=1), learn_rate)
        update(6, gain_grad[...], gain_rate)


def fused_body(*args):
    (item_ids, lengths, home_row, log_freq) = args[:4]
    weights = args[4:]
    item_table = weights[0]
    rows_dev, width = item_table.shape
    chips = lax.axis_size("dp")
    seq_len = item_ids.shape[1]
    tokens = seq_len // 2
    hidden = weights[12].shape[1] * 2 * chips
    capacity = 2 * tokens // chips
    key_rows = -(-home_row.shape[0] // (128 * 128)) * 128
    sizes = (chips, rows_dev, seq_len, width, hidden, capacity, tokens, key_rows)
    me = lax.axis_index("dp") * 2 + lax.axis_index("sub")
    dense = [w.T for w in weights[3:18]]
    gains = weights[18]
    gains_in = jnp.pad(gains.T, ((0, 0), (0, width - 3)))
    shapes = scratch_of(sizes)
    vmem = pl.BlockSpec(memory_space=pltpu.VMEM)
    smem = pl.BlockSpec(memory_space=pltpu.SMEM)
    f32 = jnp.float32
    table_grad, shard, gain_grad, sums = pl.pallas_call(
        functools.partial(step_kernel, sizes),
        out_shape=[
            jax.ShapeDtypeStruct((rows_dev, width), f32),
            jax.ShapeDtypeStruct((112, width), f32),
            jax.ShapeDtypeStruct((1, 3 * width), f32),
            jax.ShapeDtypeStruct((1, 128), f32),
        ],
        in_specs=[vmem, smem] + [vmem] * 9,
        out_specs=[vmem] * 4,
        scratch_shapes=list(shapes.values()),
        compiler_params=pltpu.CompilerParams(
            collective_id=0, has_side_effects=True, vmem_limit_bytes=60 * 2**20
        ),
    )(
        item_ids, lengths, home_row.reshape(-1, 128), log_freq.reshape(-1, 128), item_table,
        dense[0], dense[3], dense[6], dense[9], dense[12], gains_in,
    )
    gain_own = lax.dynamic_slice_in_dim(gain_grad.reshape(3, width), me * 8, 8, 1)
    part = TABLE_PART if rows_dev % TABLE_PART == 0 else 8
    table_spec = pl.BlockSpec((part, width), lambda i: (i, 0))

    def whole(x):
        return pl.BlockSpec(x.shape, lambda i: (0,) * len(x.shape))

    small = dense + [weights[18], weights[19], weights[20]]
    one = jax.ShapeDtypeStruct((1, 1), f32)
    outs = pl.pallas_call(
        functools.partial(update_kernel, width),
        grid=(rows_dev // part,),
        out_shape=[one] * 3 + [jax.ShapeDtypeStruct(x.shape, f32) for x in list(weights[:3]) + small],
        in_specs=[table_spec, whole(shard), whole(gain_own), whole(sums)] + [table_spec] * 3 + [whole(x) for x in small],
        out_specs=[whole(one)] * 3 + [table_spec] * 3 + [whole(x) for x in small],
    )(table_grad, shard, gain_own, sums, *weights[:3], *small)
    outs = list(outs)
    return tuple(
        [x.reshape(()) for x in outs[:3]] + outs[3:6] + [x.T for x in outs[6:21]] + outs[21:]
    )


def solution(mesh):
    placed = (
        P(),
        P(),
        P(),
        P(),
        P("dp", None),
        P("dp", None),
        P("dp", None),
        P(None, ("dp", "sub")),
        P(None, ("dp", "sub")),
        P(None, ("dp", "sub")),
        P(None, ("dp", "sub")),
        P(None, ("dp", "sub")),
        P(None, ("dp", "sub")),
        P(None, ("dp", "sub")),
        P(None, ("dp", "sub")),
        P(None, ("dp", "sub")),
        P(None, ("dp", "sub")),
        P(None, ("dp", "sub")),
        P(None, ("dp", "sub")),
        P(None, ("dp", "sub")),
        P(None, ("dp", "sub")),
        P(None, ("dp", "sub")),
        P(None, ("dp", "sub")),
        P(None, ("dp", "sub")),
        P(None, ("dp", "sub")),
    )
    fits = mesh.shape["sub"] == 2 and mesh.shape["dp"] == 16
    return jax.shard_map(
        fused_body if fits else body,
        mesh=mesh,
        in_specs=placed,
        out_specs=(
            P(),
            P(),
            P(),
            P("dp", None),
            P("dp", None),
            P("dp", None),
            P(None, ("dp", "sub")),
            P(None, ("dp", "sub")),
            P(None, ("dp", "sub")),
            P(None, ("dp", "sub")),
            P(None, ("dp", "sub")),
            P(None, ("dp", "sub")),
            P(None, ("dp", "sub")),
            P(None, ("dp", "sub")),
            P(None, ("dp", "sub")),
            P(None, ("dp", "sub")),
            P(None, ("dp", "sub")),
            P(None, ("dp", "sub")),
            P(None, ("dp", "sub")),
            P(None, ("dp", "sub")),
            P(None, ("dp", "sub")),
            P(None, ("dp", "sub")),
            P(None, ("dp", "sub")),
            P(None, ("dp", "sub")),
        ),
        check_vma=False,
    )
```

```python
import functools
import math
import types

import jax
import jax.numpy as jnp
from jax import lax
from jax.experimental import pallas as pl
from jax.experimental.pallas import tpu as pltpu
from jax.sharding import PartitionSpec as P

HEADS = 8
STEP = 10


norm_eps = 1e-06
beta_one = 0.9
beta_two = 0.999
adam_eps = 1e-08
decay_rate = 0.01
learn_rate = 0.1
gain_rate = 0.5
clip_limit = 0.01
big_negative = -1e30
block_cols = 4096


def dot_plain(left_mat, right_mat):
    return jnp.dot(left_mat, right_mat, preferred_element_type=jnp.float32)


def dot_left_t(left_mat, right_mat):
    return lax.dot_general(
        left_mat, right_mat, (((0,), (0,)), ((), ())), preferred_element_type=jnp.float32
    )


def dot_right_t(left_mat, right_mat):
    return lax.dot_general(
        left_mat, right_mat, (((1,), (1,)), ((), ())), preferred_element_type=jnp.float32
    )


def rms_forward(values, gain_row):
    inverse = lax.rsqrt(jnp.mean(values * values, axis=-1, keepdims=True) + norm_eps)
    return (values * inverse * gain_row, inverse)


def rms_backward(upstream, values, inverse, gain_row):
    unit_vals = values * inverse
    gain_grad = jnp.sum(upstream * unit_vals, axis=0)
    scaled = upstream * gain_row
    inner_mean = jnp.mean(scaled * unit_vals, axis=-1, keepdims=True)
    return (inverse * (scaled - unit_vals * inner_mean), gain_grad)


def head_scores(queries, keys_all, allowed):
    scaling = queries.shape[-1] ** (-0.5)
    plain_scores = (
        jnp.einsum("bqhe,bkhe->bhqk", queries, keys_all, preferred_element_type=jnp.float32)
        * scaling
    )
    return jnp.where(allowed, plain_scores, big_negative)


def target_of(indices, slice_len, tokens_dev):
    within = indices % slice_len
    return jnp.where(within + 1 < slice_len, indices + 1, indices - within + tokens_dev)


def logits_for(user_rows, cand_rows, corr_rows, valid_rows):
    logits = dot_right_t(user_rows, cand_rows) - corr_rows[None, :]
    return jnp.where(valid_rows[None, :], logits, big_negative)


def coefficient(logits, log_total, weights, columns, targets):
    hits = (columns[None, :] == targets[:, None]).astype(jnp.float32)
    return (weights[:, None] * (jnp.exp(logits - log_total[:, None]) - hits)).astype(jnp.bfloat16)


def block_forward(resid_zero, dense_w, allowed, hist_local):
    qkv_full, merge_full, widen_full, narrow_full, gains_full = dense_w
    gain_float = gains_full.astype(jnp.float32)
    tokens_dev, model_width = resid_zero.shape
    normed_one, inverse_one = rms_forward(resid_zero, gain_float[0])
    input_one = normed_one.astype(jnp.bfloat16)
    qkv_parts = (
        dot_plain(input_one, qkv_full)
        .astype(jnp.bfloat16)
        .reshape(hist_local, -1, 3, HEADS, model_width // HEADS)
    )
    queries = qkv_parts[:, :, 0]
    keys_all, values_all = (
        lax.all_gather(qkv_parts[:, :, 1], "sub", axis=1, tiled=True),
        lax.all_gather(qkv_parts[:, :, 2], "sub", axis=1, tiled=True),
    )
    scores = head_scores(queries, keys_all, allowed)
    row_peak = jnp.max(scores, axis=-1, keepdims=True)
    expo_vals = jnp.exp(scores - row_peak)
    row_total = jnp.sum(expo_vals, axis=-1, keepdims=True)
    log_total = row_peak + jnp.log(row_total)
    attn_prob = (expo_vals / row_total).astype(jnp.bfloat16)
    attended = jnp.einsum(
        "bhqk,bkhe->bqhe", attn_prob, values_all, preferred_element_type=jnp.float32
    )
    attended = attended.astype(jnp.bfloat16).reshape(tokens_dev, model_width)
    resid_one = resid_zero + dot_plain(attended, merge_full)
    normed_two, inverse_two = rms_forward(resid_one, gain_float[1])
    input_two = normed_two.astype(jnp.bfloat16)
    hidden_pre = dot_plain(input_two, widen_full)
    hidden_act = jax.nn.gelu(hidden_pre).astype(jnp.bfloat16)
    resid_two = resid_one + dot_plain(hidden_act, narrow_full)
    normed_three, inverse_three = rms_forward(resid_two, gain_float[2])
    kept = (
        resid_zero,
        inverse_one,
        input_one,
        queries,
        keys_all,
        values_all,
        log_total,
        attended,
        resid_one,
        inverse_two,
        input_two,
        hidden_pre,
        hidden_act,
        resid_two,
        inverse_three,
    )
    return (normed_three.astype(jnp.bfloat16), kept)


def block_backward(user_grad, kept, dense_w, allowed):
    (
        resid_zero,
        inverse_one,
        input_one,
        queries,
        keys_all,
        values_all,
        log_total,
        attended,
        resid_one,
        inverse_two,
        input_two,
        hidden_pre,
        hidden_act,
        resid_two,
        inverse_three,
    ) = kept
    qkv_full, merge_full, widen_full, narrow_full, gains_full = dense_w
    gain_float = gains_full.astype(jnp.float32)
    tokens_dev, model_width = resid_zero.shape
    head_dim = queries.shape[-1]
    grad_two, gain_three = rms_backward(user_grad, resid_two, inverse_three, gain_float[2])
    branch_two = grad_two.astype(jnp.bfloat16)
    narrow_grad = dot_left_t(hidden_act, branch_two)
    hidden_grad = dot_right_t(branch_two, narrow_full)
    pre_grad = jax.vjp(jax.nn.gelu, hidden_pre)[1](hidden_grad)[0].astype(jnp.bfloat16)
    widen_grad = dot_left_t(input_two, pre_grad)
    from_two, gain_two = rms_backward(
        dot_right_t(pre_grad, widen_full), resid_one, inverse_two, gain_float[1]
    )
    grad_one = grad_two + from_two
    branch_one = grad_one.astype(jnp.bfloat16)
    merge_grad = dot_left_t(attended, branch_one)
    mixed_grad = dot_right_t(branch_one, merge_full).astype(jnp.bfloat16).reshape(queries.shape)
    scores = head_scores(queries, keys_all, allowed)
    attn_prob = jnp.exp(scores - log_total)
    prob_grad = jnp.einsum(
        "bqhe,bkhe->bhqk", mixed_grad, values_all, preferred_element_type=jnp.float32
    )
    score_grad = attn_prob * (prob_grad - jnp.sum(attn_prob * prob_grad, axis=-1, keepdims=True))
    score_grad = score_grad.astype(jnp.bfloat16)
    scaling = head_dim ** (-0.5)
    query_grad = (
        jnp.einsum("bhqk,bkhe->bqhe", score_grad, keys_all, preferred_element_type=jnp.float32)
        * scaling
    )
    keys_grad = (
        jnp.einsum("bhqk,bqhe->bkhe", score_grad, queries, preferred_element_type=jnp.float32)
        * scaling
    )
    values_grad = jnp.einsum(
        "bhqk,bqhe->bkhe",
        attn_prob.astype(jnp.bfloat16),
        mixed_grad,
        preferred_element_type=jnp.float32,
    )
    key_own, value_own = (
        lax.psum_scatter(
            keys_grad.astype(jnp.bfloat16), "sub", scatter_dimension=1, tiled=True
        ).astype(jnp.float32),
        lax.psum_scatter(
            values_grad.astype(jnp.bfloat16), "sub", scatter_dimension=1, tiled=True
        ).astype(jnp.float32),
    )
    qkv_grad = (
        jnp.stack([query_grad, key_own, value_own], axis=2)
        .astype(jnp.bfloat16)
        .reshape(tokens_dev, 3 * model_width)
    )
    qkv_wgrad = dot_left_t(input_one, qkv_grad)
    from_one, gain_one = rms_backward(
        dot_right_t(qkv_grad, qkv_full), resid_zero, inverse_one, gain_float[0]
    )
    gain_grads = jnp.stack([gain_one, gain_two, gain_three])
    return (grad_one + from_one, (qkv_wgrad, merge_grad, widen_grad, narrow_grad, gain_grads))


def adamw(weight, moment_one, moment_two, gradient, rate):
    moment_one = beta_one * moment_one + (1.0 - beta_one) * gradient
    moment_two = beta_two * moment_two + (1.0 - beta_two) * gradient * gradient
    fix_one = 1.0 - beta_one**STEP
    fix_two = 1.0 - beta_two**STEP
    update = (
        moment_one / fix_one / (jnp.sqrt(moment_two / fix_two) + adam_eps) + decay_rate * weight
    )
    return (weight - rate * update, moment_one, moment_two)


def body(
    item_ids,
    lengths,
    home_row,
    log_freq,
    item_table,
    table_first,
    table_second,
    pos_table,
    pos_first,
    pos_second,
    qkv_weight,
    qkv_first,
    qkv_second,
    merge_weight,
    merge_first,
    merge_second,
    widen_weight,
    widen_first,
    widen_second,
    narrow_weight,
    narrow_first,
    narrow_second,
    norm_gains,
    gains_first,
    gains_second,
):
    dp_count = lax.axis_size("dp")
    sub_count = lax.axis_size("sub")
    dp_index = lax.axis_index("dp")
    sub_index = lax.axis_index("sub")
    rows_dev, model_width = item_table.shape
    hist_local = item_ids.shape[0] // dp_count
    seq_len = item_ids.shape[1]
    slice_len = seq_len // sub_count
    tokens_dev = hist_local * slice_len
    capacity = max(2, (2 * tokens_dev + dp_count - 1) // dp_count)
    all_tokens = dp_count * sub_count * tokens_dev
    pos_full, qkv_full, merge_full, widen_full, narrow_full, gains_full = (
        lax.all_gather(pos_table.astype(jnp.bfloat16), ("dp", "sub"), axis=1, tiled=True),
        lax.all_gather(qkv_weight.astype(jnp.bfloat16), ("dp", "sub"), axis=1, tiled=True),
        lax.all_gather(merge_weight.astype(jnp.bfloat16), ("dp", "sub"), axis=1, tiled=True),
        lax.all_gather(widen_weight.astype(jnp.bfloat16), ("dp", "sub"), axis=1, tiled=True),
        lax.all_gather(narrow_weight.astype(jnp.bfloat16), ("dp", "sub"), axis=1, tiled=True),
        lax.all_gather(norm_gains.astype(jnp.bfloat16), ("dp", "sub"), axis=1, tiled=True),
    )
    dense_w = (qkv_full, merge_full, widen_full, narrow_full, gains_full)
    own_items = lax.dynamic_slice(
        item_ids, (dp_index * hist_local, sub_index * slice_len), (hist_local, slice_len)
    ).reshape(tokens_dev)
    stored_at = home_row[own_items]
    owner_dev = stored_at // rows_dev
    local_row = stored_at % rows_dev
    owner_hot = (owner_dev[:, None] == jnp.arange(dp_count, dtype=jnp.int32)[None, :]).astype(
        jnp.int32
    )
    owner_rank = jnp.sum(jnp.cumsum(owner_hot, axis=0) * owner_hot, axis=1) - 1
    slot_index = owner_dev * capacity + owner_rank
    request = (
        jnp.zeros((dp_count * capacity,), jnp.int32)
        .at[slot_index]
        .set(local_row)
        .reshape(dp_count, capacity)
    )
    arrived = lax.all_to_all(request, "dp", split_axis=0, concat_axis=0, tiled=True)
    found_rows = item_table[arrived].astype(jnp.bfloat16)
    arrived_rows = lax.all_to_all(found_rows, "dp", split_axis=0, concat_axis=0, tiled=True)
    embedded = arrived_rows.reshape(dp_count * capacity, model_width)[slot_index]
    pos_rows = lax.dynamic_slice_in_dim(pos_full, sub_index * slice_len, slice_len, 0).astype(
        jnp.float32
    )
    resid_zero = (
        embedded.astype(jnp.float32).reshape(hist_local, slice_len, model_width) + pos_rows[None]
    ).reshape(tokens_dev, model_width)
    query_pos = sub_index * slice_len + jnp.arange(slice_len)
    allowed = jnp.arange(seq_len)[None, :] <= query_pos[:, None]
    user_vecs, kept = block_forward(resid_zero, dense_w, allowed, hist_local)
    candidates = lax.all_gather(embedded, ("dp", "sub"), axis=0, tiled=True)
    layout = (dp_count, hist_local, sub_count, slice_len)

    def by_device(values):
        return values.reshape(layout).transpose(0, 2, 1, 3).reshape(all_tokens)

    all_items = by_device(item_ids)
    all_pos = by_device(
        jnp.broadcast_to(jnp.arange(seq_len, dtype=jnp.int32)[None, :], item_ids.shape)
    )
    all_len = by_device(jnp.broadcast_to(lengths[:, None], item_ids.shape))
    valid_all = (all_pos >= 1) & (all_pos < all_len)
    correction = log_freq[all_items]
    base_index = (dp_index * sub_count + sub_index) * tokens_dev
    own_index = base_index + jnp.arange(tokens_dev)
    own_pos = lax.dynamic_slice_in_dim(all_pos, base_index, tokens_dev)
    own_len = lax.dynamic_slice_in_dim(all_len, base_index, tokens_dev)
    event_count = jnp.sum(lengths - 1).astype(jnp.float32)
    valid_rows = (own_pos + 1 < own_len).astype(jnp.float32)
    row_weight = valid_rows / event_count
    targets = target_of(own_index, slice_len, tokens_dev)
    col_block = min(block_cols, all_tokens)
    starts = jnp.arange(all_tokens // col_block) * col_block

    def block_logits(block_start):
        cand_rows = lax.dynamic_slice_in_dim(candidates, block_start, col_block, 0)
        corr_rows = lax.dynamic_slice_in_dim(correction, block_start, col_block)
        valid_cols = lax.dynamic_slice_in_dim(valid_all, block_start, col_block)
        return (
            cand_rows,
            logits_for(user_vecs, cand_rows, corr_rows, valid_cols),
            block_start + jnp.arange(col_block),
        )

    def forward_block(running, block_start):
        row_peak, row_total, target_logit = running
        cand_rows, logits, columns = block_logits(block_start)
        new_peak = jnp.maximum(row_peak, jnp.max(logits, axis=1))
        row_total = row_total * jnp.exp(row_peak - new_peak) + jnp.sum(
            jnp.exp(logits - new_peak[:, None]), axis=1
        )
        target_logit = target_logit + jnp.sum(
            jnp.where(columns[None, :] == targets[:, None], logits, 0.0), axis=1
        )
        return ((new_peak, row_total, target_logit), None)

    start_state = (
        jnp.full((tokens_dev,), big_negative, jnp.float32),
        jnp.zeros((tokens_dev,), jnp.float32),
        jnp.zeros((tokens_dev,), jnp.float32),
    )
    (row_peak, row_total, target_logit), _ = lax.scan(forward_block, start_state, starts)
    log_total = row_peak + jnp.log(row_total)
    loss_local = jnp.sum(valid_rows * (log_total - target_logit))

    def user_block(running, block_start):
        cand_rows, logits, columns = block_logits(block_start)
        coeffs = coefficient(logits, log_total, row_weight, columns, targets)
        return (running + dot_plain(coeffs, cand_rows), None)

    user_grad, _ = lax.scan(user_block, jnp.zeros((tokens_dev, model_width), jnp.float32), starts)
    step_rows = math.gcd(tokens_dev * lax.axis_size(("dp", "sub")), max(block_cols, tokens_dev))

    def one_block(offset):
        cand_rows = lax.dynamic_slice_in_dim(candidates, offset, step_rows, 0)
        corr_rows = lax.dynamic_slice_in_dim(correction, offset, step_rows)
        valid_cols = lax.dynamic_slice_in_dim(valid_all, offset, step_rows)
        logits = logits_for(user_vecs, cand_rows, corr_rows, valid_cols)
        coeffs = coefficient(logits, log_total, row_weight, offset + jnp.arange(step_rows), targets)
        return dot_left_t(coeffs, user_vecs)

    pieces = lax.map(
        one_block, jnp.arange(tokens_dev * lax.axis_size(("dp", "sub")) // step_rows) * step_rows
    )
    cand_grad = lax.psum_scatter(
        pieces.reshape(tokens_dev * lax.axis_size(("dp", "sub")), model_width),
        ("dp", "sub"),
        scatter_dimension=0,
        tiled=True,
    )
    resid_grad, weight_grads = block_backward(user_grad, kept, dense_w, allowed)
    qkv_wgrad, merge_grad, widen_grad, narrow_grad, gain_grads = weight_grads
    emb_grad = resid_grad + cand_grad
    pos_rows_grad = jnp.sum(resid_grad.reshape(hist_local, slice_len, model_width), axis=0)
    pos_grad = lax.dynamic_update_slice_in_dim(
        jnp.zeros((seq_len, model_width), jnp.float32), pos_rows_grad, sub_index * slice_len, 0
    )
    outgoing = (
        jnp.zeros((dp_count * capacity, model_width), jnp.float32).at[slot_index].set(emb_grad)
    )
    incoming = lax.all_to_all(
        outgoing.reshape(dp_count, capacity, model_width),
        "dp",
        split_axis=0,
        concat_axis=0,
        tiled=True,
    )
    incoming_rows = incoming.reshape(-1, model_width)
    arrived_flat = arrived.reshape(-1)
    plane_grad = jnp.zeros((rows_dev, model_width), jnp.float32).at[arrived_flat].add(incoming_rows)
    table_grad = lax.psum(plane_grad, "sub")
    shard_grads = (
        lax.psum_scatter(pos_grad, ("dp", "sub"), scatter_dimension=1, tiled=True),
        lax.psum_scatter(qkv_wgrad, ("dp", "sub"), scatter_dimension=1, tiled=True),
        lax.psum_scatter(merge_grad, ("dp", "sub"), scatter_dimension=1, tiled=True),
        lax.psum_scatter(widen_grad, ("dp", "sub"), scatter_dimension=1, tiled=True),
        lax.psum_scatter(narrow_grad, ("dp", "sub"), scatter_dimension=1, tiled=True),
        lax.psum_scatter(gain_grads, ("dp", "sub"), scatter_dimension=1, tiled=True),
    )
    square_part = sum((jnp.sum(gradient * gradient) for gradient in shard_grads))
    square_part = square_part + jnp.where(sub_index == 0, jnp.sum(table_grad * table_grad), 0.0)
    loss_sum, square_sum = lax.psum((loss_local, square_part), ("dp", "sub"))
    grad_norm = jnp.sqrt(square_sum)
    factor = jnp.minimum(1.0, clip_limit / grad_norm)
    masters = (
        item_table,
        pos_table,
        qkv_weight,
        merge_weight,
        widen_weight,
        narrow_weight,
        norm_gains,
    )
    firsts = (
        table_first,
        pos_first,
        qkv_first,
        merge_first,
        widen_first,
        narrow_first,
        gains_first,
    )
    seconds = (
        table_second,
        pos_second,
        qkv_second,
        merge_second,
        widen_second,
        narrow_second,
        gains_second,
    )
    rates = (learn_rate,) * 6 + (gain_rate,)
    all_grads = (table_grad,) + tuple(shard_grads)
    results = [loss_sum, event_count, grad_norm]
    for weight, moment_one, moment_two, gradient, rate in zip(
        masters, firsts, seconds, all_grads, rates
    ):
        results.extend(adamw(weight, moment_one, moment_two, gradient * factor, rate))
    return tuple(results)


MESH_ID = pl.DeviceIdType.MESH
FF_CHUNK = 256


def dot_nn(left, right):
    return lax.dot_general(
        left, right, (((1,), (0,)), ((), ())), preferred_element_type=jnp.float32
    )


def dot_nt(left, right):
    return lax.dot_general(
        left, right, (((1,), (1,)), ((), ())), preferred_element_type=jnp.float32
    )


def dot_tn(left, right):
    return lax.dot_general(
        left, right, (((0,), (0,)), ((), ())), preferred_element_type=jnp.float32
    )


def low(values):
    return values.astype(jnp.bfloat16)


def wide(values):
    return values.astype(jnp.float32)


def iota_of(shape, axis):
    return lax.broadcasted_iota(jnp.int32, shape, axis)


def flip(index, bits):
    total = 0
    for power in (1, 2, 4, 8):
        a = lax.rem(lax.div(index, power), 2)
        b = (bits // power) % 2 if isinstance(bits, int) else lax.rem(lax.div(bits, power), 2)
        total = total + power * (a + b - 2 * a * b)
    return total


def arrival_order(levels):
    if levels == 4:
        return [(0, 0), (0, 1), (0, 2), (1, 0), (2, 0), (0, 3), (1, 1), (1, 2), (3, 0), (2, 1), (2, 2), (1, 3), (3, 1), (3, 2), (2, 3), (3, 3)]
    return [(level, corner) for level in range(levels) for corner in range(4)]


class Place:
    def __init__(self, chips):
        self.chips = chips
        self.chip = lax.axis_index("dp")
        self.core = lax.axis_index("sub")
        self.level = lax.div(self.chip, 4)
        self.corner = lax.rem(self.chip, 4)
        self.inner = (self.level == 1) | (self.level == 2)
        self.near_x = self.level * 4 + flip(self.corner, 1)
        self.near_y = self.level * 4 + flip(self.corner, 2)

    def step(self, way):
        return arrival_order(self.chips // 4).index(way)

    def way(self, step):
        order = arrival_order(self.chips // 4)
        if isinstance(step, int):
            return order[step]
        return tuple(
            sum(jnp.where(step == i, place[axis], 0) for i, place in enumerate(order) if place[axis])
            for axis in range(2)
        )

    def relative(self, step):
        level, corner = self.way(step)
        return flip(self.level, level) * 4 + flip(self.corner, corner)


def remote(src, dst, send, recv, chip, core):
    return pltpu.make_async_remote_copy(
        src_ref=src,
        dst_ref=dst,
        send_sem=send,
        recv_sem=recv,
        device_id=(chip, core),
        device_id_type=MESH_ID,
    )


class Gather:
    def __init__(self, place, buf, send, recv):
        self.place, self.buf, self.send, self.recv = place, buf, send, recv
        self.levels = place.chips // 4
        order = [(0, 1), (1, 0), (2, 0), (1, 2), (3, 0), (2, 1)]
        self.queue = [place.step(at) for at in order]
        self.waiting = set(range(1, place.chips))

    def copy(self, block, sem, chip):
        return remote(
            self.buf.at[block], self.buf.at[block], self.send.at[sem], self.recv.at[block], chip, self.place.core
        )

    def send_on(self, step, action):
        place = self.place
        block = place.relative(step)
        level, corner = place.way(step)
        last = level == self.levels - 1
        if corner == 0 or (corner == 2 and level % 2 == 1 and not last):
            action(self.copy(block, step * 2, place.near_x))
        if corner == 0 or (corner == 1 and level % 2 == 0 and not last):
            action(self.copy(block, step * 2 + 1, place.near_y))
        if corner == 0 and last:
            action(self.copy(block, place.chips * 2, place.level * 4 + 3 - place.corner))
        if corner == 0 and level == 2:
            @pl.when(place.inner)
            def _():
                action(self.copy(block, place.chips * 2 + 4, flip(place.level, 1) * 4 + place.corner))

    def along_z(self, action):
        place = self.place
        for step in (1, 3, 2):
            chip = flip(place.level, step) * 4 + place.corner
            copy = self.copy(place.chip, place.chips * 2 + step, chip)
            if step == 3:
                pl.when(place.inner)(lambda copy=copy: action(copy))
            else:
                action(copy)

    def start(self):
        self.along_z(lambda copy: copy.start())
        self.send_on(0, lambda copy: copy.start())

    def need(self, steps):
        for step in steps:
            if step in self.waiting:
                self.waiting.remove(step)
                self.copy(self.place.relative(step), 0, self.place.chip).wait_recv()
            if step in self.queue:
                self.queue.remove(step)
                self.send_on(step, lambda copy: copy.start())

    def advance(self, count):
        self.need(self.queue[:count])

    def complete(self):
        self.advance(len(self.queue))
        self.need(sorted(self.waiting))

    def sent(self):
        self.along_z(lambda copy: copy.wait_send())
        for step in range(self.place.chips):
            self.send_on(step, lambda copy: copy.wait_send())

    @staticmethod
    def sends(chips):
        return chips * 2 + 8


class ShortGather(Gather):
    def __init__(self, place, buf, send, recv):
        super().__init__(place, buf, send, recv)
        self.queue = [place.step((level, 0)) for level in range(1, self.levels)]

    def send_on(self, step, action):
        place = self.place
        block = place.relative(step)
        if place.way(step)[1] == 0:
            action(self.copy(block, step * 2, place.near_x))
            action(self.copy(block, step * 2 + 1, place.near_y))
            action(self.copy(block, place.chips * 2 + 4 + place.way(step)[0], place.level * 4 + 3 - place.corner))

    def along_z(self, action):
        place = self.place
        for step in (1, 3, 2):
            chip = flip(place.level, step) * 4 + place.corner
            action(self.copy(place.chip, place.chips * 2 + step, chip))


def to_sibling(place, src, dst, sems):
    return remote(src, dst, sems.at[0], sems.at[1], place.chip, 1 - place.core)


class Scatter:
    def __init__(self, place, src, dst, send, recv):
        self.place, self.src, self.dst, self.send, self.recv = place, src, dst, send, recv

    def copy(self, to, at):
        place = self.place
        return remote(
            self.src.at[to] if self.src is not None else self.dst.at[place.chip],
            self.dst.at[at],
            self.send.at[to],
            self.recv.at[at],
            to,
            place.core,
        )

    def each(self, action):
        place = self.place

        def step(index, carry):
            action(lax.rem(place.chip + index, place.chips))
            return carry

        lax.fori_loop(1, place.chips, step, 0)

    def start(self):
        self.each(lambda chip: self.copy(chip, self.place.chip).start())

    def arrived(self):
        self.each(lambda chip: self.copy(chip, chip).wait_recv())

    def sent(self):
        self.each(lambda chip: self.copy(chip, self.place.chip).wait_send())


class Reduce:
    def __init__(self, place, pack, pair, summed, plane, part, line, sems):
        self.place, self.pack, self.pair, self.summed = place, pack, pair, summed
        self.plane, self.part, self.line, self.sems = plane, part, line, sems
        self.levels = place.chips // 4

    def pair_copy(self):
        place = self.place
        return remote(
            self.pack.at[1 - place.core], self.pair, self.sems.at[0], self.sems.at[1], place.chip, 1 - place.core
        )

    def plane_copy(self, way, coming=False):
        place = self.place
        corner = flip(place.corner, way)
        return remote(
            self.summed.at[corner], self.plane.at[corner if coming else place.corner],
            self.sems.at[2 + way], self.sems.at[6 + way], place.level * 4 + corner, place.core,
        )

    def line_copy(self, way, coming=False):
        place = self.place
        level = flip(place.level, way)
        return remote(
            self.part.at[level], self.line.at[level if coming else place.level],
            self.sems.at[10 + way], self.sems.at[10 + self.levels + way], level * 4 + place.corner, place.core,
        )

    def to_pair(self):
        self.pair_copy().start()

    def to_plane(self):
        self.pair_copy().wait_recv()
        place = self.place
        for way in (3, 1, 2, 0):
            corner = flip(place.corner, way)
            for level in range(self.levels):
                self.summed[corner, level] = low(
                    wide(self.pack[place.core, corner, level]) + wide(self.pair[corner, level])
                )
            if way:
                self.plane_copy(way).start()

    def to_line(self):
        place = self.place
        corners = [flip(place.corner, way) for way in (1, 2, 3)]
        for way in (1, 2, 3):
            self.plane_copy(way, True).wait_recv()
        for way in [*range(1, self.levels), 0]:
            level = flip(place.level, way)
            total = wide(self.summed[place.corner, level])
            for corner in corners:
                total = total + wide(self.plane[corner, level])
            self.part[level] = low(total)
            if way:
                self.line_copy(way).start()

    def total(self):
        place = self.place
        total = wide(self.part[place.level])
        for way in range(1, self.levels):
            self.line_copy(way, True).wait_recv()
            total = total + wide(self.line[flip(place.level, way)])
        return total

    def sent(self):
        self.pair_copy().wait_send()
        for way in (1, 2, 3):
            self.plane_copy(way).wait_send()
        for way in range(1, self.levels):
            self.line_copy(way).wait_send()


def rms_apply(values, gain_row):
    inverse = lax.rsqrt(jnp.mean(values * values, axis=-1, keepdims=True) + norm_eps)
    return values * inverse * gain_row, inverse


def rms_back(upstream, values, inverse, gain_row):
    unit = values * inverse
    gain_grad = jnp.sum(upstream * unit, axis=0, keepdims=True)
    scaled = upstream * gain_row
    inner = jnp.mean(scaled * unit, axis=-1, keepdims=True)
    return inverse * (scaled - unit * inner), gain_grad


GELU_A = math.sqrt(2.0 / math.pi)
GELU_B = 0.044715


def gelu_both(x):
    square = x * x
    curve = jnp.tanh(GELU_A * x * (1.0 + GELU_B * square))
    half = 0.5 * (1.0 + curve)
    slope = half + 0.5 * x * (1.0 - curve * curve) * (GELU_A * (1.0 + 3.0 * GELU_B * square))
    return x * half, slope


def pieces_of(values):
    first = wide(low(values))
    second = wide(low(values - first))
    return first, second, values - first - second


def step_kernel(sizes, *refs):
    (chips, rows_dev, seq_len, width, hidden, capacity, half_slots, key_rows) = sizes
    refs = list(refs)
    names = list(dict(ENDS)) + list(scratch_of(sizes))
    r = types.SimpleNamespace(**dict(zip(names, refs, strict=True)))
    place = Place(chips)
    chip, core = place.chip, place.core
    me = chip * 2 + core
    tokens = half_slots
    wa, wb, cand_buf, user_buf = r.wa, r.wb, r.cand, r.user
    gather_a = ShortGather(place, wa.at[core], r.wa_send, r.wa_recv)
    gather_b = ShortGather(place, wb.at[core], r.wb_send, r.wb_recv)
    gather_c = Gather(place, cand_buf, r.cand_send, r.cand_recv)
    gather_u = Gather(place, user_buf, r.user_send, r.user_recv)
    spread_corr = Scatter(place, None, r.corr, r.corr_send, r.corr_recv)
    spread_norm = Scatter(place, None, r.norm, r.norm_send, r.norm_recv)
    pair_a = to_sibling(place, wa.at[core], wa.at[core], r.wa_pair)
    pair_b = to_sibling(place, wb.at[core], wb.at[core], r.wb_pair)
    pair_emb = to_sibling(place, r.emb_pair.at[core], r.emb_pair.at[core], r.emb_sems)
    pair_corr = to_sibling(place, r.corr_pair.at[core], r.corr_pair.at[core], r.corr_sems)
    pair_user = to_sibling(place, r.user_pair.at[core], r.user_pair.at[core], r.user_sems)
    pair_soft = to_sibling(place, r.soft_out, r.soft_in, r.soft_sems)
    pair_cand = to_sibling(place, r.cand_out, r.cand_in, r.cand_sems)
    spread_sums = Scatter(place, None, r.scalar_buf, r.scalar_send, r.scalar_recv)
    pair_sums = to_sibling(place, r.scalar_pair.at[core], r.scalar_pair.at[core], r.sums_sems)

    barrier = pltpu.get_barrier_semaphore()

    def greet(index, carry):
        other = lax.rem(chip + index, chips)
        pl.semaphore_signal(barrier, inc=1, device_id=(other, core), device_id_type=MESH_ID)
        return carry

    lax.fori_loop(1, chips, greet, 0)
    pl.semaphore_signal(barrier, inc=1, device_id=(chip, 1 - core), device_id_type=MESH_ID)

    turn = r.turn
    turn[...] = jnp.zeros_like(turn)
    turn[0:3, 0:8] = r.gains[...]
    gains_t = jnp.concatenate([jnp.transpose(turn[...])[0:8, :], jnp.zeros((8, width - 128), jnp.float32)], axis=1)
    pos_t = r.pos[...]
    wa[core, chip] = low(
        jnp.concatenate([r.qkv[...], gains_t, pos_t[:, :width], pos_t[:, width:]], axis=0)
    )
    narrow_t = r.narrow[...]
    wb[core, chip] = low(
        jnp.concatenate(
            [r.merge[...], r.widen[...]]
            + [narrow_t[:, i * width : (i + 1) * width] for i in range(hidden // width)]
            + [jnp.zeros((8, width), jnp.float32)],
            axis=0,
        )
    )

    low_table = r.low_table
    low_table[pl.ds(0, rows_dev), :] = low(r.table[...])
    pad_rows = low_table.shape[0] - rows_dev
    low_table[pl.ds(rows_dev, pad_rows), :] = jnp.zeros((pad_rows, width), jnp.bfloat16)
    keys = r.keys
    keys[...] = jnp.zeros_like(keys)
    home = r.home[...]
    used = home.shape[0]
    keys[pl.ds(0, used), pl.ds(0, 128)] = wide(lax.div(home, 256))
    keys[pl.ds(0, used), pl.ds(128, 128)] = wide(lax.rem(home, 256))
    home_look = low(jnp.transpose(keys[:, 0:256]))
    ids_all = r.ids[:, pl.ds(pl.multiple_of(core * tokens, tokens), tokens)]
    lane_of = iota_of((128, tokens), 0)
    key_of = iota_of((key_rows, tokens), 0)

    def look(table_t, ids_row, parts):
        hot = low(wide(key_of == lax.div(ids_row, 128)))
        picked = dot_nn(table_t, hot)
        mask = lane_of == lax.rem(ids_row, 128)
        return [
            jnp.sum(jnp.where(mask, picked[128 * i : 128 * i + 128], 0.0), axis=0, keepdims=True)
            for i in range(parts)
        ]

    home_rows = []
    for d in range(chips):
        top, bottom = look(home_look, ids_all[d : d + 1, :], 2)
        home_rows.append(top * 256.0 + bottom)
    home_all = jnp.concatenate(home_rows, axis=0)
    r.home_all[...] = home_all

    pl.semaphore_wait(barrier, chips)
    gather_a.start()

    upper = low(wide(iota_of((tokens, tokens), 0) <= iota_of((tokens, tokens), 1)))
    first_row = wide(chip * rows_dev)
    local_all = home_all - first_row
    owned = (local_all >= 0.0) & (local_all < float(rows_dev))
    rank = dot_nn(low(wide(owned)), upper) - 1.0
    slot_rank = wide(iota_of((capacity, tokens), 0))
    wanted = []
    for d in range(chips):
        chosen = (rank[d : d + 1, :] == slot_rank) & owned[d : d + 1, :]
        wanted.append(
            jnp.sum(jnp.where(chosen, local_all[d : d + 1, :] + 1.0, 0.0), axis=1, keepdims=True) - 1.0
        )
    wanted = jnp.concatenate(wanted, axis=0)
    asked = chips * capacity
    lanes = low_table.shape[0]
    hot_rows = low(wide(iota_of((asked, lanes), 1) == wanted.astype(jnp.int32)))
    out_rows = low(dot_nn(hot_rows, low_table[...])).reshape(chips, capacity, width)
    r.row_out[...] = out_rows
    r.row_in[chip] = r.row_out[chip]
    rows_there = Scatter(place, r.row_out, r.row_in, r.row_send, r.row_recv)
    rows_there.start()
    wanted_row = jnp.transpose(jnp.broadcast_to(wanted, (asked, 128)))[0:1, :]
    r.asked[core] = wanted_row
    asked_copy = remote(
        r.asked.at[core], r.asked.at[core], r.asked_send, r.asked_recv, chip, 1 - core
    )
    asked_copy.start()

    own_home = r.home_all[pl.ds(chip, 1), :]
    owner_first = wide(iota_of((chips, tokens), 0) * rows_dev)
    at_owner = (own_home >= owner_first) & (own_home < owner_first + float(rows_dev))
    own_rank = dot_nn(low(wide(at_owner)), upper) - 1.0
    spread = jnp.concatenate(
        [
            wide((own_rank[o : o + 1, :] == slot_rank) & at_owner[o : o + 1, :])
            for o in range(chips)
        ],
        axis=0,
    )
    r.spread[...] = low(spread)

    freq = r.freq[...]
    for i, piece in enumerate(pieces_of(freq)):
        keys[pl.ds(0, used), pl.ds(128 * i, 128)] = piece
    freq_look = low(jnp.transpose(keys[...]))
    own_ids = r.ids[pl.ds(chip, 1), pl.ds(pl.multiple_of(core * tokens, tokens), tokens)]
    fa, fb, fc = look(freq_look, own_ids, 3)
    own_length = r.lengths[chip]
    row_pos = core * tokens + iota_of((1, tokens), 1)
    is_cand = (row_pos >= 1) & (row_pos < own_length)
    own_corr = jnp.where(is_cand, fa + fb + fc, -big_negative)
    r.corr[chip] = own_corr
    r.corr_pair[core] = own_corr
    spread_corr.start()
    pair_corr.start()

    def turned(row):
        return jnp.transpose(jnp.broadcast_to(row, (128, tokens)))[:, 0:1]

    corr_col = turned(own_corr)
    r.corr_col[...] = jnp.broadcast_to(corr_col, (tokens, 128))

    total_events = jnp.float32(0.0)
    for d in range(chips):
        total_events = total_events + wide(r.lengths[d] - 1)
    col_pos = core * tokens + iota_of((tokens, 1), 0)
    is_event = col_pos + 1 < own_length

    gather_a.advance(3)
    gather_b.start()
    rows_there.arrived()
    embedded = low(dot_tn(r.spread[...], r.row_in[...].reshape(asked, width)))
    cand_buf[chip] = embedded
    r.emb_pair[core] = embedded
    gather_c.start()
    pair_emb.start()
    gather_a.complete()
    pair_a.start()
    gather_b.advance(3)
    pair_a.wait_recv()
    qkv_w, pos_w, gain_w = r.qkv_w, r.pos_w, r.gain_w

    def unpack_a(index, carry):
        one, two = wide(wa[0, index]), wide(wa[1, index])
        qkv_w[pl.ds(pl.multiple_of(index * 48, 16), 48), :] = low(jnp.concatenate([one[0:24], two[0:24]], axis=0))
        gain_w[pl.ds(pl.multiple_of(index * 16, 16), 16), :] = jnp.concatenate([one[24:32], two[24:32]], axis=0)[:, 0:128]
        early = jnp.concatenate([one[32:40], two[32:40]], axis=0)
        late = jnp.concatenate([one[40:48], two[40:48]], axis=0)
        pos_w[pl.ds(pl.multiple_of(index * 16, 16), 16), :] = jnp.where(core == 0, early, late)
        return carry

    lax.fori_loop(0, chips, unpack_a, 0)
    gain_rows = jnp.transpose(gain_w[...])[0:8, :]
    r.gain_rows[...] = gain_rows
    gain_one, gain_two, gain_three = (r.gain_rows[i : i + 1, :] for i in range(3))

    resid_zero = wide(cand_buf[chip]) + jnp.transpose(pos_w[...])
    r.resid_zero[...] = resid_zero
    normed, _ = rms_apply(resid_zero, gain_one)
    r.input_one[...] = low(normed)
    qkv_own = low(dot_nt(r.input_one[...], qkv_w[...]))
    kv = r.kv
    kv[0] = qkv_own[:, width : 3 * width]
    kv_copy = remote(kv.at[0], kv.at[1], r.kv_send, r.kv_recv, chip, 1 - core)
    kv_copy.start()

    kv_copy.wait_recv()

    head_dim = width // HEADS
    scaling = head_dim ** (-0.5)
    causal = iota_of((tokens, tokens), 1) <= iota_of((tokens, tokens), 0)
    other_bias = jnp.where(core == 0, big_negative, 0.0)
    head_lane = lax.div(iota_of((1, width), 1), head_dim)
    prob = r.prob
    zero_low = jnp.zeros((), jnp.bfloat16)
    both = 2 * tokens

    def of_head(values, head):
        return jnp.where(head_lane == head, values, zero_low)

    def rows_of(head, size=tokens):
        return slice(head * size, (head + 1) * size)

    def stack(to, values):
        for head in range(HEADS):
            to[rows_of(head), :] = of_head(values, head)

    def stack_pair(to, pair, lanes):
        for head in range(HEADS):
            to[rows_of(2 * head), :] = of_head(pair[0, :, lanes], head)
            to[rows_of(2 * head + 1), :] = of_head(pair[1, :, lanes], head)

    stack(r.query_rows, qkv_own[:, 0:width])
    stack_pair(r.value_rows, kv, slice(width, 2 * width))

    def attend(head):
        query = r.query_rows[rows_of(head), :]
        own = dot_nt(query, kv[0, :, 0:width]) * scaling
        own = jnp.where(causal, own, big_negative)
        other = dot_nt(query, kv[1, :, 0:width]) * scaling + other_bias
        peak = jnp.max(jnp.maximum(own, other), axis=-1, keepdims=True)
        own = jnp.exp(own - peak)
        other = jnp.exp(other - peak)
        share = 1.0 / jnp.sum(own + other, axis=-1, keepdims=True)
        own = own * share
        other = other * share
        prob[head, :, 0:tokens] = own
        prob[head, :, tokens:both] = other
        own, other = low(own), low(other)
        r.prob_own[rows_of(head), :] = own
        r.prob_other[rows_of(head), :] = other
        r.prob_lanes[:, rows_of(2 * head)] = own
        r.prob_lanes[:, rows_of(2 * head + 1)] = other

    for head in range(HEADS):
        attend(head)
    gather_b.complete()
    pair_b.start()
    gather_c.advance(2)
    pair_b.wait_recv()
    merge_w, widen_w, narrow_w = r.merge_w, r.widen_w, r.narrow_w

    def unpack_b(index, carry):
        one, two = wide(wb[0, index]), wide(wb[1, index])
        at16 = pl.ds(pl.multiple_of(index * 16, 16), 16)
        merge_w[at16, :] = low(jnp.concatenate([one[0:8], two[0:8]], axis=0))
        widen_w[pl.ds(pl.multiple_of(index * 64, 16), 64), :] = low(jnp.concatenate([one[8:40], two[8:40]], axis=0))
        for i in range(hidden // width):
            top = 40 + 8 * i
            narrow_w[at16, pl.ds(i * width, width)] = low(
                jnp.concatenate([one[top : top + 8], two[top : top + 8]], axis=0)
            )
        return carry

    lax.fori_loop(0, chips, unpack_b, 0)
    r.attended[...] = low(dot_nn(r.prob_lanes[...], r.value_rows[...]))
    resid_one = r.resid_zero[...] + dot_nt(r.attended[...], merge_w[...])
    r.resid_one[...] = resid_one
    normed, _ = rms_apply(resid_one, gain_two)
    r.input_two[...] = low(normed)
    r.resid_two[...] = resid_one
    for i in range(hidden // FF_CHUNK):
        part = slice(i * FF_CHUNK, (i + 1) * FF_CHUNK)
        act, slope = gelu_both(dot_nt(r.input_two[...], widen_w[part, :]))
        r.act[:, part] = low(act)
        r.slope[:, part] = slope
    r.resid_two[...] += dot_nt(r.act[...], narrow_w[...])
    normed, _ = rms_apply(r.resid_two[...], gain_three)
    user_buf[chip] = low(normed)
    r.user_pair[core] = user_buf[chip]
    gather_u.start()
    pair_user.start()

    gather_c.advance(2)
    spread_corr.arrived()
    pair_emb.wait_recv()
    pair_corr.wait_recv()
    shifted = jnp.concatenate([wide(cand_buf[chip])[1:, :], wide(r.emb_pair[1, pl.ds(0, 16), :])[0:1, :]], axis=0)
    target_corr = jnp.concatenate([corr_col[1:, :], r.corr_pair[1][:, 0:1]], axis=0)
    target_logit = jnp.sum(wide(user_buf[chip]) * shifted, axis=-1, keepdims=True) - target_corr
    target_logit = jnp.where(is_event, target_logit, 0.0)
    pair_user.wait_recv()
    users = r.user_pair[...].reshape(2 * tokens, width)
    logit_buf, peaks, totals, acc = r.logit, r.peaks, r.totals, r.acc
    totals[...] = jnp.zeros_like(totals)
    acc[...] = jnp.zeros_like(acc)
    group = chips // CHUNKS
    pair_row = iota_of((both, tokens), 0)
    pair_col = core * tokens + iota_of((both, tokens), 1)

    def fold(values, how):
        parts = [values[:, i : i + 128] for i in range(0, values.shape[1], 128)]
        return functools.reduce(how, parts)

    peak = jnp.full((both, 1), big_negative, jnp.float32)
    for chunk in range(CHUNKS):
        gather_c.advance(1)
        gather_c.need(range(group * chunk, group * (chunk + 1)))
        peaks[...] = jnp.broadcast_to(peak, peaks.shape)

        steps = range(chunk * group, (chunk + 1) * group)
        for index, step in enumerate(steps):
            there = place.relative(step)
            logits = dot_nt(users, cand_buf[there]) - r.corr[there]
            logit_buf[index] = logits
            peaks[...] = jnp.maximum(peaks[...], fold(logits, jnp.maximum))
        before, peak = peak, jnp.max(peaks[...], axis=-1, keepdims=True)
        scale = jnp.exp(before - peak)
        totals[...] *= scale
        acc[...] *= scale
        if chunk > 0:
            gather_u.advance(1)

        for index, step in enumerate(steps):
            expo = jnp.exp(logit_buf[index] - peak)
            totals[...] += fold(expo, jnp.add)
            if step == 0:
                expo = jnp.where(pair_col == pair_row + 1, 0.0, expo)
            acc[...] += dot_nn(low(expo), cand_buf[place.relative(step)])
    total = jnp.sum(totals[...], axis=-1, keepdims=True)
    peaks[...] = jnp.broadcast_to(peak, peaks.shape)
    totals[...] = jnp.broadcast_to(total, totals.shape)
    own_rows = pl.ds(pl.multiple_of(core * tokens, tokens), tokens)
    other_rows = pl.ds(pl.multiple_of((1 - core) * tokens, tokens), tokens)
    soft_out, soft_in = r.soft_out, r.soft_in
    soft_out[:, 0:width] = acc[other_rows, :]
    soft_out[:, width : width + 128] = peaks[other_rows, :]
    soft_out[:, width + 128 : width + 256] = totals[other_rows, :]
    pair_soft.start()
    pair_soft.wait_recv()
    own_peak, own_total = peaks[own_rows, :][:, 0:1], totals[own_rows, :][:, 0:1]
    other_peak = soft_in[:, width : width + 1]
    peak = jnp.maximum(own_peak, other_peak)
    own_scale, other_scale = jnp.exp(own_peak - peak), jnp.exp(other_peak - peak)
    total = own_total * own_scale + soft_in[:, width + 128 : width + 129] * other_scale
    soft = acc[own_rows, :] * own_scale + soft_in[:, 0:width] * other_scale
    log_total = peak + jnp.log(total)
    loss_own = jnp.sum(jnp.where(is_event, log_total - target_logit, 0.0), axis=0, keepdims=True)
    weight = jnp.where(is_event, 1.0 / total_events, 0.0)
    target_coef = wide(low(weight * (jnp.exp(target_logit - log_total) - 1.0)))
    user_grad = soft * (weight / total) + target_coef * shifted
    shift_col = jnp.where(is_event, log_total + jnp.log(total_events), -big_negative)
    norm_buf = r.norm
    norm_buf[chip] = jnp.transpose(jnp.broadcast_to(shift_col, (tokens, 128)))[0:1, :]
    spread_norm.start()
    grad_two, gain_grad_three = rms_back(
        user_grad, r.resid_two[...],
        lax.rsqrt(jnp.mean(r.resid_two[...] * r.resid_two[...], axis=-1, keepdims=True) + norm_eps),
        gain_three,
    )
    branch_two = low(grad_two)
    narrow_grad = dot_tn(branch_two, r.act[...])
    r.pre[...] = low(dot_nn(branch_two, narrow_w[...]) * r.slope[...])
    widen_grad = dot_tn(r.pre[...], r.input_two[...])
    resid_one = r.resid_one[...]
    inverse_two = lax.rsqrt(jnp.mean(resid_one * resid_one, axis=-1, keepdims=True) + norm_eps)
    from_two, gain_grad_two = rms_back(dot_nn(r.pre[...], widen_w[...]), resid_one, inverse_two, gain_two)
    grad_one = grad_two + from_two
    r.grad_one[...] = grad_one
    branch_one = low(grad_one)
    merge_grad = dot_tn(branch_one, r.attended[...])
    r.mixed[...] = low(dot_nn(branch_one, merge_w[...]))

    tail, head_pack = r.tail_pack, r.head_pack
    for d in range(2 * chips):
        at = (d % 2, d // 2 % 4, d // 8)
        tail[*at, pl.ds(0, 32), :] = low(widen_grad[32 * d : 32 * d + 32])
        tail[*at, pl.ds(32, 32), :] = low(
            jnp.concatenate(
                [
                    narrow_grad[8 * d : 8 * d + 8, i * width : (i + 1) * width]
                    for i in range(hidden // width)
                ],
                axis=0,
            )
        )
    reduce_tail = Reduce(place, tail, r.tail_pair, r.tail_sum, r.tail_plane, r.tail_part, r.tail_line, r.tail_sems)
    reduce_head = Reduce(place, head_pack, r.head_pair, r.head_sum, r.head_plane, r.head_part, r.head_line, r.head_sems)
    reduce_tail.to_pair()
    gather_u.advance(1)
    stack(r.mixed_rows, r.mixed[...])
    stack_pair(r.key_rows, kv, slice(0, width))

    def attend_back(head):
        mixed = r.mixed_rows[rows_of(head), :]
        own, other = prob[head, :, 0:tokens], prob[head, :, tokens:both]
        own_grad = dot_nt(mixed, kv[0, :, width : 2 * width])
        other_grad = dot_nt(mixed, kv[1, :, width : 2 * width])
        inner = jnp.sum(own * own_grad + other * other_grad, axis=-1, keepdims=True)
        own_score = low(own * (own_grad - inner))
        other_score = low(other * (other_grad - inner))
        r.score_own[rows_of(head), :] = own_score
        r.score_other[rows_of(head), :] = other_score
        r.score_lanes[:, rows_of(2 * head)] = own_score
        r.score_lanes[:, rows_of(2 * head + 1)] = other_score

    for head in range(HEADS):
        attend_back(head)
        if head == 1:
            gather_u.advance(1)
        if head == 3:
            reduce_tail.to_plane()
            gather_u.advance(1)
        if head == 5:
            gather_u.advance(1)
    back = r.back
    back[0, :, 0:width] = low(dot_tn(r.score_other[...], r.query_rows[...]) * scaling)
    back[0, :, width : 2 * width] = low(dot_tn(r.prob_other[...], r.mixed_rows[...]))
    back_copy = remote(back.at[0], back.at[1], r.back_send, r.back_recv, chip, 1 - core)
    back_copy.start()
    qkv_grad = r.qkv_grad
    qkv_grad[:, 0:width] = low(dot_nn(r.score_lanes[...], r.key_rows[...]) * scaling)
    key_own = dot_tn(r.score_own[...], r.query_rows[...]) * scaling
    value_own = dot_tn(r.prob_own[...], r.mixed_rows[...])
    back_copy.wait_recv()
    qkv_grad[:, width : 2 * width] = low(key_own + wide(back[1, :, 0:width]))
    qkv_grad[:, 2 * width : 3 * width] = low(value_own + wide(back[1, :, width : 2 * width]))
    qkv_wgrad = dot_tn(qkv_grad[...], r.input_one[...])
    resid_zero = r.resid_zero[...]
    inverse_one = lax.rsqrt(jnp.mean(resid_zero * resid_zero, axis=-1, keepdims=True) + norm_eps)
    from_one, gain_grad_one = rms_back(dot_nn(qkv_grad[...], qkv_w[...]), resid_zero, inverse_one, gain_one)
    resid_grad = r.grad_one[...] + from_one
    r.resid_grad[...] = resid_grad
    pos_grad = jnp.transpose(resid_grad)
    nothing = jnp.zeros((8, width), jnp.float32)
    for d in range(2 * chips):
        at = (d % 2, d // 2 % 4, d // 8)
        head_pack[*at, pl.ds(0, 32), :] = low(
            jnp.concatenate([qkv_wgrad[24 * d : 24 * d + 24], merge_grad[8 * d : 8 * d + 8]], axis=0)
        )
        pos_piece = pos_grad[8 * d : 8 * d + 8]
        head_pack[*at, pl.ds(32, 16), :] = low(
            jnp.concatenate(
                [jnp.where(core == 0, pos_piece, nothing), jnp.where(core == 0, nothing, pos_piece)], axis=0
            )
        )
    reduce_head.to_pair()
    gain_buf = r.gain_buf
    gain_buf[chip] = jnp.concatenate([gain_grad_one, gain_grad_two, gain_grad_three], axis=1)
    gain_there = Scatter(place, None, gain_buf, r.gain_send, r.gain_recv)
    gain_there.start()
    gather_u.complete()
    spread_norm.arrived()
    cand_grad = r.acc
    cand_grad[...] = jnp.zeros_like(cand_grad)
    both_cand = r.emb_pair[...].reshape(both, width)
    both_corr = jnp.concatenate([turned(r.corr_pair[0]), turned(r.corr_pair[1])], axis=0)
    event_row = jnp.where(row_pos + 1 < own_length, 1.0 / total_events, 0.0)

    def give_block(there, own):
        block_rows = user_buf[there]
        coef = jnp.exp((dot_nt(both_cand, block_rows) - both_corr) - norm_buf[there])
        if own:
            coef = coef - jnp.where((pair_row == pair_col + 1) & (both_corr < 1e29), event_row, 0.0)
        cand_grad[...] += dot_nn(low(coef), block_rows)

    for step in range(chips):
        give_block(place.relative(step), step == 0)
    r.cand_out[...] = cand_grad[other_rows, :]
    pair_cand.start()
    reduce_head.to_plane()
    pair_cand.wait_recv()

    emb_grad = low(r.resid_grad[...] + (cand_grad[own_rows, :] + r.cand_in[...]))
    back_out, back_in = r.back_out, r.back_in
    back_out[...] = low(dot_nn(r.spread[...], emb_grad)).reshape(chips, capacity, width)
    back_in[core, chip] = back_out[chip]
    rows_back = Scatter(place, back_out, back_in.at[core], r.rows_send, r.rows_recv)
    rows_back.start()
    reduce_tail.to_line()
    asked_copy.wait_recv()
    asked_all = jnp.concatenate([r.asked[0], r.asked[1]], axis=1).astype(jnp.int32)
    part_rows = TABLE_PART if rows_dev % TABLE_PART == 0 else 8
    parts = [pl.ds(first, part_rows) for first in range(0, rows_dev, part_rows)]
    for part in parts:
        r.hot[part, :] = low(wide(iota_of((part_rows, 2 * asked), 0) + part.start == asked_all))

    reduce_head.to_line()
    shard = r.shard_grad
    shard[0:64] = reduce_tail.total()
    shard[64:112] = reduce_head.total()
    total = shard[...]
    gain_there.arrived()
    gain_total = gain_buf[0]
    for step in range(1, chips):
        gain_total = gain_total + gain_buf[step]
    gain_pair = r.gain_pair
    gain_pair[core] = gain_total
    gain_copy = remote(gain_pair.at[core], gain_pair.at[core], r.gp_send, r.gp_recv, chip, 1 - core)
    gain_copy.start()
    gain_copy.wait_recv()
    gain_total = gain_pair[0] + gain_pair[1]
    gain_three_rows = [gain_total[:, i * width : (i + 1) * width] for i in range(3)]
    gain_w[:, 0:8] = jnp.transpose(jnp.concatenate(gain_three_rows + [jnp.zeros((5, width), jnp.float32)], axis=0))
    r.gain_grad[...] = gain_w[pl.ds(pl.multiple_of(me * 8, 8), 8), :]
    gain_lane = iota_of((1, 3 * width), 1)
    gain_mine = lax.div(lax.rem(gain_lane, width), 8) == me
    square = jnp.sum(total * total, axis=0, keepdims=True)
    square = jnp.sum(square, axis=1, keepdims=True)
    square = square + jnp.sum(jnp.where(gain_mine, gain_total * gain_total, 0.0), axis=1, keepdims=True)

    rows_back.arrived()
    rows_pair = remote(back_in.at[core], back_in.at[core], r.rp_send, r.rp_recv, chip, 1 - core)
    rows_pair.start()
    rows_pair.wait_recv()
    table_grad = r.table_grad
    incoming = back_in[...].reshape(2 * asked, width)
    table_square = jnp.zeros((1, width), jnp.float32)
    for part in parts:
        grads = dot_nn(r.hot[part, :], incoming)
        table_grad[part, :] = grads
        table_square = table_square + jnp.sum(grads * grads, axis=0, keepdims=True)
    square = square + 0.5 * jnp.sum(table_square, axis=1, keepdims=True)

    scalar_buf = r.scalar_buf
    lane = iota_of((1, 128), 1)
    r.scalar_pair[core] = jnp.where(lane == 0, square, jnp.where(lane == 1, loss_own, 0.0))
    pair_sums.start()
    pair_sums.wait_recv()
    scalar_buf[chip] = r.scalar_pair[0] + r.scalar_pair[1]
    spread_sums.start()
    gather_a.sent()
    gather_b.sent()
    gather_c.sent()
    gather_u.sent()
    rows_there.sent()
    rows_back.sent()
    gain_there.sent()
    spread_corr.sent()
    spread_norm.sent()
    reduce_tail.sent()
    reduce_head.sent()
    pairs = (pair_a, pair_b, pair_emb, pair_corr, pair_user, pair_soft, pair_cand, pair_sums)
    for copy in (asked_copy, kv_copy, back_copy, gain_copy, rows_pair, *pairs):
        copy.wait_send()
    spread_sums.arrived()
    sums = scalar_buf[0]
    for d in range(1, chips):
        sums = sums + scalar_buf[d]
    r.sums[...] = jnp.where(lane == 2, total_events, sums)
    spread_sums.sent()


TABLE_PART = 224
CHUNKS = 4
ENDS = dict(
    ids=0, lengths=0, home=0, freq=0, table=0, pos=0, qkv=0, merge=0, widen=0, narrow=0, gains=0,
    table_grad=1, shard_grad=1, gain_grad=1, sums=1,
)


def scratch_of(sizes):
    (chips, rows_dev, seq_len, width, hidden, capacity, tokens, key_rows) = sizes
    f32, b16 = jnp.float32, jnp.bfloat16
    devices, levels = 2 * chips, chips // 4
    dma = pltpu.SemaphoreType.DMA
    lanes = -(-rows_dev // 128) * 128
    if lanes == rows_dev:
        lanes += 128
    sends = Gather.sends(chips)
    shapes = dict(
        wa=pltpu.VMEM((2, chips, 48, width), b16),
        wb=pltpu.VMEM((2, chips, 80, width), b16),
        cand=pltpu.VMEM((chips, tokens, width), b16),
        corr=pltpu.VMEM((chips, 1, tokens), f32),
        logit=pltpu.VMEM((chips // CHUNKS, 2 * tokens, tokens), f32),
        user=pltpu.VMEM((chips, tokens, width), b16),
        emb_pair=pltpu.VMEM((2, tokens, width), b16),
        corr_pair=pltpu.VMEM((2, 1, tokens), f32),
        user_pair=pltpu.VMEM((2, tokens, width), b16),
        soft_out=pltpu.VMEM((tokens, width + 256), f32),
        soft_in=pltpu.VMEM((tokens, width + 256), f32),
        cand_out=pltpu.VMEM((tokens, width), f32),
        cand_in=pltpu.VMEM((tokens, width), f32),
        wa_pair=dma((2,)), wb_pair=dma((2,)), emb_sems=dma((2,)), corr_sems=dma((2,)),
        user_sems=dma((2,)), soft_sems=dma((2,)), cand_sems=dma((2,)),
        low_table=pltpu.VMEM((lanes, width), b16),
        keys=pltpu.VMEM((key_rows, 384), f32),
        home_all=pltpu.VMEM((chips, tokens), f32),
        row_out=pltpu.VMEM((chips, capacity, width), b16),
        row_in=pltpu.VMEM((chips, capacity, width), b16),
        asked=pltpu.VMEM((2, 1, chips * capacity), f32),
        spread=pltpu.VMEM((chips * capacity, tokens), b16),
        corr_col=pltpu.VMEM((tokens, 128), f32),
        qkv_w=pltpu.VMEM((3 * width, width), b16),
        pos_w=pltpu.VMEM((width, tokens), f32),
        gain_w=pltpu.VMEM((width, 128), f32),
        turn=pltpu.VMEM((128, 128), f32),
        gain_rows=pltpu.VMEM((8, width), f32),
        merge_w=pltpu.VMEM((width, width), b16),
        widen_w=pltpu.VMEM((hidden, width), b16),
        narrow_w=pltpu.VMEM((width, hidden), b16),
        resid_zero=pltpu.VMEM((tokens, width), f32),
        resid_one=pltpu.VMEM((tokens, width), f32),
        resid_two=pltpu.VMEM((tokens, width), f32),
        input_one=pltpu.VMEM((tokens, width), b16),
        input_two=pltpu.VMEM((tokens, width), b16),
        query_rows=pltpu.VMEM((HEADS * tokens, width), b16),
        mixed_rows=pltpu.VMEM((HEADS * tokens, width), b16),
        key_rows=pltpu.VMEM((2 * HEADS * tokens, width), b16),
        value_rows=pltpu.VMEM((2 * HEADS * tokens, width), b16),
        prob_own=pltpu.VMEM((HEADS * tokens, tokens), b16),
        prob_other=pltpu.VMEM((HEADS * tokens, tokens), b16),
        prob_lanes=pltpu.VMEM((tokens, 2 * HEADS * tokens), b16),
        score_own=pltpu.VMEM((HEADS * tokens, tokens), b16),
        score_other=pltpu.VMEM((HEADS * tokens, tokens), b16),
        score_lanes=pltpu.VMEM((tokens, 2 * HEADS * tokens), b16),
        kv=pltpu.VMEM((2, tokens, 2 * width), b16),
        prob=pltpu.VMEM((HEADS, tokens, 2 * tokens), f32),
        acc=pltpu.VMEM((2 * tokens, width), f32),
        attended=pltpu.VMEM((tokens, width), b16),
        act=pltpu.VMEM((tokens, hidden), b16),
        slope=pltpu.VMEM((tokens, hidden), f32),
        pre=pltpu.VMEM((tokens, hidden), b16),
        peaks=pltpu.VMEM((2 * tokens, 128), f32),
        totals=pltpu.VMEM((2 * tokens, 128), f32),
        norm=pltpu.VMEM((chips, 1, tokens), f32),
        grad_one=pltpu.VMEM((tokens, width), f32),
        mixed=pltpu.VMEM((tokens, width), b16),
        tail_pack=pltpu.VMEM((2, 4, levels, 64, width), b16),
        tail_pair=pltpu.VMEM((4, levels, 64, width), b16),
        tail_sum=pltpu.VMEM((4, levels, 64, width), b16),
        tail_plane=pltpu.VMEM((4, levels, 64, width), b16),
        tail_part=pltpu.VMEM((levels, 64, width), b16),
        tail_line=pltpu.VMEM((levels, 64, width), b16),
        tail_sems=dma((10 + 2 * levels,)),
        head_pack=pltpu.VMEM((2, 4, levels, 48, width), b16),
        head_pair=pltpu.VMEM((4, levels, 48, width), b16),
        head_sum=pltpu.VMEM((4, levels, 48, width), b16),
        head_plane=pltpu.VMEM((4, levels, 48, width), b16),
        head_part=pltpu.VMEM((levels, 48, width), b16),
        head_line=pltpu.VMEM((levels, 48, width), b16),
        head_sems=dma((10 + 2 * levels,)),
        back=pltpu.VMEM((2, tokens, 2 * width), b16),
        qkv_grad=pltpu.VMEM((tokens, 3 * width), b16),
        resid_grad=pltpu.VMEM((tokens, width), f32),
        gain_buf=pltpu.VMEM((chips, 1, 3 * width), f32),
        gain_pair=pltpu.VMEM((2, 1, 3 * width), f32),
        back_out=pltpu.VMEM((chips, capacity, width), b16),
        back_in=pltpu.VMEM((2, chips, capacity, width), b16),
        hot=pltpu.VMEM((rows_dev, 2 * chips * capacity), b16),
        scalar_buf=pltpu.VMEM((chips, 1, 128), f32),
        scalar_pair=pltpu.VMEM((2, 1, 128), f32),
        sums_sems=dma((2,)),
        wa_send=dma((sends,)), wa_recv=dma((chips,)),
        wb_send=dma((sends,)), wb_recv=dma((chips,)),
        cand_send=dma((sends,)), cand_recv=dma((chips,)),
        user_send=dma((sends,)), user_recv=dma((chips,)),
        row_send=dma((chips,)), row_recv=dma((chips,)),
        rows_send=dma((chips,)), rows_recv=dma((chips,)),
        gain_send=dma((chips,)), gain_recv=dma((chips,)),
        norm_send=dma((chips,)), norm_recv=dma((chips,)),
        corr_send=dma((chips,)), corr_recv=dma((chips,)),
        scalar_send=dma((chips,)), scalar_recv=dma((chips,)),
        asked_send=dma, asked_recv=dma,
        kv_send=dma, kv_recv=dma,
        back_send=dma, back_recv=dma,
        gp_send=dma, gp_recv=dma,
        rp_send=dma, rp_recv=dma,
    )
    return shapes


def adam(weight, first, second, grad, rate):
    first = beta_one * first + (1.0 - beta_one) * grad
    second = beta_two * second + (1.0 - beta_two) * grad * grad
    fix_one = 1.0 - beta_one**STEP
    fix_two = 1.0 - beta_two**STEP
    update = first / fix_one / (jnp.sqrt(second / fix_two) + adam_eps) + decay_rate * weight
    return weight - rate * update, first, second


def update_kernel(*refs):
    (table_grad, shard, gain_grad, sums), refs = refs[:4], refs[4:]
    ins, outs, turn = refs[:21], refs[21:-1], refs[-1]
    square = sums[0:1, 0:1]
    norm = jnp.sqrt(square)
    factor = jnp.minimum(1.0, clip_limit / norm)

    def update(index, grad, rate):
        new = adam(*(ref[...] for ref in ins[3 * index : 3 * index + 3]), grad * factor, rate)
        for ref, value in zip(outs[3 + 3 * index : 6 + 3 * index], new):
            ref[...] = value

    update(0, table_grad[...], learn_rate)

    @pl.when(pl.program_id(0) == 0)
    def _():
        outs[0][...] = sums[0:1, 1:2]
        outs[1][...] = sums[0:1, 2:3]
        outs[2][...] = norm
        update(1, jnp.concatenate([shard[96:104, :], shard[104:112, :]], axis=1), learn_rate)
        update(2, shard[64:88, :], learn_rate)
        update(3, shard[88:96, :], learn_rate)
        update(4, shard[0:32, :], learn_rate)
        update(5, jnp.concatenate([shard[32 + 8 * i : 40 + 8 * i, :] for i in range(4)], axis=1), learn_rate)
        turn[0:8, :] = gain_grad[...]
        update(6, jnp.transpose(turn[...])[0:3, 0:8], gain_rate)


def fused_body(*args):
    (item_ids, lengths, home_row, log_freq) = args[:4]
    weights = args[4:]
    item_table = weights[0]
    rows_dev, width = item_table.shape
    chips = lax.axis_size("dp")
    seq_len = item_ids.shape[1]
    tokens = seq_len // 2
    hidden = weights[12].shape[1] * 2 * chips
    capacity = 2 * tokens // chips
    key_rows = -(-home_row.shape[0] // (128 * 128)) * 128
    sizes = (chips, rows_dev, seq_len, width, hidden, capacity, tokens, key_rows)
    dense = [w.T for w in weights[3:18]]
    shapes = scratch_of(sizes)
    vmem = pl.BlockSpec(memory_space=pltpu.VMEM)
    smem = pl.BlockSpec(memory_space=pltpu.SMEM)
    f32 = jnp.float32
    table_grad, shard, gain_grad, sums = pl.pallas_call(
        functools.partial(step_kernel, sizes),
        out_shape=[
            jax.ShapeDtypeStruct((rows_dev, width), f32),
            jax.ShapeDtypeStruct((112, width), f32),
            jax.ShapeDtypeStruct((8, 128), f32),
            jax.ShapeDtypeStruct((1, 128), f32),
        ],
        in_specs=[vmem, smem] + [vmem] * 9,
        out_specs=[vmem] * 4,
        scratch_shapes=list(shapes.values()),
        compiler_params=pltpu.CompilerParams(
            collective_id=0, has_side_effects=True, vmem_limit_bytes=60 * 2**20
        ),
    )(
        item_ids, lengths, home_row.reshape(-1, 128), log_freq.reshape(-1, 128), item_table,
        dense[0], dense[3], dense[6], dense[9], dense[12], weights[18],
    )
    part = rows_dev // 2 if rows_dev % 16 == 0 else rows_dev
    table_spec = pl.BlockSpec((part, width), lambda i: (i, 0))

    def whole(x):
        return pl.BlockSpec(x.shape, lambda i: (0,) * len(x.shape))

    small = dense + [weights[18], weights[19], weights[20]]
    one = jax.ShapeDtypeStruct((1, 1), f32)
    outs = pl.pallas_call(
        update_kernel,
        grid=(rows_dev // part,),
        out_shape=[one] * 3 + [jax.ShapeDtypeStruct(x.shape, f32) for x in list(weights[:3]) + small],
        in_specs=[table_spec, whole(shard), whole(gain_grad), whole(sums)] + [table_spec] * 3 + [whole(x) for x in small],
        out_specs=[whole(one)] * 3 + [table_spec] * 3 + [whole(x) for x in small],
        scratch_shapes=[pltpu.VMEM((128, 128), f32)],
        compiler_params=pltpu.CompilerParams(vmem_limit_bytes=60 * 2**20),
    )(table_grad, shard, gain_grad, sums, *weights[:3], *small)
    outs = list(outs)
    return tuple(
        [x.reshape(()) for x in outs[:3]] + outs[3:6] + [x.T for x in outs[6:21]] + outs[21:]
    )


def solution(mesh):
    placed = (
        P(),
        P(),
        P(),
        P(),
        P("dp", None),
        P("dp", None),
        P("dp", None),
        P(None, ("dp", "sub")),
        P(None, ("dp", "sub")),
        P(None, ("dp", "sub")),
        P(None, ("dp", "sub")),
        P(None, ("dp", "sub")),
        P(None, ("dp", "sub")),
        P(None, ("dp", "sub")),
        P(None, ("dp", "sub")),
        P(None, ("dp", "sub")),
        P(None, ("dp", "sub")),
        P(None, ("dp", "sub")),
        P(None, ("dp", "sub")),
        P(None, ("dp", "sub")),
        P(None, ("dp", "sub")),
        P(None, ("dp", "sub")),
        P(None, ("dp", "sub")),
        P(None, ("dp", "sub")),
        P(None, ("dp", "sub")),
    )
    fits = mesh.shape["sub"] == 2 and mesh.shape["dp"] == 16
    return jax.shard_map(
        fused_body if fits else body,
        mesh=mesh,
        in_specs=placed,
        out_specs=(
            P(),
            P(),
            P(),
            P("dp", None),
            P("dp", None),
            P("dp", None),
            P(None, ("dp", "sub")),
            P(None, ("dp", "sub")),
            P(None, ("dp", "sub")),
            P(None, ("dp", "sub")),
            P(None, ("dp", "sub")),
            P(None, ("dp", "sub")),
            P(None, ("dp", "sub")),
            P(None, ("dp", "sub")),
            P(None, ("dp", "sub")),
            P(None, ("dp", "sub")),
            P(None, ("dp", "sub")),
            P(None, ("dp", "sub")),
            P(None, ("dp", "sub")),
            P(None, ("dp", "sub")),
            P(None, ("dp", "sub")),
            P(None, ("dp", "sub")),
            P(None, ("dp", "sub")),
            P(None, ("dp", "sub")),
        ),
        check_vma=False,
    )
```

```python
import functools
import math
import types

import jax
import jax.numpy as jnp
from jax import lax
from jax.experimental import pallas as pl
from jax.experimental.pallas import tpu as pltpu
from jax.sharding import PartitionSpec as P

HEADS = 8
STEP = 10


norm_eps = 1e-06
beta_one = 0.9
beta_two = 0.999
adam_eps = 1e-08
decay_rate = 0.01
learn_rate = 0.1
gain_rate = 0.5
clip_limit = 0.01
big_negative = -1e30
block_cols = 4096


def dot_plain(left_mat, right_mat):
    return jnp.dot(left_mat, right_mat, preferred_element_type=jnp.float32)


def dot_left_t(left_mat, right_mat):
    return lax.dot_general(
        left_mat, right_mat, (((0,), (0,)), ((), ())), preferred_element_type=jnp.float32
    )


def dot_right_t(left_mat, right_mat):
    return lax.dot_general(
        left_mat, right_mat, (((1,), (1,)), ((), ())), preferred_element_type=jnp.float32
    )


def rms_forward(values, gain_row):
    inverse = lax.rsqrt(jnp.mean(values * values, axis=-1, keepdims=True) + norm_eps)
    return (values * inverse * gain_row, inverse)


def rms_backward(upstream, values, inverse, gain_row):
    unit_vals = values * inverse
    gain_grad = jnp.sum(upstream * unit_vals, axis=0)
    scaled = upstream * gain_row
    inner_mean = jnp.mean(scaled * unit_vals, axis=-1, keepdims=True)
    return (inverse * (scaled - unit_vals * inner_mean), gain_grad)


def head_scores(queries, keys_all, allowed):
    scaling = queries.shape[-1] ** (-0.5)
    plain_scores = (
        jnp.einsum("bqhe,bkhe->bhqk", queries, keys_all, preferred_element_type=jnp.float32)
        * scaling
    )
    return jnp.where(allowed, plain_scores, big_negative)


def target_of(indices, slice_len, tokens_dev):
    within = indices % slice_len
    return jnp.where(within + 1 < slice_len, indices + 1, indices - within + tokens_dev)


def logits_for(user_rows, cand_rows, corr_rows, valid_rows):
    logits = dot_right_t(user_rows, cand_rows) - corr_rows[None, :]
    return jnp.where(valid_rows[None, :], logits, big_negative)


def coefficient(logits, log_total, weights, columns, targets):
    hits = (columns[None, :] == targets[:, None]).astype(jnp.float32)
    return (weights[:, None] * (jnp.exp(logits - log_total[:, None]) - hits)).astype(jnp.bfloat16)


def block_forward(resid_zero, dense_w, allowed, hist_local):
    qkv_full, merge_full, widen_full, narrow_full, gains_full = dense_w
    gain_float = gains_full.astype(jnp.float32)
    tokens_dev, model_width = resid_zero.shape
    normed_one, inverse_one = rms_forward(resid_zero, gain_float[0])
    input_one = normed_one.astype(jnp.bfloat16)
    qkv_parts = (
        dot_plain(input_one, qkv_full)
        .astype(jnp.bfloat16)
        .reshape(hist_local, -1, 3, HEADS, model_width // HEADS)
    )
    queries = qkv_parts[:, :, 0]
    keys_all, values_all = (
        lax.all_gather(qkv_parts[:, :, 1], "sub", axis=1, tiled=True),
        lax.all_gather(qkv_parts[:, :, 2], "sub", axis=1, tiled=True),
    )
    scores = head_scores(queries, keys_all, allowed)
    row_peak = jnp.max(scores, axis=-1, keepdims=True)
    expo_vals = jnp.exp(scores - row_peak)
    row_total = jnp.sum(expo_vals, axis=-1, keepdims=True)
    log_total = row_peak + jnp.log(row_total)
    attn_prob = (expo_vals / row_total).astype(jnp.bfloat16)
    attended = jnp.einsum(
        "bhqk,bkhe->bqhe", attn_prob, values_all, preferred_element_type=jnp.float32
    )
    attended = attended.astype(jnp.bfloat16).reshape(tokens_dev, model_width)
    resid_one = resid_zero + dot_plain(attended, merge_full)
    normed_two, inverse_two = rms_forward(resid_one, gain_float[1])
    input_two = normed_two.astype(jnp.bfloat16)
    hidden_pre = dot_plain(input_two, widen_full)
    hidden_act = jax.nn.gelu(hidden_pre).astype(jnp.bfloat16)
    resid_two = resid_one + dot_plain(hidden_act, narrow_full)
    normed_three, inverse_three = rms_forward(resid_two, gain_float[2])
    kept = (
        resid_zero,
        inverse_one,
        input_one,
        queries,
        keys_all,
        values_all,
        log_total,
        attended,
        resid_one,
        inverse_two,
        input_two,
        hidden_pre,
        hidden_act,
        resid_two,
        inverse_three,
    )
    return (normed_three.astype(jnp.bfloat16), kept)


def block_backward(user_grad, kept, dense_w, allowed):
    (
        resid_zero,
        inverse_one,
        input_one,
        queries,
        keys_all,
        values_all,
        log_total,
        attended,
        resid_one,
        inverse_two,
        input_two,
        hidden_pre,
        hidden_act,
        resid_two,
        inverse_three,
    ) = kept
    qkv_full, merge_full, widen_full, narrow_full, gains_full = dense_w
    gain_float = gains_full.astype(jnp.float32)
    tokens_dev, model_width = resid_zero.shape
    head_dim = queries.shape[-1]
    grad_two, gain_three = rms_backward(user_grad, resid_two, inverse_three, gain_float[2])
    branch_two = grad_two.astype(jnp.bfloat16)
    narrow_grad = dot_left_t(hidden_act, branch_two)
    hidden_grad = dot_right_t(branch_two, narrow_full)
    pre_grad = jax.vjp(jax.nn.gelu, hidden_pre)[1](hidden_grad)[0].astype(jnp.bfloat16)
    widen_grad = dot_left_t(input_two, pre_grad)
    from_two, gain_two = rms_backward(
        dot_right_t(pre_grad, widen_full), resid_one, inverse_two, gain_float[1]
    )
    grad_one = grad_two + from_two
    branch_one = grad_one.astype(jnp.bfloat16)
    merge_grad = dot_left_t(attended, branch_one)
    mixed_grad = dot_right_t(branch_one, merge_full).astype(jnp.bfloat16).reshape(queries.shape)
    scores = head_scores(queries, keys_all, allowed)
    attn_prob = jnp.exp(scores - log_total)
    prob_grad = jnp.einsum(
        "bqhe,bkhe->bhqk", mixed_grad, values_all, preferred_element_type=jnp.float32
    )
    score_grad = attn_prob * (prob_grad - jnp.sum(attn_prob * prob_grad, axis=-1, keepdims=True))
    score_grad = score_grad.astype(jnp.bfloat16)
    scaling = head_dim ** (-0.5)
    query_grad = (
        jnp.einsum("bhqk,bkhe->bqhe", score_grad, keys_all, preferred_element_type=jnp.float32)
        * scaling
    )
    keys_grad = (
        jnp.einsum("bhqk,bqhe->bkhe", score_grad, queries, preferred_element_type=jnp.float32)
        * scaling
    )
    values_grad = jnp.einsum(
        "bhqk,bqhe->bkhe",
        attn_prob.astype(jnp.bfloat16),
        mixed_grad,
        preferred_element_type=jnp.float32,
    )
    key_own, value_own = (
        lax.psum_scatter(
            keys_grad.astype(jnp.bfloat16), "sub", scatter_dimension=1, tiled=True
        ).astype(jnp.float32),
        lax.psum_scatter(
            values_grad.astype(jnp.bfloat16), "sub", scatter_dimension=1, tiled=True
        ).astype(jnp.float32),
    )
    qkv_grad = (
        jnp.stack([query_grad, key_own, value_own], axis=2)
        .astype(jnp.bfloat16)
        .reshape(tokens_dev, 3 * model_width)
    )
    qkv_wgrad = dot_left_t(input_one, qkv_grad)
    from_one, gain_one = rms_backward(
        dot_right_t(qkv_grad, qkv_full), resid_zero, inverse_one, gain_float[0]
    )
    gain_grads = jnp.stack([gain_one, gain_two, gain_three])
    return (grad_one + from_one, (qkv_wgrad, merge_grad, widen_grad, narrow_grad, gain_grads))


def adamw(weight, moment_one, moment_two, gradient, rate):
    moment_one = beta_one * moment_one + (1.0 - beta_one) * gradient
    moment_two = beta_two * moment_two + (1.0 - beta_two) * gradient * gradient
    fix_one = 1.0 - beta_one**STEP
    fix_two = 1.0 - beta_two**STEP
    update = (
        moment_one / fix_one / (jnp.sqrt(moment_two / fix_two) + adam_eps) + decay_rate * weight
    )
    return (weight - rate * update, moment_one, moment_two)


def body(
    item_ids,
    lengths,
    home_row,
    log_freq,
    item_table,
    table_first,
    table_second,
    pos_table,
    pos_first,
    pos_second,
    qkv_weight,
    qkv_first,
    qkv_second,
    merge_weight,
    merge_first,
    merge_second,
    widen_weight,
    widen_first,
    widen_second,
    narrow_weight,
    narrow_first,
    narrow_second,
    norm_gains,
    gains_first,
    gains_second,
):
    dp_count = lax.axis_size("dp")
    sub_count = lax.axis_size("sub")
    dp_index = lax.axis_index("dp")
    sub_index = lax.axis_index("sub")
    rows_dev, model_width = item_table.shape
    hist_local = item_ids.shape[0] // dp_count
    seq_len = item_ids.shape[1]
    slice_len = seq_len // sub_count
    tokens_dev = hist_local * slice_len
    capacity = max(2, (2 * tokens_dev + dp_count - 1) // dp_count)
    all_tokens = dp_count * sub_count * tokens_dev
    pos_full, qkv_full, merge_full, widen_full, narrow_full, gains_full = (
        lax.all_gather(pos_table.astype(jnp.bfloat16), ("dp", "sub"), axis=1, tiled=True),
        lax.all_gather(qkv_weight.astype(jnp.bfloat16), ("dp", "sub"), axis=1, tiled=True),
        lax.all_gather(merge_weight.astype(jnp.bfloat16), ("dp", "sub"), axis=1, tiled=True),
        lax.all_gather(widen_weight.astype(jnp.bfloat16), ("dp", "sub"), axis=1, tiled=True),
        lax.all_gather(narrow_weight.astype(jnp.bfloat16), ("dp", "sub"), axis=1, tiled=True),
        lax.all_gather(norm_gains.astype(jnp.bfloat16), ("dp", "sub"), axis=1, tiled=True),
    )
    dense_w = (qkv_full, merge_full, widen_full, narrow_full, gains_full)
    own_items = lax.dynamic_slice(
        item_ids, (dp_index * hist_local, sub_index * slice_len), (hist_local, slice_len)
    ).reshape(tokens_dev)
    stored_at = home_row[own_items]
    owner_dev = stored_at // rows_dev
    local_row = stored_at % rows_dev
    owner_hot = (owner_dev[:, None] == jnp.arange(dp_count, dtype=jnp.int32)[None, :]).astype(
        jnp.int32
    )
    owner_rank = jnp.sum(jnp.cumsum(owner_hot, axis=0) * owner_hot, axis=1) - 1
    slot_index = owner_dev * capacity + owner_rank
    request = (
        jnp.zeros((dp_count * capacity,), jnp.int32)
        .at[slot_index]
        .set(local_row)
        .reshape(dp_count, capacity)
    )
    arrived = lax.all_to_all(request, "dp", split_axis=0, concat_axis=0, tiled=True)
    found_rows = item_table[arrived].astype(jnp.bfloat16)
    arrived_rows = lax.all_to_all(found_rows, "dp", split_axis=0, concat_axis=0, tiled=True)
    embedded = arrived_rows.reshape(dp_count * capacity, model_width)[slot_index]
    pos_rows = lax.dynamic_slice_in_dim(pos_full, sub_index * slice_len, slice_len, 0).astype(
        jnp.float32
    )
    resid_zero = (
        embedded.astype(jnp.float32).reshape(hist_local, slice_len, model_width) + pos_rows[None]
    ).reshape(tokens_dev, model_width)
    query_pos = sub_index * slice_len + jnp.arange(slice_len)
    allowed = jnp.arange(seq_len)[None, :] <= query_pos[:, None]
    user_vecs, kept = block_forward(resid_zero, dense_w, allowed, hist_local)
    candidates = lax.all_gather(embedded, ("dp", "sub"), axis=0, tiled=True)
    layout = (dp_count, hist_local, sub_count, slice_len)

    def by_device(values):
        return values.reshape(layout).transpose(0, 2, 1, 3).reshape(all_tokens)

    all_items = by_device(item_ids)
    all_pos = by_device(
        jnp.broadcast_to(jnp.arange(seq_len, dtype=jnp.int32)[None, :], item_ids.shape)
    )
    all_len = by_device(jnp.broadcast_to(lengths[:, None], item_ids.shape))
    valid_all = (all_pos >= 1) & (all_pos < all_len)
    correction = log_freq[all_items]
    base_index = (dp_index * sub_count + sub_index) * tokens_dev
    own_index = base_index + jnp.arange(tokens_dev)
    own_pos = lax.dynamic_slice_in_dim(all_pos, base_index, tokens_dev)
    own_len = lax.dynamic_slice_in_dim(all_len, base_index, tokens_dev)
    event_count = jnp.sum(lengths - 1).astype(jnp.float32)
    valid_rows = (own_pos + 1 < own_len).astype(jnp.float32)
    row_weight = valid_rows / event_count
    targets = target_of(own_index, slice_len, tokens_dev)
    col_block = min(block_cols, all_tokens)
    starts = jnp.arange(all_tokens // col_block) * col_block

    def block_logits(block_start):
        cand_rows = lax.dynamic_slice_in_dim(candidates, block_start, col_block, 0)
        corr_rows = lax.dynamic_slice_in_dim(correction, block_start, col_block)
        valid_cols = lax.dynamic_slice_in_dim(valid_all, block_start, col_block)
        return (
            cand_rows,
            logits_for(user_vecs, cand_rows, corr_rows, valid_cols),
            block_start + jnp.arange(col_block),
        )

    def forward_block(running, block_start):
        row_peak, row_total, target_logit = running
        cand_rows, logits, columns = block_logits(block_start)
        new_peak = jnp.maximum(row_peak, jnp.max(logits, axis=1))
        row_total = row_total * jnp.exp(row_peak - new_peak) + jnp.sum(
            jnp.exp(logits - new_peak[:, None]), axis=1
        )
        target_logit = target_logit + jnp.sum(
            jnp.where(columns[None, :] == targets[:, None], logits, 0.0), axis=1
        )
        return ((new_peak, row_total, target_logit), None)

    start_state = (
        jnp.full((tokens_dev,), big_negative, jnp.float32),
        jnp.zeros((tokens_dev,), jnp.float32),
        jnp.zeros((tokens_dev,), jnp.float32),
    )
    (row_peak, row_total, target_logit), _ = lax.scan(forward_block, start_state, starts)
    log_total = row_peak + jnp.log(row_total)
    loss_local = jnp.sum(valid_rows * (log_total - target_logit))

    def user_block(running, block_start):
        cand_rows, logits, columns = block_logits(block_start)
        coeffs = coefficient(logits, log_total, row_weight, columns, targets)
        return (running + dot_plain(coeffs, cand_rows), None)

    user_grad, _ = lax.scan(user_block, jnp.zeros((tokens_dev, model_width), jnp.float32), starts)
    step_rows = math.gcd(tokens_dev * lax.axis_size(("dp", "sub")), max(block_cols, tokens_dev))

    def one_block(offset):
        cand_rows = lax.dynamic_slice_in_dim(candidates, offset, step_rows, 0)
        corr_rows = lax.dynamic_slice_in_dim(correction, offset, step_rows)
        valid_cols = lax.dynamic_slice_in_dim(valid_all, offset, step_rows)
        logits = logits_for(user_vecs, cand_rows, corr_rows, valid_cols)
        coeffs = coefficient(logits, log_total, row_weight, offset + jnp.arange(step_rows), targets)
        return dot_left_t(coeffs, user_vecs)

    pieces = lax.map(
        one_block, jnp.arange(tokens_dev * lax.axis_size(("dp", "sub")) // step_rows) * step_rows
    )
    cand_grad = lax.psum_scatter(
        pieces.reshape(tokens_dev * lax.axis_size(("dp", "sub")), model_width),
        ("dp", "sub"),
        scatter_dimension=0,
        tiled=True,
    )
    resid_grad, weight_grads = block_backward(user_grad, kept, dense_w, allowed)
    qkv_wgrad, merge_grad, widen_grad, narrow_grad, gain_grads = weight_grads
    emb_grad = resid_grad + cand_grad
    pos_rows_grad = jnp.sum(resid_grad.reshape(hist_local, slice_len, model_width), axis=0)
    pos_grad = lax.dynamic_update_slice_in_dim(
        jnp.zeros((seq_len, model_width), jnp.float32), pos_rows_grad, sub_index * slice_len, 0
    )
    outgoing = (
        jnp.zeros((dp_count * capacity, model_width), jnp.float32).at[slot_index].set(emb_grad)
    )
    incoming = lax.all_to_all(
        outgoing.reshape(dp_count, capacity, model_width),
        "dp",
        split_axis=0,
        concat_axis=0,
        tiled=True,
    )
    incoming_rows = incoming.reshape(-1, model_width)
    arrived_flat = arrived.reshape(-1)
    plane_grad = jnp.zeros((rows_dev, model_width), jnp.float32).at[arrived_flat].add(incoming_rows)
    table_grad = lax.psum(plane_grad, "sub")
    shard_grads = (
        lax.psum_scatter(pos_grad, ("dp", "sub"), scatter_dimension=1, tiled=True),
        lax.psum_scatter(qkv_wgrad, ("dp", "sub"), scatter_dimension=1, tiled=True),
        lax.psum_scatter(merge_grad, ("dp", "sub"), scatter_dimension=1, tiled=True),
        lax.psum_scatter(widen_grad, ("dp", "sub"), scatter_dimension=1, tiled=True),
        lax.psum_scatter(narrow_grad, ("dp", "sub"), scatter_dimension=1, tiled=True),
        lax.psum_scatter(gain_grads, ("dp", "sub"), scatter_dimension=1, tiled=True),
    )
    square_part = sum((jnp.sum(gradient * gradient) for gradient in shard_grads))
    square_part = square_part + jnp.where(sub_index == 0, jnp.sum(table_grad * table_grad), 0.0)
    loss_sum, square_sum = lax.psum((loss_local, square_part), ("dp", "sub"))
    grad_norm = jnp.sqrt(square_sum)
    factor = jnp.minimum(1.0, clip_limit / grad_norm)
    masters = (
        item_table,
        pos_table,
        qkv_weight,
        merge_weight,
        widen_weight,
        narrow_weight,
        norm_gains,
    )
    firsts = (
        table_first,
        pos_first,
        qkv_first,
        merge_first,
        widen_first,
        narrow_first,
        gains_first,
    )
    seconds = (
        table_second,
        pos_second,
        qkv_second,
        merge_second,
        widen_second,
        narrow_second,
        gains_second,
    )
    rates = (learn_rate,) * 6 + (gain_rate,)
    all_grads = (table_grad,) + tuple(shard_grads)
    results = [loss_sum, event_count, grad_norm]
    for weight, moment_one, moment_two, gradient, rate in zip(
        masters, firsts, seconds, all_grads, rates
    ):
        results.extend(adamw(weight, moment_one, moment_two, gradient * factor, rate))
    return tuple(results)


MESH_ID = pl.DeviceIdType.MESH
FF_CHUNK = 256


def dot_nn(left, right):
    return lax.dot_general(
        left, right, (((1,), (0,)), ((), ())), preferred_element_type=jnp.float32
    )


def dot_nt(left, right):
    return lax.dot_general(
        left, right, (((1,), (1,)), ((), ())), preferred_element_type=jnp.float32
    )


def dot_tn(left, right):
    return lax.dot_general(
        left, right, (((0,), (0,)), ((), ())), preferred_element_type=jnp.float32
    )


def low(values):
    return values.astype(jnp.bfloat16)


def wide(values):
    return values.astype(jnp.float32)


def iota_of(shape, axis):
    return lax.broadcasted_iota(jnp.int32, shape, axis)


def flip(index, bits):
    total = 0
    for power in (1, 2, 4, 8):
        a = lax.rem(lax.div(index, power), 2)
        b = (bits // power) % 2 if isinstance(bits, int) else lax.rem(lax.div(bits, power), 2)
        total = total + power * (a + b - 2 * a * b)
    return total


def arrival_order(levels):
    if levels == 4:
        return [(0, 0), (0, 1), (0, 2), (1, 0), (2, 0), (0, 3), (1, 1), (1, 2), (3, 0), (2, 1), (2, 2), (1, 3), (3, 1), (3, 2), (2, 3), (3, 3)]
    return [(level, corner) for level in range(levels) for corner in range(4)]


class Place:
    def __init__(self, chips):
        self.chips = chips
        self.chip = lax.axis_index("dp")
        self.core = lax.axis_index("sub")
        self.level = lax.div(self.chip, 4)
        self.corner = lax.rem(self.chip, 4)
        self.inner = (self.level == 1) | (self.level == 2)
        self.near_x = self.level * 4 + flip(self.corner, 1)
        self.near_y = self.level * 4 + flip(self.corner, 2)

    def step(self, way):
        return arrival_order(self.chips // 4).index(way)

    def way(self, step):
        order = arrival_order(self.chips // 4)
        if isinstance(step, int):
            return order[step]
        return tuple(
            sum(jnp.where(step == i, place[axis], 0) for i, place in enumerate(order) if place[axis])
            for axis in range(2)
        )

    def relative(self, step):
        level, corner = self.way(step)
        return flip(self.level, level) * 4 + flip(self.corner, corner)


def remote(src, dst, send, recv, chip, core):
    return pltpu.make_async_remote_copy(
        src_ref=src,
        dst_ref=dst,
        send_sem=send,
        recv_sem=recv,
        device_id=(chip, core),
        device_id_type=MESH_ID,
    )


class Gather:
    def __init__(self, place, buf, send, recv):
        self.place, self.buf, self.send, self.recv = place, buf, send, recv
        self.levels = place.chips // 4
        order = [(0, 1), (1, 0), (2, 0), (1, 2), (3, 0), (2, 1)]
        self.queue = [place.step(at) for at in order]
        self.waiting = set(range(1, place.chips))

    def copy(self, block, sem, chip):
        return remote(
            self.buf.at[block], self.buf.at[block], self.send.at[sem], self.recv.at[block], chip, self.place.core
        )

    def send_on(self, step, action):
        place = self.place
        block = place.relative(step)
        level, corner = place.way(step)
        last = level == self.levels - 1
        if corner == 0 or (corner == 2 and level % 2 == 1 and not last):
            action(self.copy(block, step * 2, place.near_x))
        if corner == 0 or (corner == 1 and level % 2 == 0 and not last):
            action(self.copy(block, step * 2 + 1, place.near_y))
        if corner == 0 and last:
            action(self.copy(block, place.chips * 2, place.level * 4 + 3 - place.corner))
        if corner == 0 and level == 2:
            @pl.when(place.inner)
            def _():
                action(self.copy(block, place.chips * 2 + 4, flip(place.level, 1) * 4 + place.corner))

    def along_z(self, action):
        place = self.place
        for step in (1, 3, 2):
            chip = flip(place.level, step) * 4 + place.corner
            copy = self.copy(place.chip, place.chips * 2 + step, chip)
            if step == 3:
                pl.when(place.inner)(lambda copy=copy: action(copy))
            else:
                action(copy)

    def start(self):
        self.along_z(lambda copy: copy.start())
        self.send_on(0, lambda copy: copy.start())

    def need(self, steps):
        for step in steps:
            if step in self.waiting:
                self.waiting.remove(step)
                self.copy(self.place.relative(step), 0, self.place.chip).wait_recv()
            if step in self.queue:
                self.queue.remove(step)
                self.send_on(step, lambda copy: copy.start())

    def advance(self, count):
        self.need(self.queue[:count])

    def complete(self):
        self.advance(len(self.queue))
        self.need(sorted(self.waiting))

    def sent(self):
        self.along_z(lambda copy: copy.wait_send())
        for step in range(self.place.chips):
            self.send_on(step, lambda copy: copy.wait_send())

    @staticmethod
    def sends(chips):
        return chips * 2 + 8


class ShortGather(Gather):
    def __init__(self, place, buf, send, recv):
        super().__init__(place, buf, send, recv)
        self.queue = [place.step((level, 0)) for level in range(1, self.levels)]

    def send_on(self, step, action):
        place = self.place
        block = place.relative(step)
        if place.way(step)[1] == 0:
            action(self.copy(block, step * 2, place.near_x))
            action(self.copy(block, step * 2 + 1, place.near_y))
            action(self.copy(block, place.chips * 2 + 4 + place.way(step)[0], place.level * 4 + 3 - place.corner))

    def along_z(self, action):
        place = self.place
        for step in (1, 3, 2):
            chip = flip(place.level, step) * 4 + place.corner
            action(self.copy(place.chip, place.chips * 2 + step, chip))


def to_sibling(place, src, dst, sems):
    return remote(src, dst, sems.at[0], sems.at[1], place.chip, 1 - place.core)


class Scatter:
    def __init__(self, place, src, dst, send, recv):
        self.place, self.src, self.dst, self.send, self.recv = place, src, dst, send, recv

    def copy(self, to, at):
        place = self.place
        return remote(
            self.src.at[to] if self.src is not None else self.dst.at[place.chip],
            self.dst.at[at],
            self.send.at[to],
            self.recv.at[at],
            to,
            place.core,
        )

    def each(self, action):
        place = self.place

        def step(index, carry):
            action(lax.rem(place.chip + index, place.chips))
            return carry

        lax.fori_loop(1, place.chips, step, 0)

    def start(self):
        self.each(lambda chip: self.copy(chip, self.place.chip).start())

    def arrived(self):
        self.each(lambda chip: self.copy(chip, chip).wait_recv())

    def sent(self):
        self.each(lambda chip: self.copy(chip, self.place.chip).wait_send())


class Reduce:
    def __init__(self, place, pack, pair, summed, plane, part, line, sems):
        self.place, self.pack, self.pair, self.summed = place, pack, pair, summed
        self.plane, self.part, self.line, self.sems = plane, part, line, sems
        self.levels = place.chips // 4

    def pair_copy(self):
        place = self.place
        return remote(
            self.pack.at[1 - place.core], self.pair, self.sems.at[0], self.sems.at[1], place.chip, 1 - place.core
        )

    def plane_copy(self, way, coming=False):
        place = self.place
        corner = flip(place.corner, way)
        return remote(
            self.summed.at[corner], self.plane.at[corner if coming else place.corner],
            self.sems.at[2 + way], self.sems.at[6 + way], place.level * 4 + corner, place.core,
        )

    def line_copy(self, way, coming=False):
        place = self.place
        level = flip(place.level, way)
        return remote(
            self.part.at[level], self.line.at[level if coming else place.level],
            self.sems.at[10 + way], self.sems.at[10 + self.levels + way], level * 4 + place.corner, place.core,
        )

    def to_pair(self):
        self.pair_copy().start()

    def to_plane(self):
        self.pair_copy().wait_recv()
        place = self.place
        for way in (3, 1, 2, 0):
            corner = flip(place.corner, way)
            for level in range(self.levels):
                self.summed[corner, level] = low(
                    wide(self.pack[place.core, corner, level]) + wide(self.pair[corner, level])
                )
            if way:
                self.plane_copy(way).start()

    def to_line(self):
        place = self.place
        corners = [flip(place.corner, way) for way in (1, 2, 3)]
        for way in (1, 2, 3):
            self.plane_copy(way, True).wait_recv()
        for way in [*range(1, self.levels), 0]:
            level = flip(place.level, way)
            total = wide(self.summed[place.corner, level])
            for corner in corners:
                total = total + wide(self.plane[corner, level])
            self.part[level] = low(total)
            if way:
                self.line_copy(way).start()

    def total(self):
        place = self.place
        total = wide(self.part[place.level])
        for way in range(1, self.levels):
            self.line_copy(way, True).wait_recv()
            total = total + wide(self.line[flip(place.level, way)])
        return total

    def sent(self):
        self.pair_copy().wait_send()
        for way in (1, 2, 3):
            self.plane_copy(way).wait_send()
        for way in range(1, self.levels):
            self.line_copy(way).wait_send()


def rms_apply(values, gain_row):
    inverse = lax.rsqrt(jnp.mean(values * values, axis=-1, keepdims=True) + norm_eps)
    return values * inverse * gain_row, inverse


def rms_back(upstream, values, inverse, gain_row):
    unit = values * inverse
    gain_grad = jnp.sum(upstream * unit, axis=0, keepdims=True)
    scaled = upstream * gain_row
    inner = jnp.mean(scaled * unit, axis=-1, keepdims=True)
    return inverse * (scaled - unit * inner), gain_grad


GELU_A = math.sqrt(2.0 / math.pi)
GELU_B = 0.044715


def gelu_both(x):
    square = x * x
    curve = jnp.tanh(GELU_A * x * (1.0 + GELU_B * square))
    half = 0.5 * (1.0 + curve)
    slope = half + 0.5 * x * (1.0 - curve * curve) * (GELU_A * (1.0 + 3.0 * GELU_B * square))
    return x * half, slope


def pieces_of(values):
    first = wide(low(values))
    second = wide(low(values - first))
    return first, second, values - first - second


def step_kernel(sizes, *refs):
    (chips, rows_dev, seq_len, width, hidden, capacity, half_slots, key_rows) = sizes
    refs = list(refs)
    names = list(dict(ENDS)) + list(scratch_of(sizes))
    r = types.SimpleNamespace(**dict(zip(names, refs, strict=True)))
    place = Place(chips)
    chip, core = place.chip, place.core
    me = chip * 2 + core
    tokens = half_slots
    wa, wb, cand_buf, user_buf = r.wa, r.wb, r.cand, r.user
    gather_a = ShortGather(place, wa.at[core], r.wa_send, r.wa_recv)
    gather_b = ShortGather(place, wb.at[core], r.wb_send, r.wb_recv)
    gather_c = Gather(place, cand_buf, r.cand_send, r.cand_recv)
    gather_u = Gather(place, user_buf, r.user_send, r.user_recv)
    spread_corr = Scatter(place, None, r.corr, r.corr_send, r.corr_recv)
    spread_norm = Scatter(place, None, r.norm, r.norm_send, r.norm_recv)
    pair_a = to_sibling(place, wa.at[core], wa.at[core], r.wa_pair)
    pair_b = to_sibling(place, wb.at[core], wb.at[core], r.wb_pair)
    pair_emb = to_sibling(place, r.emb_pair.at[core], r.emb_pair.at[core], r.emb_sems)
    pair_corr = to_sibling(place, r.corr_pair.at[core], r.corr_pair.at[core], r.corr_sems)
    pair_user = to_sibling(place, r.user_pair.at[core], r.user_pair.at[core], r.user_sems)
    pair_soft = to_sibling(place, r.soft_out, r.soft_in, r.soft_sems)
    pair_cand = to_sibling(place, r.cand_out, r.cand_in, r.cand_sems)
    spread_sums = Scatter(place, None, r.scalar_buf, r.scalar_send, r.scalar_recv)
    pair_sums = to_sibling(place, r.scalar_pair.at[core], r.scalar_pair.at[core], r.sums_sems)

    barrier = pltpu.get_barrier_semaphore()
    table_copy = pltpu.make_async_copy(r.table, r.table_here, r.table_sem)
    table_copy.start()

    def greet(index, carry):
        other = lax.rem(chip + index, chips)
        pl.semaphore_signal(barrier, inc=1, device_id=(other, core), device_id_type=MESH_ID)
        return carry

    lax.fori_loop(1, chips, greet, 0)
    pl.semaphore_signal(barrier, inc=1, device_id=(chip, 1 - core), device_id_type=MESH_ID)

    turn = r.turn
    turn[...] = jnp.zeros_like(turn)
    turn[0:3, 0:8] = r.gains[...]
    gains_t = jnp.concatenate([jnp.transpose(turn[...])[0:8, :], jnp.zeros((8, width - 128), jnp.float32)], axis=1)
    pos_t = r.pos[...]
    wa[core, chip] = low(
        jnp.concatenate([r.qkv[...], gains_t, pos_t[:, :width], pos_t[:, width:]], axis=0)
    )
    narrow_t = r.narrow[...]
    wb[core, chip] = low(
        jnp.concatenate(
            [r.merge[...], r.widen[...]]
            + [narrow_t[:, i * width : (i + 1) * width] for i in range(hidden // width)]
            + [jnp.zeros((8, width), jnp.float32)],
            axis=0,
        )
    )

    low_table = r.low_table
    pad_rows = low_table.shape[0] - rows_dev
    low_table[pl.ds(rows_dev, pad_rows), :] = jnp.zeros((pad_rows, width), jnp.bfloat16)
    keys = r.keys
    keys[...] = jnp.zeros_like(keys)
    home = r.home[...]
    used = home.shape[0]
    keys[pl.ds(0, used), pl.ds(0, 128)] = wide(lax.div(home, 256))
    keys[pl.ds(0, used), pl.ds(128, 128)] = wide(lax.rem(home, 256))
    home_look = low(jnp.transpose(keys[:, 0:256]))
    ids_all = r.ids[:, pl.ds(pl.multiple_of(core * tokens, tokens), tokens)]
    lane_of = iota_of((128, tokens), 0)
    key_of = iota_of((key_rows, tokens), 0)

    def look(table_t, ids_row, parts):
        hot = low(wide(key_of == lax.div(ids_row, 128)))
        picked = dot_nn(table_t, hot)
        mask = lane_of == lax.rem(ids_row, 128)
        return [
            jnp.sum(jnp.where(mask, picked[128 * i : 128 * i + 128], 0.0), axis=0, keepdims=True)
            for i in range(parts)
        ]

    home_rows = []
    for d in range(chips):
        top, bottom = look(home_look, ids_all[d : d + 1, :], 2)
        home_rows.append(top * 256.0 + bottom)
    home_all = jnp.concatenate(home_rows, axis=0)
    r.home_all[...] = home_all

    pl.semaphore_wait(barrier, chips)
    gather_a.start()

    upper = low(wide(iota_of((tokens, tokens), 0) <= iota_of((tokens, tokens), 1)))
    first_row = wide(chip * rows_dev)
    local_all = home_all - first_row
    owned = (local_all >= 0.0) & (local_all < float(rows_dev))
    rank = dot_nn(low(wide(owned)), upper) - 1.0
    slot_rank = wide(iota_of((capacity, tokens), 0))
    wanted = []
    for d in range(chips):
        chosen = (rank[d : d + 1, :] == slot_rank) & owned[d : d + 1, :]
        wanted.append(
            jnp.sum(jnp.where(chosen, local_all[d : d + 1, :] + 1.0, 0.0), axis=1, keepdims=True) - 1.0
        )
    wanted = jnp.concatenate(wanted, axis=0)
    asked = chips * capacity
    lanes = low_table.shape[0]
    table_copy.wait()
    low_table[pl.ds(0, rows_dev), :] = low(r.table_here[...])
    hot_rows = low(wide(iota_of((asked, lanes), 1) == wanted.astype(jnp.int32)))
    out_rows = low(dot_nn(hot_rows, low_table[...])).reshape(chips, capacity, width)
    r.row_out[...] = out_rows
    r.row_in[chip] = r.row_out[chip]
    rows_there = Scatter(place, r.row_out, r.row_in, r.row_send, r.row_recv)
    rows_there.start()
    wanted_row = jnp.transpose(jnp.broadcast_to(wanted, (asked, 128)))[0:1, :]
    r.asked[core] = wanted_row
    asked_copy = remote(
        r.asked.at[core], r.asked.at[core], r.asked_send, r.asked_recv, chip, 1 - core
    )
    asked_copy.start()

    own_home = r.home_all[pl.ds(chip, 1), :]
    owner_first = wide(iota_of((chips, tokens), 0) * rows_dev)
    at_owner = (own_home >= owner_first) & (own_home < owner_first + float(rows_dev))
    own_rank = dot_nn(low(wide(at_owner)), upper) - 1.0
    spread = jnp.concatenate(
        [
            wide((own_rank[o : o + 1, :] == slot_rank) & at_owner[o : o + 1, :])
            for o in range(chips)
        ],
        axis=0,
    )
    r.spread[...] = low(spread)

    freq = r.freq[...]
    for i, piece in enumerate(pieces_of(freq)):
        keys[pl.ds(0, used), pl.ds(128 * i, 128)] = piece
    freq_look = low(jnp.transpose(keys[...]))
    own_ids = r.ids[pl.ds(chip, 1), pl.ds(pl.multiple_of(core * tokens, tokens), tokens)]
    fa, fb, fc = look(freq_look, own_ids, 3)
    own_length = r.lengths[chip]
    row_pos = core * tokens + iota_of((1, tokens), 1)
    is_cand = (row_pos >= 1) & (row_pos < own_length)
    own_corr = jnp.where(is_cand, fa + fb + fc, -big_negative)
    r.corr[chip] = own_corr
    r.corr_pair[core] = own_corr
    spread_corr.start()
    pair_corr.start()

    def turned(row):
        return jnp.transpose(jnp.broadcast_to(row, (128, tokens)))[:, 0:1]

    corr_col = turned(own_corr)
    r.corr_col[...] = jnp.broadcast_to(corr_col, (tokens, 128))

    total_events = jnp.float32(0.0)
    for d in range(chips):
        total_events = total_events + wide(r.lengths[d] - 1)
    col_pos = core * tokens + iota_of((tokens, 1), 0)
    is_event = col_pos + 1 < own_length

    gather_a.advance(3)
    gather_b.start()
    rows_there.arrived()
    embedded = low(dot_tn(r.spread[...], r.row_in[...].reshape(asked, width)))
    cand_buf[chip] = embedded
    r.emb_pair[core] = embedded
    gather_c.start()
    pair_emb.start()
    gather_a.complete()
    pair_a.start()
    gather_b.advance(3)
    pair_a.wait_recv()
    qkv_w, pos_w, gain_w = r.qkv_w, r.pos_w, r.gain_w

    def unpack_a(index, carry):
        one, two = wide(wa[0, index]), wide(wa[1, index])
        qkv_w[pl.ds(pl.multiple_of(index * 48, 16), 48), :] = low(jnp.concatenate([one[0:24], two[0:24]], axis=0))
        gain_w[pl.ds(pl.multiple_of(index * 16, 16), 16), :] = jnp.concatenate([one[24:32], two[24:32]], axis=0)[:, 0:128]
        early = jnp.concatenate([one[32:40], two[32:40]], axis=0)
        late = jnp.concatenate([one[40:48], two[40:48]], axis=0)
        pos_w[pl.ds(pl.multiple_of(index * 16, 16), 16), :] = jnp.where(core == 0, early, late)
        return carry

    lax.fori_loop(0, chips, unpack_a, 0)
    gain_rows = jnp.transpose(gain_w[...])[0:8, :]
    r.gain_rows[...] = gain_rows
    gain_one, gain_two, gain_three = (r.gain_rows[i : i + 1, :] for i in range(3))

    resid_zero = wide(cand_buf[chip]) + jnp.transpose(pos_w[...])
    r.resid_zero[...] = resid_zero
    normed, _ = rms_apply(resid_zero, gain_one)
    r.input_one[...] = low(normed)
    qkv_own = low(dot_nt(r.input_one[...], qkv_w[...]))
    kv = r.kv
    kv[0] = qkv_own[:, width : 3 * width]
    kv_copy = remote(kv.at[0], kv.at[1], r.kv_send, r.kv_recv, chip, 1 - core)
    kv_copy.start()

    kv_copy.wait_recv()

    head_dim = width // HEADS
    scaling = head_dim ** (-0.5)
    causal = iota_of((tokens, tokens), 1) <= iota_of((tokens, tokens), 0)
    other_bias = jnp.where(core == 0, big_negative, 0.0)
    head_lane = lax.div(iota_of((1, width), 1), head_dim)
    prob = r.prob
    zero_low = jnp.zeros((), jnp.bfloat16)
    both = 2 * tokens

    def of_head(values, head):
        return jnp.where(head_lane == head, values, zero_low)

    def rows_of(head, size=tokens):
        return slice(head * size, (head + 1) * size)

    def stack(to, values):
        for head in range(HEADS):
            to[rows_of(head), :] = of_head(values, head)

    def stack_pair(to, pair, lanes):
        for head in range(HEADS):
            to[rows_of(2 * head), :] = of_head(pair[0, :, lanes], head)
            to[rows_of(2 * head + 1), :] = of_head(pair[1, :, lanes], head)

    stack(r.query_rows, qkv_own[:, 0:width])
    stack_pair(r.value_rows, kv, slice(width, 2 * width))

    def attend(head):
        query = r.query_rows[rows_of(head), :]
        own = dot_nt(query, kv[0, :, 0:width]) * scaling
        own = jnp.where(causal, own, big_negative)
        other = dot_nt(query, kv[1, :, 0:width]) * scaling + other_bias
        peak = jnp.max(jnp.maximum(own, other), axis=-1, keepdims=True)
        own = jnp.exp(own - peak)
        other = jnp.exp(other - peak)
        share = 1.0 / jnp.sum(own + other, axis=-1, keepdims=True)
        own = own * share
        other = other * share
        prob[head, :, 0:tokens] = own
        prob[head, :, tokens:both] = other
        own, other = low(own), low(other)
        r.prob_own[rows_of(head), :] = own
        r.prob_other[rows_of(head), :] = other
        r.prob_lanes[:, rows_of(2 * head)] = own
        r.prob_lanes[:, rows_of(2 * head + 1)] = other

    gather_c.advance(1)
    for head in range(HEADS):
        attend(head)
    gather_b.complete()
    pair_b.start()
    gather_c.advance(2)
    pair_b.wait_recv()
    merge_w, widen_w, narrow_w = r.merge_w, r.widen_w, r.narrow_w

    def unpack_b(index, carry):
        one, two = wide(wb[0, index]), wide(wb[1, index])
        at16 = pl.ds(pl.multiple_of(index * 16, 16), 16)
        merge_w[at16, :] = low(jnp.concatenate([one[0:8], two[0:8]], axis=0))
        widen_w[pl.ds(pl.multiple_of(index * 64, 16), 64), :] = low(jnp.concatenate([one[8:40], two[8:40]], axis=0))
        for i in range(hidden // width):
            top = 40 + 8 * i
            narrow_w[at16, pl.ds(i * width, width)] = low(
                jnp.concatenate([one[top : top + 8], two[top : top + 8]], axis=0)
            )
        return carry

    lax.fori_loop(0, chips, unpack_b, 0)
    r.attended[...] = low(dot_nn(r.prob_lanes[...], r.value_rows[...]))
    resid_one = r.resid_zero[...] + dot_nt(r.attended[...], merge_w[...])
    r.resid_one[...] = resid_one
    normed, _ = rms_apply(resid_one, gain_two)
    r.input_two[...] = low(normed)
    r.resid_two[...] = resid_one
    for i in range(hidden // FF_CHUNK):
        part = slice(i * FF_CHUNK, (i + 1) * FF_CHUNK)
        act, slope = gelu_both(dot_nt(r.input_two[...], widen_w[part, :]))
        r.act[:, part] = low(act)
        r.slope[:, part] = slope
    r.resid_two[...] += dot_nt(r.act[...], narrow_w[...])
    normed, _ = rms_apply(r.resid_two[...], gain_three)
    user_buf[chip] = low(normed)
    r.user_pair[core] = user_buf[chip]
    gather_u.start()
    pair_user.start()

    gather_c.advance(2)
    spread_corr.arrived()
    pair_emb.wait_recv()
    pair_corr.wait_recv()
    shifted = jnp.concatenate([wide(cand_buf[chip])[1:, :], wide(r.emb_pair[1, pl.ds(0, 16), :])[0:1, :]], axis=0)
    target_corr = jnp.concatenate([corr_col[1:, :], r.corr_pair[1][:, 0:1]], axis=0)
    target_logit = jnp.sum(wide(user_buf[chip]) * shifted, axis=-1, keepdims=True) - target_corr
    target_logit = jnp.where(is_event, target_logit, 0.0)
    pair_user.wait_recv()
    users = r.user_pair[...].reshape(2 * tokens, width)
    logit_buf, peaks, totals, acc = r.logit, r.peaks, r.totals, r.acc
    totals[...] = jnp.zeros_like(totals)
    acc[...] = jnp.zeros_like(acc)
    group = chips // CHUNKS
    pair_row = iota_of((both, tokens), 0)
    pair_col = core * tokens + iota_of((both, tokens), 1)

    def fold(values, how):
        parts = [values[:, i : i + 128] for i in range(0, values.shape[1], 128)]
        return functools.reduce(how, parts)

    peak = jnp.full((both, 1), big_negative, jnp.float32)
    for chunk in range(CHUNKS):
        gather_c.advance(1)
        gather_c.need(range(group * chunk, group * (chunk + 1)))
        peaks[...] = jnp.broadcast_to(peak, peaks.shape)

        steps = range(chunk * group, (chunk + 1) * group)
        for index, step in enumerate(steps):
            there = place.relative(step)
            logits = dot_nt(users, cand_buf[there]) - r.corr[there]
            logit_buf[index] = logits
            peaks[...] = jnp.maximum(peaks[...], fold(logits, jnp.maximum))
        before, peak = peak, jnp.max(peaks[...], axis=-1, keepdims=True)
        scale = jnp.exp(before - peak)
        totals[...] *= scale
        acc[...] *= scale
        gather_u.advance((1, 2, 2, 1)[chunk])

        for index, step in enumerate(steps):
            expo = jnp.exp(logit_buf[index] - peak)
            totals[...] += fold(expo, jnp.add)
            if step == 0:
                expo = jnp.where(pair_col == pair_row + 1, 0.0, expo)
            acc[...] += dot_nn(low(expo), cand_buf[place.relative(step)])
    total = jnp.sum(totals[...], axis=-1, keepdims=True)
    peaks[...] = jnp.broadcast_to(peak, peaks.shape)
    totals[...] = jnp.broadcast_to(total, totals.shape)
    own_rows = pl.ds(pl.multiple_of(core * tokens, tokens), tokens)
    other_rows = pl.ds(pl.multiple_of((1 - core) * tokens, tokens), tokens)
    soft_out, soft_in = r.soft_out, r.soft_in
    soft_out[:, 0:width] = acc[other_rows, :]
    soft_out[:, width : width + 128] = peaks[other_rows, :]
    soft_out[:, width + 128 : width + 256] = totals[other_rows, :]
    pair_soft.start()
    pair_soft.wait_recv()
    own_peak, own_total = peaks[own_rows, :][:, 0:1], totals[own_rows, :][:, 0:1]
    other_peak = soft_in[:, width : width + 1]
    peak = jnp.maximum(own_peak, other_peak)
    own_scale, other_scale = jnp.exp(own_peak - peak), jnp.exp(other_peak - peak)
    total = own_total * own_scale + soft_in[:, width + 128 : width + 129] * other_scale
    soft = acc[own_rows, :] * own_scale + soft_in[:, 0:width] * other_scale
    log_total = peak + jnp.log(total)
    loss_own = jnp.sum(jnp.where(is_event, log_total - target_logit, 0.0), axis=0, keepdims=True)
    weight = jnp.where(is_event, 1.0 / total_events, 0.0)
    target_coef = wide(low(weight * (jnp.exp(target_logit - log_total) - 1.0)))
    user_grad = soft * (weight / total) + target_coef * shifted
    shift_col = jnp.where(is_event, log_total + jnp.log(total_events), -big_negative)
    norm_buf = r.norm
    norm_buf[chip] = jnp.transpose(jnp.broadcast_to(shift_col, (tokens, 128)))[0:1, :]
    spread_norm.start()
    grad_two, gain_grad_three = rms_back(
        user_grad, r.resid_two[...],
        lax.rsqrt(jnp.mean(r.resid_two[...] * r.resid_two[...], axis=-1, keepdims=True) + norm_eps),
        gain_three,
    )
    branch_two = low(grad_two)
    narrow_grad = dot_tn(branch_two, r.act[...])
    r.pre[...] = low(dot_nn(branch_two, narrow_w[...]) * r.slope[...])
    widen_grad = dot_tn(r.pre[...], r.input_two[...])
    resid_one = r.resid_one[...]
    inverse_two = lax.rsqrt(jnp.mean(resid_one * resid_one, axis=-1, keepdims=True) + norm_eps)
    from_two, gain_grad_two = rms_back(dot_nn(r.pre[...], widen_w[...]), resid_one, inverse_two, gain_two)
    grad_one = grad_two + from_two
    r.grad_one[...] = grad_one
    branch_one = low(grad_one)
    merge_grad = dot_tn(branch_one, r.attended[...])
    r.mixed[...] = low(dot_nn(branch_one, merge_w[...]))

    tail, head_pack = r.tail_pack, r.head_pack
    for d in range(2 * chips):
        at = (d % 2, d // 2 % 4, d // 8)
        tail[*at, pl.ds(0, 32), :] = low(widen_grad[32 * d : 32 * d + 32])
        tail[*at, pl.ds(32, 32), :] = low(
            jnp.concatenate(
                [
                    narrow_grad[8 * d : 8 * d + 8, i * width : (i + 1) * width]
                    for i in range(hidden // width)
                ],
                axis=0,
            )
        )
    reduce_tail = Reduce(place, tail, r.tail_pair, r.tail_sum, r.tail_plane, r.tail_part, r.tail_line, r.tail_sems)
    reduce_head = Reduce(place, head_pack, r.head_pair, r.head_sum, r.head_plane, r.head_part, r.head_line, r.head_sems)
    reduce_tail.to_pair()
    gather_u.advance(1)
    stack(r.mixed_rows, r.mixed[...])
    stack_pair(r.key_rows, kv, slice(0, width))

    def attend_back(head):
        mixed = r.mixed_rows[rows_of(head), :]
        own, other = prob[head, :, 0:tokens], prob[head, :, tokens:both]
        own_grad = dot_nt(mixed, kv[0, :, width : 2 * width])
        other_grad = dot_nt(mixed, kv[1, :, width : 2 * width])
        inner = jnp.sum(own * own_grad + other * other_grad, axis=-1, keepdims=True)
        own_score = low(own * (own_grad - inner))
        other_score = low(other * (other_grad - inner))
        r.score_own[rows_of(head), :] = own_score
        r.score_other[rows_of(head), :] = other_score
        r.score_lanes[:, rows_of(2 * head)] = own_score
        r.score_lanes[:, rows_of(2 * head + 1)] = other_score

    for head in range(HEADS):
        attend_back(head)
        if head == 1:
            gather_u.advance(1)
        if head == 3:
            reduce_tail.to_plane()
            gather_u.advance(1)
        if head == 5:
            gather_u.advance(1)
    back = r.back
    back[0, :, 0:width] = low(dot_tn(r.score_other[...], r.query_rows[...]) * scaling)
    back[0, :, width : 2 * width] = low(dot_tn(r.prob_other[...], r.mixed_rows[...]))
    back_copy = remote(back.at[0], back.at[1], r.back_send, r.back_recv, chip, 1 - core)
    back_copy.start()
    qkv_grad = r.qkv_grad
    qkv_grad[:, 0:width] = low(dot_nn(r.score_lanes[...], r.key_rows[...]) * scaling)
    key_own = dot_tn(r.score_own[...], r.query_rows[...]) * scaling
    value_own = dot_tn(r.prob_own[...], r.mixed_rows[...])
    back_copy.wait_recv()
    qkv_grad[:, width : 2 * width] = low(key_own + wide(back[1, :, 0:width]))
    qkv_grad[:, 2 * width : 3 * width] = low(value_own + wide(back[1, :, width : 2 * width]))
    qkv_wgrad = dot_tn(qkv_grad[...], r.input_one[...])
    resid_zero = r.resid_zero[...]
    inverse_one = lax.rsqrt(jnp.mean(resid_zero * resid_zero, axis=-1, keepdims=True) + norm_eps)
    from_one, gain_grad_one = rms_back(dot_nn(qkv_grad[...], qkv_w[...]), resid_zero, inverse_one, gain_one)
    resid_grad = r.grad_one[...] + from_one
    r.resid_grad[...] = resid_grad
    pos_grad = jnp.transpose(resid_grad)
    nothing = jnp.zeros((8, width), jnp.float32)
    for d in range(2 * chips):
        at = (d % 2, d // 2 % 4, d // 8)
        head_pack[*at, pl.ds(0, 32), :] = low(
            jnp.concatenate([qkv_wgrad[24 * d : 24 * d + 24], merge_grad[8 * d : 8 * d + 8]], axis=0)
        )
        pos_piece = pos_grad[8 * d : 8 * d + 8]
        head_pack[*at, pl.ds(32, 16), :] = low(
            jnp.concatenate(
                [jnp.where(core == 0, pos_piece, nothing), jnp.where(core == 0, nothing, pos_piece)], axis=0
            )
        )
    reduce_head.to_pair()
    gain_buf = r.gain_buf
    gain_buf[chip] = jnp.concatenate([gain_grad_one, gain_grad_two, gain_grad_three], axis=1)
    gain_there = Scatter(place, None, gain_buf, r.gain_send, r.gain_recv)
    gain_there.start()
    gather_u.complete()
    spread_norm.arrived()
    cand_grad = r.acc
    cand_grad[...] = jnp.zeros_like(cand_grad)
    both_cand = r.emb_pair[...].reshape(both, width)
    both_corr = jnp.concatenate([turned(r.corr_pair[0]), turned(r.corr_pair[1])], axis=0)
    event_row = jnp.where(row_pos + 1 < own_length, 1.0 / total_events, 0.0)

    def give_block(there, own):
        block_rows = user_buf[there]
        coef = jnp.exp((dot_nt(both_cand, block_rows) - both_corr) - norm_buf[there])
        if own:
            coef = coef - jnp.where((pair_row == pair_col + 1) & (both_corr < 1e29), event_row, 0.0)
        cand_grad[...] += dot_nn(low(coef), block_rows)

    for step in range(chips):
        give_block(place.relative(step), step == 0)
    r.cand_out[...] = cand_grad[other_rows, :]
    pair_cand.start()
    reduce_head.to_plane()
    pair_cand.wait_recv()

    emb_grad = low(r.resid_grad[...] + (cand_grad[own_rows, :] + r.cand_in[...]))
    back_out, back_in = r.back_out, r.back_in
    back_out[...] = low(dot_nn(r.spread[...], emb_grad)).reshape(chips, capacity, width)
    back_in[core, chip] = back_out[chip]
    rows_back = Scatter(place, back_out, back_in.at[core], r.rows_send, r.rows_recv)
    rows_back.start()
    reduce_tail.to_line()
    asked_copy.wait_recv()
    asked_all = jnp.concatenate([r.asked[0], r.asked[1]], axis=1).astype(jnp.int32)
    part_rows = TABLE_PART if rows_dev % TABLE_PART == 0 else 8
    parts = [pl.ds(first, part_rows) for first in range(0, rows_dev, part_rows)]
    for part in parts:
        r.hot[part, :] = low(wide(iota_of((part_rows, 2 * asked), 0) + part.start == asked_all))

    reduce_head.to_line()
    shard = r.shard_grad
    shard[0:64] = reduce_tail.total()
    shard[64:112] = reduce_head.total()
    total = shard[...]
    gain_there.arrived()
    gain_total = gain_buf[0]
    for step in range(1, chips):
        gain_total = gain_total + gain_buf[step]
    gain_pair = r.gain_pair
    gain_pair[core] = gain_total
    gain_copy = remote(gain_pair.at[core], gain_pair.at[core], r.gp_send, r.gp_recv, chip, 1 - core)
    gain_copy.start()
    gain_copy.wait_recv()
    gain_total = gain_pair[0] + gain_pair[1]
    gain_three_rows = [gain_total[:, i * width : (i + 1) * width] for i in range(3)]
    gain_w[:, 0:8] = jnp.transpose(jnp.concatenate(gain_three_rows + [jnp.zeros((5, width), jnp.float32)], axis=0))
    r.gain_grad[...] = gain_w[pl.ds(pl.multiple_of(me * 8, 8), 8), :]
    gain_lane = iota_of((1, 3 * width), 1)
    gain_mine = lax.div(lax.rem(gain_lane, width), 8) == me
    square = jnp.sum(total * total, axis=0, keepdims=True)
    square = jnp.sum(square, axis=1, keepdims=True)
    square = square + jnp.sum(jnp.where(gain_mine, gain_total * gain_total, 0.0), axis=1, keepdims=True)
    lane = iota_of((1, 128), 1)
    r.scalar_pair[core] = jnp.where(lane == 0, square, jnp.where(lane == 1, loss_own, 0.0))
    pair_sums.start()

    rows_back.arrived()
    rows_pair = remote(back_in.at[core], back_in.at[core], r.rp_send, r.rp_recv, chip, 1 - core)
    rows_pair.start()
    rows_pair.wait_recv()
    table_grad = r.table_grad
    incoming = back_in[...].reshape(2 * asked, width)
    table_square = jnp.zeros((1, width), jnp.float32)
    for part in parts:
        grads = dot_nn(r.hot[part, :], incoming)
        table_grad[part, :] = grads
        table_square = table_square + jnp.sum(grads * grads, axis=0, keepdims=True)
    square = jnp.sum(table_square, axis=1, keepdims=True)

    scalar_buf = r.scalar_buf
    pair_sums.wait_recv()
    scalar_buf[chip] = r.scalar_pair[0] + r.scalar_pair[1] + jnp.where(lane == 0, square, 0.0)
    spread_sums.start()
    gather_a.sent()
    gather_b.sent()
    gather_c.sent()
    gather_u.sent()
    rows_there.sent()
    rows_back.sent()
    gain_there.sent()
    spread_corr.sent()
    spread_norm.sent()
    reduce_tail.sent()
    reduce_head.sent()
    pairs = (pair_a, pair_b, pair_emb, pair_corr, pair_user, pair_soft, pair_cand, pair_sums)
    for copy in (asked_copy, kv_copy, back_copy, gain_copy, rows_pair, *pairs):
        copy.wait_send()
    spread_sums.arrived()
    sums = scalar_buf[0]
    for d in range(1, chips):
        sums = sums + scalar_buf[d]
    r.sums[...] = jnp.where(lane == 2, total_events, sums)
    spread_sums.sent()


TABLE_PART = 224
CHUNKS = 4
ENDS = dict(
    ids=0, lengths=0, home=0, freq=0, table=0, pos=0, qkv=0, merge=0, widen=0, narrow=0, gains=0,
    table_grad=1, shard_grad=1, gain_grad=1, sums=1,
)


def scratch_of(sizes):
    (chips, rows_dev, seq_len, width, hidden, capacity, tokens, key_rows) = sizes
    f32, b16 = jnp.float32, jnp.bfloat16
    devices, levels = 2 * chips, chips // 4
    dma = pltpu.SemaphoreType.DMA
    lanes = -(-rows_dev // 128) * 128
    if lanes == rows_dev:
        lanes += 128
    sends = Gather.sends(chips)
    shapes = dict(
        table_here=pltpu.VMEM((rows_dev, width), f32),
        table_sem=dma,
        wa=pltpu.VMEM((2, chips, 48, width), b16),
        wb=pltpu.VMEM((2, chips, 80, width), b16),
        cand=pltpu.VMEM((chips, tokens, width), b16),
        corr=pltpu.VMEM((chips, 1, tokens), f32),
        logit=pltpu.VMEM((chips // CHUNKS, 2 * tokens, tokens), f32),
        user=pltpu.VMEM((chips, tokens, width), b16),
        emb_pair=pltpu.VMEM((2, tokens, width), b16),
        corr_pair=pltpu.VMEM((2, 1, tokens), f32),
        user_pair=pltpu.VMEM((2, tokens, width), b16),
        soft_out=pltpu.VMEM((tokens, width + 256), f32),
        soft_in=pltpu.VMEM((tokens, width + 256), f32),
        cand_out=pltpu.VMEM((tokens, width), f32),
        cand_in=pltpu.VMEM((tokens, width), f32),
        wa_pair=dma((2,)), wb_pair=dma((2,)), emb_sems=dma((2,)), corr_sems=dma((2,)),
        user_sems=dma((2,)), soft_sems=dma((2,)), cand_sems=dma((2,)),
        low_table=pltpu.VMEM((lanes, width), b16),
        keys=pltpu.VMEM((key_rows, 384), f32),
        home_all=pltpu.VMEM((chips, tokens), f32),
        row_out=pltpu.VMEM((chips, capacity, width), b16),
        row_in=pltpu.VMEM((chips, capacity, width), b16),
        asked=pltpu.VMEM((2, 1, chips * capacity), f32),
        spread=pltpu.VMEM((chips * capacity, tokens), b16),
        corr_col=pltpu.VMEM((tokens, 128), f32),
        qkv_w=pltpu.VMEM((3 * width, width), b16),
        pos_w=pltpu.VMEM((width, tokens), f32),
        gain_w=pltpu.VMEM((width, 128), f32),
        turn=pltpu.VMEM((128, 128), f32),
        gain_rows=pltpu.VMEM((8, width), f32),
        merge_w=pltpu.VMEM((width, width), b16),
        widen_w=pltpu.VMEM((hidden, width), b16),
        narrow_w=pltpu.VMEM((width, hidden), b16),
        resid_zero=pltpu.VMEM((tokens, width), f32),
        resid_one=pltpu.VMEM((tokens, width), f32),
        resid_two=pltpu.VMEM((tokens, width), f32),
        input_one=pltpu.VMEM((tokens, width), b16),
        input_two=pltpu.VMEM((tokens, width), b16),
        query_rows=pltpu.VMEM((HEADS * tokens, width), b16),
        mixed_rows=pltpu.VMEM((HEADS * tokens, width), b16),
        key_rows=pltpu.VMEM((2 * HEADS * tokens, width), b16),
        value_rows=pltpu.VMEM((2 * HEADS * tokens, width), b16),
        prob_own=pltpu.VMEM((HEADS * tokens, tokens), b16),
        prob_other=pltpu.VMEM((HEADS * tokens, tokens), b16),
        prob_lanes=pltpu.VMEM((tokens, 2 * HEADS * tokens), b16),
        score_own=pltpu.VMEM((HEADS * tokens, tokens), b16),
        score_other=pltpu.VMEM((HEADS * tokens, tokens), b16),
        score_lanes=pltpu.VMEM((tokens, 2 * HEADS * tokens), b16),
        kv=pltpu.VMEM((2, tokens, 2 * width), b16),
        prob=pltpu.VMEM((HEADS, tokens, 2 * tokens), f32),
        acc=pltpu.VMEM((2 * tokens, width), f32),
        attended=pltpu.VMEM((tokens, width), b16),
        act=pltpu.VMEM((tokens, hidden), b16),
        slope=pltpu.VMEM((tokens, hidden), f32),
        pre=pltpu.VMEM((tokens, hidden), b16),
        peaks=pltpu.VMEM((2 * tokens, 128), f32),
        totals=pltpu.VMEM((2 * tokens, 128), f32),
        norm=pltpu.VMEM((chips, 1, tokens), f32),
        grad_one=pltpu.VMEM((tokens, width), f32),
        mixed=pltpu.VMEM((tokens, width), b16),
        tail_pack=pltpu.VMEM((2, 4, levels, 64, width), b16),
        tail_pair=pltpu.VMEM((4, levels, 64, width), b16),
        tail_sum=pltpu.VMEM((4, levels, 64, width), b16),
        tail_plane=pltpu.VMEM((4, levels, 64, width), b16),
        tail_part=pltpu.VMEM((levels, 64, width), b16),
        tail_line=pltpu.VMEM((levels, 64, width), b16),
        tail_sems=dma((10 + 2 * levels,)),
        head_pack=pltpu.VMEM((2, 4, levels, 48, width), b16),
        head_pair=pltpu.VMEM((4, levels, 48, width), b16),
        head_sum=pltpu.VMEM((4, levels, 48, width), b16),
        head_plane=pltpu.VMEM((4, levels, 48, width), b16),
        head_part=pltpu.VMEM((levels, 48, width), b16),
        head_line=pltpu.VMEM((levels, 48, width), b16),
        head_sems=dma((10 + 2 * levels,)),
        back=pltpu.VMEM((2, tokens, 2 * width), b16),
        qkv_grad=pltpu.VMEM((tokens, 3 * width), b16),
        resid_grad=pltpu.VMEM((tokens, width), f32),
        gain_buf=pltpu.VMEM((chips, 1, 3 * width), f32),
        gain_pair=pltpu.VMEM((2, 1, 3 * width), f32),
        back_out=pltpu.VMEM((chips, capacity, width), b16),
        back_in=pltpu.VMEM((2, chips, capacity, width), b16),
        hot=pltpu.VMEM((rows_dev, 2 * chips * capacity), b16),
        scalar_buf=pltpu.VMEM((chips, 1, 128), f32),
        scalar_pair=pltpu.VMEM((2, 1, 128), f32),
        sums_sems=dma((2,)),
        wa_send=dma((sends,)), wa_recv=dma((chips,)),
        wb_send=dma((sends,)), wb_recv=dma((chips,)),
        cand_send=dma((sends,)), cand_recv=dma((chips,)),
        user_send=dma((sends,)), user_recv=dma((chips,)),
        row_send=dma((chips,)), row_recv=dma((chips,)),
        rows_send=dma((chips,)), rows_recv=dma((chips,)),
        gain_send=dma((chips,)), gain_recv=dma((chips,)),
        norm_send=dma((chips,)), norm_recv=dma((chips,)),
        corr_send=dma((chips,)), corr_recv=dma((chips,)),
        scalar_send=dma((chips,)), scalar_recv=dma((chips,)),
        asked_send=dma, asked_recv=dma,
        kv_send=dma, kv_recv=dma,
        back_send=dma, back_recv=dma,
        gp_send=dma, gp_recv=dma,
        rp_send=dma, rp_recv=dma,
    )
    return shapes


def adam(weight, first, second, grad, rate):
    first = beta_one * first + (1.0 - beta_one) * grad
    second = beta_two * second + (1.0 - beta_two) * grad * grad
    fix_one = 1.0 - beta_one**STEP
    fix_two = 1.0 - beta_two**STEP
    update = first / fix_one / (jnp.sqrt(second / fix_two) + adam_eps) + decay_rate * weight
    return weight - rate * update, first, second


def update_kernel(*refs):
    (table_grad, shard, gain_grad, sums), refs = refs[:4], refs[4:]
    ins, outs, turn = refs[:21], refs[21:-1], refs[-1]
    square = sums[0:1, 0:1]
    norm = jnp.sqrt(square)
    factor = jnp.minimum(1.0, clip_limit / norm)

    def update(index, grad, rate):
        new = adam(*(ref[...] for ref in ins[3 * index : 3 * index + 3]), grad * factor, rate)
        for ref, value in zip(outs[3 + 3 * index : 6 + 3 * index], new):
            ref[...] = value

    update(0, table_grad[...], learn_rate)

    @pl.when(pl.program_id(0) == 0)
    def _():
        outs[0][...] = sums[0:1, 1:2]
        outs[1][...] = sums[0:1, 2:3]
        outs[2][...] = norm
        update(1, jnp.concatenate([shard[96:104, :], shard[104:112, :]], axis=1), learn_rate)
        update(2, shard[64:88, :], learn_rate)
        update(3, shard[88:96, :], learn_rate)
        update(4, shard[0:32, :], learn_rate)
        update(5, jnp.concatenate([shard[32 + 8 * i : 40 + 8 * i, :] for i in range(4)], axis=1), learn_rate)
        turn[0:8, :] = gain_grad[...]
        update(6, jnp.transpose(turn[...])[0:3, 0:8], gain_rate)


def fused_body(*args):
    (item_ids, lengths, home_row, log_freq) = args[:4]
    weights = args[4:]
    item_table = weights[0]
    rows_dev, width = item_table.shape
    chips = lax.axis_size("dp")
    seq_len = item_ids.shape[1]
    tokens = seq_len // 2
    hidden = weights[12].shape[1] * 2 * chips
    capacity = 2 * tokens // chips
    key_rows = -(-home_row.shape[0] // (128 * 128)) * 128
    sizes = (chips, rows_dev, seq_len, width, hidden, capacity, tokens, key_rows)
    dense = [w.T for w in weights[3:18]]
    shapes = scratch_of(sizes)
    vmem = pl.BlockSpec(memory_space=pltpu.VMEM)
    smem = pl.BlockSpec(memory_space=pltpu.SMEM)
    f32 = jnp.float32
    table_grad, shard, gain_grad, sums = pl.pallas_call(
        functools.partial(step_kernel, sizes),
        out_shape=[
            jax.ShapeDtypeStruct((rows_dev, width), f32),
            jax.ShapeDtypeStruct((112, width), f32),
            jax.ShapeDtypeStruct((8, 128), f32),
            jax.ShapeDtypeStruct((1, 128), f32),
        ],
        in_specs=[vmem, smem, vmem, vmem, pl.BlockSpec(memory_space=pl.ANY)] + [vmem] * 6,
        out_specs=[vmem] * 4,
        scratch_shapes=list(shapes.values()),
        compiler_params=pltpu.CompilerParams(
            collective_id=0, has_side_effects=True, vmem_limit_bytes=60 * 2**20
        ),
    )(
        item_ids, lengths, home_row.reshape(-1, 128), log_freq.reshape(-1, 128), item_table,
        dense[0], dense[3], dense[6], dense[9], dense[12], weights[18],
    )
    part = rows_dev // 2 if rows_dev % 16 == 0 else rows_dev
    table_spec = pl.BlockSpec((part, width), lambda i: (i, 0))

    def whole(x):
        return pl.BlockSpec(x.shape, lambda i: (0,) * len(x.shape))

    small = dense + [weights[18], weights[19], weights[20]]
    one = jax.ShapeDtypeStruct((1, 1), f32)
    outs = pl.pallas_call(
        update_kernel,
        grid=(rows_dev // part,),
        out_shape=[one] * 3 + [jax.ShapeDtypeStruct(x.shape, f32) for x in list(weights[:3]) + small],
        in_specs=[table_spec, whole(shard), whole(gain_grad), whole(sums)] + [table_spec] * 3 + [whole(x) for x in small],
        out_specs=[whole(one)] * 3 + [table_spec] * 3 + [whole(x) for x in small],
        scratch_shapes=[pltpu.VMEM((128, 128), f32)],
        compiler_params=pltpu.CompilerParams(vmem_limit_bytes=60 * 2**20),
    )(table_grad, shard, gain_grad, sums, *weights[:3], *small)
    outs = list(outs)
    return tuple(
        [x.reshape(()) for x in outs[:3]] + outs[3:6] + [x.T for x in outs[6:21]] + outs[21:]
    )


def solution(mesh):
    placed = (
        P(),
        P(),
        P(),
        P(),
        P("dp", None),
        P("dp", None),
        P("dp", None),
        P(None, ("dp", "sub")),
        P(None, ("dp", "sub")),
        P(None, ("dp", "sub")),
        P(None, ("dp", "sub")),
        P(None, ("dp", "sub")),
        P(None, ("dp", "sub")),
        P(None, ("dp", "sub")),
        P(None, ("dp", "sub")),
        P(None, ("dp", "sub")),
        P(None, ("dp", "sub")),
        P(None, ("dp", "sub")),
        P(None, ("dp", "sub")),
        P(None, ("dp", "sub")),
        P(None, ("dp", "sub")),
        P(None, ("dp", "sub")),
        P(None, ("dp", "sub")),
        P(None, ("dp", "sub")),
        P(None, ("dp", "sub")),
    )
    fits = mesh.shape["sub"] == 2 and mesh.shape["dp"] == 16
    return jax.shard_map(
        fused_body if fits else body,
        mesh=mesh,
        in_specs=placed,
        out_specs=(
            P(),
            P(),
            P(),
            P("dp", None),
            P("dp", None),
            P("dp", None),
            P(None, ("dp", "sub")),
            P(None, ("dp", "sub")),
            P(None, ("dp", "sub")),
            P(None, ("dp", "sub")),
            P(None, ("dp", "sub")),
            P(None, ("dp", "sub")),
            P(None, ("dp", "sub")),
            P(None, ("dp", "sub")),
            P(None, ("dp", "sub")),
            P(None, ("dp", "sub")),
            P(None, ("dp", "sub")),
            P(None, ("dp", "sub")),
            P(None, ("dp", "sub")),
            P(None, ("dp", "sub")),
            P(None, ("dp", "sub")),
            P(None, ("dp", "sub")),
            P(None, ("dp", "sub")),
            P(None, ("dp", "sub")),
        ),
        check_vma=False,
    )
```

```python
import functools
import math
import types

import jax
import jax.numpy as jnp
from jax import lax
from jax.experimental import pallas as pl
from jax.experimental.pallas import tpu as pltpu
from jax.sharding import PartitionSpec as P

HEADS = 8
STEP = 10


norm_eps = 1e-06
beta_one = 0.9
beta_two = 0.999
adam_eps = 1e-08
decay_rate = 0.01
learn_rate = 0.1
gain_rate = 0.5
clip_limit = 0.01
big_negative = -1e30
block_cols = 4096


def dot_plain(left_mat, right_mat):
    return jnp.dot(left_mat, right_mat, preferred_element_type=jnp.float32)


def dot_left_t(left_mat, right_mat):
    return lax.dot_general(
        left_mat, right_mat, (((0,), (0,)), ((), ())), preferred_element_type=jnp.float32
    )


def dot_right_t(left_mat, right_mat):
    return lax.dot_general(
        left_mat, right_mat, (((1,), (1,)), ((), ())), preferred_element_type=jnp.float32
    )


def rms_forward(values, gain_row):
    inverse = lax.rsqrt(jnp.mean(values * values, axis=-1, keepdims=True) + norm_eps)
    return (values * inverse * gain_row, inverse)


def rms_backward(upstream, values, inverse, gain_row):
    unit_vals = values * inverse
    gain_grad = jnp.sum(upstream * unit_vals, axis=0)
    scaled = upstream * gain_row
    inner_mean = jnp.mean(scaled * unit_vals, axis=-1, keepdims=True)
    return (inverse * (scaled - unit_vals * inner_mean), gain_grad)


def head_scores(queries, keys_all, allowed):
    scaling = queries.shape[-1] ** (-0.5)
    plain_scores = (
        jnp.einsum("bqhe,bkhe->bhqk", queries, keys_all, preferred_element_type=jnp.float32)
        * scaling
    )
    return jnp.where(allowed, plain_scores, big_negative)


def target_of(indices, slice_len, tokens_dev):
    within = indices % slice_len
    return jnp.where(within + 1 < slice_len, indices + 1, indices - within + tokens_dev)


def logits_for(user_rows, cand_rows, corr_rows, valid_rows):
    logits = dot_right_t(user_rows, cand_rows) - corr_rows[None, :]
    return jnp.where(valid_rows[None, :], logits, big_negative)


def coefficient(logits, log_total, weights, columns, targets):
    hits = (columns[None, :] == targets[:, None]).astype(jnp.float32)
    return (weights[:, None] * (jnp.exp(logits - log_total[:, None]) - hits)).astype(jnp.bfloat16)


def block_forward(resid_zero, dense_w, allowed, hist_local):
    qkv_full, merge_full, widen_full, narrow_full, gains_full = dense_w
    gain_float = gains_full.astype(jnp.float32)
    tokens_dev, model_width = resid_zero.shape
    normed_one, inverse_one = rms_forward(resid_zero, gain_float[0])
    input_one = normed_one.astype(jnp.bfloat16)
    qkv_parts = (
        dot_plain(input_one, qkv_full)
        .astype(jnp.bfloat16)
        .reshape(hist_local, -1, 3, HEADS, model_width // HEADS)
    )
    queries = qkv_parts[:, :, 0]
    keys_all, values_all = (
        lax.all_gather(qkv_parts[:, :, 1], "sub", axis=1, tiled=True),
        lax.all_gather(qkv_parts[:, :, 2], "sub", axis=1, tiled=True),
    )
    scores = head_scores(queries, keys_all, allowed)
    row_peak = jnp.max(scores, axis=-1, keepdims=True)
    expo_vals = jnp.exp(scores - row_peak)
    row_total = jnp.sum(expo_vals, axis=-1, keepdims=True)
    log_total = row_peak + jnp.log(row_total)
    attn_prob = (expo_vals / row_total).astype(jnp.bfloat16)
    attended = jnp.einsum(
        "bhqk,bkhe->bqhe", attn_prob, values_all, preferred_element_type=jnp.float32
    )
    attended = attended.astype(jnp.bfloat16).reshape(tokens_dev, model_width)
    resid_one = resid_zero + dot_plain(attended, merge_full)
    normed_two, inverse_two = rms_forward(resid_one, gain_float[1])
    input_two = normed_two.astype(jnp.bfloat16)
    hidden_pre = dot_plain(input_two, widen_full)
    hidden_act = jax.nn.gelu(hidden_pre).astype(jnp.bfloat16)
    resid_two = resid_one + dot_plain(hidden_act, narrow_full)
    normed_three, inverse_three = rms_forward(resid_two, gain_float[2])
    kept = (
        resid_zero,
        inverse_one,
        input_one,
        queries,
        keys_all,
        values_all,
        log_total,
        attended,
        resid_one,
        inverse_two,
        input_two,
        hidden_pre,
        hidden_act,
        resid_two,
        inverse_three,
    )
    return (normed_three.astype(jnp.bfloat16), kept)


def block_backward(user_grad, kept, dense_w, allowed):
    (
        resid_zero,
        inverse_one,
        input_one,
        queries,
        keys_all,
        values_all,
        log_total,
        attended,
        resid_one,
        inverse_two,
        input_two,
        hidden_pre,
        hidden_act,
        resid_two,
        inverse_three,
    ) = kept
    qkv_full, merge_full, widen_full, narrow_full, gains_full = dense_w
    gain_float = gains_full.astype(jnp.float32)
    tokens_dev, model_width = resid_zero.shape
    head_dim = queries.shape[-1]
    grad_two, gain_three = rms_backward(user_grad, resid_two, inverse_three, gain_float[2])
    branch_two = grad_two.astype(jnp.bfloat16)
    narrow_grad = dot_left_t(hidden_act, branch_two)
    hidden_grad = dot_right_t(branch_two, narrow_full)
    pre_grad = jax.vjp(jax.nn.gelu, hidden_pre)[1](hidden_grad)[0].astype(jnp.bfloat16)
    widen_grad = dot_left_t(input_two, pre_grad)
    from_two, gain_two = rms_backward(
        dot_right_t(pre_grad, widen_full), resid_one, inverse_two, gain_float[1]
    )
    grad_one = grad_two + from_two
    branch_one = grad_one.astype(jnp.bfloat16)
    merge_grad = dot_left_t(attended, branch_one)
    mixed_grad = dot_right_t(branch_one, merge_full).astype(jnp.bfloat16).reshape(queries.shape)
    scores = head_scores(queries, keys_all, allowed)
    attn_prob = jnp.exp(scores - log_total)
    prob_grad = jnp.einsum(
        "bqhe,bkhe->bhqk", mixed_grad, values_all, preferred_element_type=jnp.float32
    )
    score_grad = attn_prob * (prob_grad - jnp.sum(attn_prob * prob_grad, axis=-1, keepdims=True))
    score_grad = score_grad.astype(jnp.bfloat16)
    scaling = head_dim ** (-0.5)
    query_grad = (
        jnp.einsum("bhqk,bkhe->bqhe", score_grad, keys_all, preferred_element_type=jnp.float32)
        * scaling
    )
    keys_grad = (
        jnp.einsum("bhqk,bqhe->bkhe", score_grad, queries, preferred_element_type=jnp.float32)
        * scaling
    )
    values_grad = jnp.einsum(
        "bhqk,bqhe->bkhe",
        attn_prob.astype(jnp.bfloat16),
        mixed_grad,
        preferred_element_type=jnp.float32,
    )
    key_own, value_own = (
        lax.psum_scatter(
            keys_grad.astype(jnp.bfloat16), "sub", scatter_dimension=1, tiled=True
        ).astype(jnp.float32),
        lax.psum_scatter(
            values_grad.astype(jnp.bfloat16), "sub", scatter_dimension=1, tiled=True
        ).astype(jnp.float32),
    )
    qkv_grad = (
        jnp.stack([query_grad, key_own, value_own], axis=2)
        .astype(jnp.bfloat16)
        .reshape(tokens_dev, 3 * model_width)
    )
    qkv_wgrad = dot_left_t(input_one, qkv_grad)
    from_one, gain_one = rms_backward(
        dot_right_t(qkv_grad, qkv_full), resid_zero, inverse_one, gain_float[0]
    )
    gain_grads = jnp.stack([gain_one, gain_two, gain_three])
    return (grad_one + from_one, (qkv_wgrad, merge_grad, widen_grad, narrow_grad, gain_grads))


def adamw(weight, moment_one, moment_two, gradient, rate):
    moment_one = beta_one * moment_one + (1.0 - beta_one) * gradient
    moment_two = beta_two * moment_two + (1.0 - beta_two) * gradient * gradient
    fix_one = 1.0 - beta_one**STEP
    fix_two = 1.0 - beta_two**STEP
    update = (
        moment_one / fix_one / (jnp.sqrt(moment_two / fix_two) + adam_eps) + decay_rate * weight
    )
    return (weight - rate * update, moment_one, moment_two)


def body(
    item_ids,
    lengths,
    home_row,
    log_freq,
    item_table,
    table_first,
    table_second,
    pos_table,
    pos_first,
    pos_second,
    qkv_weight,
    qkv_first,
    qkv_second,
    merge_weight,
    merge_first,
    merge_second,
    widen_weight,
    widen_first,
    widen_second,
    narrow_weight,
    narrow_first,
    narrow_second,
    norm_gains,
    gains_first,
    gains_second,
):
    dp_count = lax.axis_size("dp")
    sub_count = lax.axis_size("sub")
    dp_index = lax.axis_index("dp")
    sub_index = lax.axis_index("sub")
    rows_dev, model_width = item_table.shape
    hist_local = item_ids.shape[0] // dp_count
    seq_len = item_ids.shape[1]
    slice_len = seq_len // sub_count
    tokens_dev = hist_local * slice_len
    capacity = max(2, (2 * tokens_dev + dp_count - 1) // dp_count)
    all_tokens = dp_count * sub_count * tokens_dev
    pos_full, qkv_full, merge_full, widen_full, narrow_full, gains_full = (
        lax.all_gather(pos_table.astype(jnp.bfloat16), ("dp", "sub"), axis=1, tiled=True),
        lax.all_gather(qkv_weight.astype(jnp.bfloat16), ("dp", "sub"), axis=1, tiled=True),
        lax.all_gather(merge_weight.astype(jnp.bfloat16), ("dp", "sub"), axis=1, tiled=True),
        lax.all_gather(widen_weight.astype(jnp.bfloat16), ("dp", "sub"), axis=1, tiled=True),
        lax.all_gather(narrow_weight.astype(jnp.bfloat16), ("dp", "sub"), axis=1, tiled=True),
        lax.all_gather(norm_gains.astype(jnp.bfloat16), ("dp", "sub"), axis=1, tiled=True),
    )
    dense_w = (qkv_full, merge_full, widen_full, narrow_full, gains_full)
    own_items = lax.dynamic_slice(
        item_ids, (dp_index * hist_local, sub_index * slice_len), (hist_local, slice_len)
    ).reshape(tokens_dev)
    stored_at = home_row[own_items]
    owner_dev = stored_at // rows_dev
    local_row = stored_at % rows_dev
    owner_hot = (owner_dev[:, None] == jnp.arange(dp_count, dtype=jnp.int32)[None, :]).astype(
        jnp.int32
    )
    owner_rank = jnp.sum(jnp.cumsum(owner_hot, axis=0) * owner_hot, axis=1) - 1
    slot_index = owner_dev * capacity + owner_rank
    request = (
        jnp.zeros((dp_count * capacity,), jnp.int32)
        .at[slot_index]
        .set(local_row)
        .reshape(dp_count, capacity)
    )
    arrived = lax.all_to_all(request, "dp", split_axis=0, concat_axis=0, tiled=True)
    found_rows = item_table[arrived].astype(jnp.bfloat16)
    arrived_rows = lax.all_to_all(found_rows, "dp", split_axis=0, concat_axis=0, tiled=True)
    embedded = arrived_rows.reshape(dp_count * capacity, model_width)[slot_index]
    pos_rows = lax.dynamic_slice_in_dim(pos_full, sub_index * slice_len, slice_len, 0).astype(
        jnp.float32
    )
    resid_zero = (
        embedded.astype(jnp.float32).reshape(hist_local, slice_len, model_width) + pos_rows[None]
    ).reshape(tokens_dev, model_width)
    query_pos = sub_index * slice_len + jnp.arange(slice_len)
    allowed = jnp.arange(seq_len)[None, :] <= query_pos[:, None]
    user_vecs, kept = block_forward(resid_zero, dense_w, allowed, hist_local)
    candidates = lax.all_gather(embedded, ("dp", "sub"), axis=0, tiled=True)
    layout = (dp_count, hist_local, sub_count, slice_len)

    def by_device(values):
        return values.reshape(layout).transpose(0, 2, 1, 3).reshape(all_tokens)

    all_items = by_device(item_ids)
    all_pos = by_device(
        jnp.broadcast_to(jnp.arange(seq_len, dtype=jnp.int32)[None, :], item_ids.shape)
    )
    all_len = by_device(jnp.broadcast_to(lengths[:, None], item_ids.shape))
    valid_all = (all_pos >= 1) & (all_pos < all_len)
    correction = log_freq[all_items]
    base_index = (dp_index * sub_count + sub_index) * tokens_dev
    own_index = base_index + jnp.arange(tokens_dev)
    own_pos = lax.dynamic_slice_in_dim(all_pos, base_index, tokens_dev)
    own_len = lax.dynamic_slice_in_dim(all_len, base_index, tokens_dev)
    event_count = jnp.sum(lengths - 1).astype(jnp.float32)
    valid_rows = (own_pos + 1 < own_len).astype(jnp.float32)
    row_weight = valid_rows / event_count
    targets = target_of(own_index, slice_len, tokens_dev)
    col_block = min(block_cols, all_tokens)
    starts = jnp.arange(all_tokens // col_block) * col_block

    def block_logits(block_start):
        cand_rows = lax.dynamic_slice_in_dim(candidates, block_start, col_block, 0)
        corr_rows = lax.dynamic_slice_in_dim(correction, block_start, col_block)
        valid_cols = lax.dynamic_slice_in_dim(valid_all, block_start, col_block)
        return (
            cand_rows,
            logits_for(user_vecs, cand_rows, corr_rows, valid_cols),
            block_start + jnp.arange(col_block),
        )

    def forward_block(running, block_start):
        row_peak, row_total, target_logit = running
        cand_rows, logits, columns = block_logits(block_start)
        new_peak = jnp.maximum(row_peak, jnp.max(logits, axis=1))
        row_total = row_total * jnp.exp(row_peak - new_peak) + jnp.sum(
            jnp.exp(logits - new_peak[:, None]), axis=1
        )
        target_logit = target_logit + jnp.sum(
            jnp.where(columns[None, :] == targets[:, None], logits, 0.0), axis=1
        )
        return ((new_peak, row_total, target_logit), None)

    start_state = (
        jnp.full((tokens_dev,), big_negative, jnp.float32),
        jnp.zeros((tokens_dev,), jnp.float32),
        jnp.zeros((tokens_dev,), jnp.float32),
    )
    (row_peak, row_total, target_logit), _ = lax.scan(forward_block, start_state, starts)
    log_total = row_peak + jnp.log(row_total)
    loss_local = jnp.sum(valid_rows * (log_total - target_logit))

    def user_block(running, block_start):
        cand_rows, logits, columns = block_logits(block_start)
        coeffs = coefficient(logits, log_total, row_weight, columns, targets)
        return (running + dot_plain(coeffs, cand_rows), None)

    user_grad, _ = lax.scan(user_block, jnp.zeros((tokens_dev, model_width), jnp.float32), starts)
    step_rows = math.gcd(tokens_dev * lax.axis_size(("dp", "sub")), max(block_cols, tokens_dev))

    def one_block(offset):
        cand_rows = lax.dynamic_slice_in_dim(candidates, offset, step_rows, 0)
        corr_rows = lax.dynamic_slice_in_dim(correction, offset, step_rows)
        valid_cols = lax.dynamic_slice_in_dim(valid_all, offset, step_rows)
        logits = logits_for(user_vecs, cand_rows, corr_rows, valid_cols)
        coeffs = coefficient(logits, log_total, row_weight, offset + jnp.arange(step_rows), targets)
        return dot_left_t(coeffs, user_vecs)

    pieces = lax.map(
        one_block, jnp.arange(tokens_dev * lax.axis_size(("dp", "sub")) // step_rows) * step_rows
    )
    cand_grad = lax.psum_scatter(
        pieces.reshape(tokens_dev * lax.axis_size(("dp", "sub")), model_width),
        ("dp", "sub"),
        scatter_dimension=0,
        tiled=True,
    )
    resid_grad, weight_grads = block_backward(user_grad, kept, dense_w, allowed)
    qkv_wgrad, merge_grad, widen_grad, narrow_grad, gain_grads = weight_grads
    emb_grad = resid_grad + cand_grad
    pos_rows_grad = jnp.sum(resid_grad.reshape(hist_local, slice_len, model_width), axis=0)
    pos_grad = lax.dynamic_update_slice_in_dim(
        jnp.zeros((seq_len, model_width), jnp.float32), pos_rows_grad, sub_index * slice_len, 0
    )
    outgoing = (
        jnp.zeros((dp_count * capacity, model_width), jnp.float32).at[slot_index].set(emb_grad)
    )
    incoming = lax.all_to_all(
        outgoing.reshape(dp_count, capacity, model_width),
        "dp",
        split_axis=0,
        concat_axis=0,
        tiled=True,
    )
    incoming_rows = incoming.reshape(-1, model_width)
    arrived_flat = arrived.reshape(-1)
    plane_grad = jnp.zeros((rows_dev, model_width), jnp.float32).at[arrived_flat].add(incoming_rows)
    table_grad = lax.psum(plane_grad, "sub")
    shard_grads = (
        lax.psum_scatter(pos_grad, ("dp", "sub"), scatter_dimension=1, tiled=True),
        lax.psum_scatter(qkv_wgrad, ("dp", "sub"), scatter_dimension=1, tiled=True),
        lax.psum_scatter(merge_grad, ("dp", "sub"), scatter_dimension=1, tiled=True),
        lax.psum_scatter(widen_grad, ("dp", "sub"), scatter_dimension=1, tiled=True),
        lax.psum_scatter(narrow_grad, ("dp", "sub"), scatter_dimension=1, tiled=True),
        lax.psum_scatter(gain_grads, ("dp", "sub"), scatter_dimension=1, tiled=True),
    )
    square_part = sum((jnp.sum(gradient * gradient) for gradient in shard_grads))
    square_part = square_part + jnp.where(sub_index == 0, jnp.sum(table_grad * table_grad), 0.0)
    loss_sum, square_sum = lax.psum((loss_local, square_part), ("dp", "sub"))
    grad_norm = jnp.sqrt(square_sum)
    factor = jnp.minimum(1.0, clip_limit / grad_norm)
    masters = (
        item_table,
        pos_table,
        qkv_weight,
        merge_weight,
        widen_weight,
        narrow_weight,
        norm_gains,
    )
    firsts = (
        table_first,
        pos_first,
        qkv_first,
        merge_first,
        widen_first,
        narrow_first,
        gains_first,
    )
    seconds = (
        table_second,
        pos_second,
        qkv_second,
        merge_second,
        widen_second,
        narrow_second,
        gains_second,
    )
    rates = (learn_rate,) * 6 + (gain_rate,)
    all_grads = (table_grad,) + tuple(shard_grads)
    results = [loss_sum, event_count, grad_norm]
    for weight, moment_one, moment_two, gradient, rate in zip(
        masters, firsts, seconds, all_grads, rates
    ):
        results.extend(adamw(weight, moment_one, moment_two, gradient * factor, rate))
    return tuple(results)


MESH_ID = pl.DeviceIdType.MESH
FF_CHUNK = 256


def dot_nn(left, right):
    return lax.dot_general(
        left, right, (((1,), (0,)), ((), ())), preferred_element_type=jnp.float32
    )


def dot_nt(left, right):
    return lax.dot_general(
        left, right, (((1,), (1,)), ((), ())), preferred_element_type=jnp.float32
    )


def dot_tn(left, right):
    return lax.dot_general(
        left, right, (((0,), (0,)), ((), ())), preferred_element_type=jnp.float32
    )


def low(values):
    return values.astype(jnp.bfloat16)


def wide(values):
    return values.astype(jnp.float32)


def iota_of(shape, axis):
    return lax.broadcasted_iota(jnp.int32, shape, axis)


def flip(index, bits):
    total = 0
    for power in (1, 2, 4, 8):
        a = lax.rem(lax.div(index, power), 2)
        b = (bits // power) % 2 if isinstance(bits, int) else lax.rem(lax.div(bits, power), 2)
        total = total + power * (a + b - 2 * a * b)
    return total


def arrival_order(levels):
    if levels == 4:
        return [(0, 0), (0, 1), (0, 2), (1, 0), (2, 0), (0, 3), (1, 1), (1, 2), (3, 0), (2, 1), (2, 2), (1, 3), (3, 1), (3, 2), (2, 3), (3, 3)]
    return [(level, corner) for level in range(levels) for corner in range(4)]


class Place:
    def __init__(self, chips):
        self.chips = chips
        self.chip = lax.axis_index("dp")
        self.core = lax.axis_index("sub")
        self.level = lax.div(self.chip, 4)
        self.corner = lax.rem(self.chip, 4)
        self.inner = (self.level == 1) | (self.level == 2)
        self.near_x = self.level * 4 + flip(self.corner, 1)
        self.near_y = self.level * 4 + flip(self.corner, 2)

    def step(self, way):
        return arrival_order(self.chips // 4).index(way)

    def way(self, step):
        order = arrival_order(self.chips // 4)
        if isinstance(step, int):
            return order[step]
        return tuple(
            sum(jnp.where(step == i, place[axis], 0) for i, place in enumerate(order) if place[axis])
            for axis in range(2)
        )

    def relative(self, step):
        level, corner = self.way(step)
        return flip(self.level, level) * 4 + flip(self.corner, corner)


def remote(src, dst, send, recv, chip, core):
    return pltpu.make_async_remote_copy(
        src_ref=src,
        dst_ref=dst,
        send_sem=send,
        recv_sem=recv,
        device_id=(chip, core),
        device_id_type=MESH_ID,
    )


class Gather:
    def __init__(self, place, buf, send, recv):
        self.place, self.buf, self.send, self.recv = place, buf, send, recv
        self.levels = place.chips // 4
        order = [(0, 1), (1, 0), (2, 0), (1, 2), (3, 0), (2, 1)]
        self.queue = [place.step(at) for at in order]
        self.waiting = set(range(1, place.chips))

    def copy(self, block, sem, chip):
        return remote(
            self.buf.at[block], self.buf.at[block], self.send.at[sem], self.recv.at[block], chip, self.place.core
        )

    def send_on(self, step, action):
        place = self.place
        block = place.relative(step)
        level, corner = place.way(step)
        last = level == self.levels - 1
        if corner == 0 or (corner == 2 and level % 2 == 1 and not last):
            action(self.copy(block, step * 2, place.near_x))
        if corner == 0 or (corner == 1 and level % 2 == 0 and not last):
            action(self.copy(block, step * 2 + 1, place.near_y))
        if corner == 0 and last:
            action(self.copy(block, place.chips * 2, place.level * 4 + 3 - place.corner))
        if corner == 0 and level == 2:
            @pl.when(place.inner)
            def _():
                action(self.copy(block, place.chips * 2 + 4, flip(place.level, 1) * 4 + place.corner))

    def along_z(self, action):
        place = self.place
        for step in (1, 3, 2):
            chip = flip(place.level, step) * 4 + place.corner
            copy = self.copy(place.chip, place.chips * 2 + step, chip)
            if step == 3:
                pl.when(place.inner)(lambda copy=copy: action(copy))
            else:
                action(copy)

    def start(self):
        self.along_z(lambda copy: copy.start())
        self.send_on(0, lambda copy: copy.start())

    def need(self, steps):
        for step in steps:
            if step in self.waiting:
                self.waiting.remove(step)
                self.copy(self.place.relative(step), 0, self.place.chip).wait_recv()
            if step in self.queue:
                self.queue.remove(step)
                self.send_on(step, lambda copy: copy.start())

    def advance(self, count):
        self.need(self.queue[:count])

    def complete(self):
        self.advance(len(self.queue))
        self.need(sorted(self.waiting))

    def sent(self):
        self.along_z(lambda copy: copy.wait_send())
        for step in range(self.place.chips):
            self.send_on(step, lambda copy: copy.wait_send())

    @staticmethod
    def sends(chips):
        return chips * 2 + 8


class ShortGather(Gather):
    def __init__(self, place, buf, send, recv):
        super().__init__(place, buf, send, recv)
        self.queue = [place.step((level, 0)) for level in range(1, self.levels)]

    def send_on(self, step, action):
        place = self.place
        block = place.relative(step)
        if place.way(step)[1] == 0:
            action(self.copy(block, step * 2, place.near_x))
            action(self.copy(block, step * 2 + 1, place.near_y))
            action(self.copy(block, place.chips * 2 + 4 + place.way(step)[0], place.level * 4 + 3 - place.corner))

    def along_z(self, action):
        place = self.place
        for step in (1, 3, 2):
            chip = flip(place.level, step) * 4 + place.corner
            action(self.copy(place.chip, place.chips * 2 + step, chip))


def to_sibling(place, src, dst, sems):
    return remote(src, dst, sems.at[0], sems.at[1], place.chip, 1 - place.core)


class Scatter:
    def __init__(self, place, src, dst, send, recv):
        self.place, self.src, self.dst, self.send, self.recv = place, src, dst, send, recv

    def copy(self, to, at):
        place = self.place
        return remote(
            self.src.at[to] if self.src is not None else self.dst.at[place.chip],
            self.dst.at[at],
            self.send.at[to],
            self.recv.at[at],
            to,
            place.core,
        )

    def each(self, action):
        place = self.place

        def step(index, carry):
            action(lax.rem(place.chip + index, place.chips))
            return carry

        lax.fori_loop(1, place.chips, step, 0, unroll=True)

    def start(self):
        self.each(lambda chip: self.copy(chip, self.place.chip).start())

    def arrived(self):
        self.each(lambda chip: self.copy(chip, chip).wait_recv())

    def sent(self):
        self.each(lambda chip: self.copy(chip, self.place.chip).wait_send())


class Reduce:
    def __init__(self, place, pack, pair, summed, plane, part, line, sems):
        self.place, self.pack, self.pair, self.summed = place, pack, pair, summed
        self.plane, self.part, self.line, self.sems = plane, part, line, sems
        self.levels = place.chips // 4

    def pair_copy(self):
        place = self.place
        return remote(
            self.pack.at[1 - place.core], self.pair, self.sems.at[0], self.sems.at[1], place.chip, 1 - place.core
        )

    def plane_copy(self, way, coming=False):
        place = self.place
        corner = flip(place.corner, way)
        return remote(
            self.summed.at[corner], self.plane.at[corner if coming else place.corner],
            self.sems.at[2 + way], self.sems.at[6 + way], place.level * 4 + corner, place.core,
        )

    def line_copy(self, way, coming=False):
        place = self.place
        level = flip(place.level, way)
        return remote(
            self.part.at[level], self.line.at[level if coming else place.level],
            self.sems.at[10 + way], self.sems.at[10 + self.levels + way], level * 4 + place.corner, place.core,
        )

    def to_pair(self):
        self.pair_copy().start()

    def to_plane(self):
        self.pair_copy().wait_recv()
        place = self.place
        for way in (3, 1, 2, 0):
            corner = flip(place.corner, way)
            for level in range(self.levels):
                self.summed[corner, level] = low(
                    wide(self.pack[place.core, corner, level]) + wide(self.pair[corner, level])
                )
            if way:
                self.plane_copy(way).start()

    def to_line(self):
        place = self.place
        corners = [flip(place.corner, way) for way in (1, 2, 3)]
        for way in (1, 2, 3):
            self.plane_copy(way, True).wait_recv()
        for way in [*range(1, self.levels), 0]:
            level = flip(place.level, way)
            total = wide(self.summed[place.corner, level])
            for corner in corners:
                total = total + wide(self.plane[corner, level])
            self.part[level] = low(total)
            if way:
                self.line_copy(way).start()

    def total(self):
        place = self.place
        total = wide(self.part[place.level])
        for way in range(1, self.levels):
            self.line_copy(way, True).wait_recv()
            total = total + wide(self.line[flip(place.level, way)])
        return total

    def sent(self):
        self.pair_copy().wait_send()
        for way in (1, 2, 3):
            self.plane_copy(way).wait_send()
        for way in range(1, self.levels):
            self.line_copy(way).wait_send()


def rms_apply(values, gain_row):
    inverse = lax.rsqrt(jnp.mean(values * values, axis=-1, keepdims=True) + norm_eps)
    return values * inverse * gain_row, inverse


def rms_back(upstream, values, inverse, gain_row):
    unit = values * inverse
    gain_grad = jnp.sum(upstream * unit, axis=0, keepdims=True)
    scaled = upstream * gain_row
    inner = jnp.mean(scaled * unit, axis=-1, keepdims=True)
    return inverse * (scaled - unit * inner), gain_grad


GELU_A = math.sqrt(2.0 / math.pi)
GELU_B = 0.044715


def gelu_both(x):
    square = x * x
    curve = jnp.tanh(GELU_A * x * (1.0 + GELU_B * square))
    half = 0.5 * (1.0 + curve)
    slope = half + 0.5 * x * (1.0 - curve * curve) * (GELU_A * (1.0 + 3.0 * GELU_B * square))
    return x * half, slope


def pieces_of(values):
    first = wide(low(values))
    second = wide(low(values - first))
    return first, second, values - first - second


def step_kernel(sizes, *refs):
    (chips, rows_dev, seq_len, width, hidden, capacity, half_slots, key_rows) = sizes
    refs = list(refs)
    names = list(dict(ENDS)) + list(scratch_of(sizes))
    r = types.SimpleNamespace(**dict(zip(names, refs, strict=True)))
    place = Place(chips)
    chip, core = place.chip, place.core
    me = chip * 2 + core
    tokens = half_slots
    wa, wb, cand_buf, user_buf = r.wa, r.wb, r.cand, r.user
    gather_a = ShortGather(place, wa.at[core], r.wa_send, r.wa_recv)
    gather_b = ShortGather(place, wb.at[core], r.wb_send, r.wb_recv)
    gather_c = Gather(place, cand_buf, r.cand_send, r.cand_recv)
    gather_u = Gather(place, user_buf, r.user_send, r.user_recv)
    spread_corr = Scatter(place, None, r.corr, r.corr_send, r.corr_recv)
    spread_norm = Scatter(place, None, r.norm, r.norm_send, r.norm_recv)
    pair_a = to_sibling(place, wa.at[core], wa.at[core], r.wa_pair)
    pair_b = to_sibling(place, wb.at[core], wb.at[core], r.wb_pair)
    pair_emb = to_sibling(place, r.emb_pair.at[core], r.emb_pair.at[core], r.emb_sems)
    pair_corr = to_sibling(place, r.corr_pair.at[core], r.corr_pair.at[core], r.corr_sems)
    pair_user = to_sibling(place, r.user_pair.at[core], r.user_pair.at[core], r.user_sems)
    pair_soft = to_sibling(place, r.soft_out, r.soft_in, r.soft_sems)
    pair_cand = to_sibling(place, r.cand_out, r.cand_in, r.cand_sems)
    spread_sums = Scatter(place, None, r.scalar_buf, r.scalar_send, r.scalar_recv)
    pair_sums = to_sibling(place, r.scalar_pair.at[core], r.scalar_pair.at[core], r.sums_sems)

    barrier = pltpu.get_barrier_semaphore()
    table_copy = pltpu.make_async_copy(r.table, r.table_here, r.table_sem)
    table_copy.start()

    def greet(index, carry):
        other = lax.rem(chip + index, chips)
        pl.semaphore_signal(barrier, inc=1, device_id=(other, core), device_id_type=MESH_ID)
        return carry

    lax.fori_loop(1, chips, greet, 0, unroll=True)
    pl.semaphore_signal(barrier, inc=1, device_id=(chip, 1 - core), device_id_type=MESH_ID)

    turn = r.turn
    turn[...] = jnp.zeros_like(turn)
    turn[0:3, 0:8] = r.gains[...]
    gains_t = jnp.concatenate([jnp.transpose(turn[...])[0:8, :], jnp.zeros((8, width - 128), jnp.float32)], axis=1)
    pos_t = r.pos[...]
    wa[core, chip] = low(
        jnp.concatenate([r.qkv[...], gains_t, pos_t[:, :width], pos_t[:, width:]], axis=0)
    )
    narrow_t = r.narrow[...]
    wb[core, chip] = low(
        jnp.concatenate(
            [r.merge[...], r.widen[...]]
            + [narrow_t[:, i * width : (i + 1) * width] for i in range(hidden // width)]
            + [jnp.zeros((8, width), jnp.float32)],
            axis=0,
        )
    )

    low_table = r.low_table
    pad_rows = low_table.shape[0] - rows_dev
    low_table[pl.ds(rows_dev, pad_rows), :] = jnp.zeros((pad_rows, width), jnp.bfloat16)
    keys = r.keys
    keys[...] = jnp.zeros_like(keys)
    home = r.home[...]
    used = home.shape[0]
    keys[pl.ds(0, used), pl.ds(0, 128)] = wide(lax.div(home, 256))
    keys[pl.ds(0, used), pl.ds(128, 128)] = wide(lax.rem(home, 256))
    home_look = low(jnp.transpose(keys[:, 0:256]))
    ids_all = r.ids[:, pl.ds(pl.multiple_of(core * tokens, tokens), tokens)]
    lane_of = iota_of((128, tokens), 0)
    key_of = iota_of((key_rows, tokens), 0)

    def look(table_t, ids_row, parts):
        hot = low(wide(key_of == lax.div(ids_row, 128)))
        picked = dot_nn(table_t, hot)
        mask = lane_of == lax.rem(ids_row, 128)
        return [
            jnp.sum(jnp.where(mask, picked[128 * i : 128 * i + 128], 0.0), axis=0, keepdims=True)
            for i in range(parts)
        ]

    home_rows = []
    for d in range(chips):
        top, bottom = look(home_look, ids_all[d : d + 1, :], 2)
        home_rows.append(top * 256.0 + bottom)
    home_all = jnp.concatenate(home_rows, axis=0)
    r.home_all[...] = home_all

    pl.semaphore_wait(barrier, chips)
    gather_a.start()

    upper = low(wide(iota_of((tokens, tokens), 0) <= iota_of((tokens, tokens), 1)))
    first_row = wide(chip * rows_dev)
    local_all = home_all - first_row
    owned = (local_all >= 0.0) & (local_all < float(rows_dev))
    rank = dot_nn(low(wide(owned)), upper) - 1.0
    slot_rank = wide(iota_of((capacity, tokens), 0))
    wanted = []
    for d in range(chips):
        chosen = (rank[d : d + 1, :] == slot_rank) & owned[d : d + 1, :]
        wanted.append(
            jnp.sum(jnp.where(chosen, local_all[d : d + 1, :] + 1.0, 0.0), axis=1, keepdims=True) - 1.0
        )
    wanted = jnp.concatenate(wanted, axis=0)
    asked = chips * capacity
    lanes = low_table.shape[0]
    table_copy.wait()
    low_table[pl.ds(0, rows_dev), :] = low(r.table_here[...])
    hot_rows = low(wide(iota_of((asked, lanes), 1) == wanted.astype(jnp.int32)))
    out_rows = low(dot_nn(hot_rows, low_table[...])).reshape(chips, capacity, width)
    r.row_out[...] = out_rows
    r.row_in[chip] = r.row_out[chip]
    rows_there = Scatter(place, r.row_out, r.row_in, r.row_send, r.row_recv)
    rows_there.start()
    wanted_row = jnp.transpose(jnp.broadcast_to(wanted, (asked, 128)))[0:1, :]
    r.asked[core] = wanted_row
    asked_copy = remote(
        r.asked.at[core], r.asked.at[core], r.asked_send, r.asked_recv, chip, 1 - core
    )
    asked_copy.start()

    own_home = r.home_all[pl.ds(chip, 1), :]
    owner_first = wide(iota_of((chips, tokens), 0) * rows_dev)
    at_owner = (own_home >= owner_first) & (own_home < owner_first + float(rows_dev))
    own_rank = dot_nn(low(wide(at_owner)), upper) - 1.0
    spread = jnp.concatenate(
        [
            wide((own_rank[o : o + 1, :] == slot_rank) & at_owner[o : o + 1, :])
            for o in range(chips)
        ],
        axis=0,
    )
    r.spread[...] = low(spread)

    freq = r.freq[...]
    for i, piece in enumerate(pieces_of(freq)):
        keys[pl.ds(0, used), pl.ds(128 * i, 128)] = piece
    freq_look = low(jnp.transpose(keys[...]))
    own_ids = r.ids[pl.ds(chip, 1), pl.ds(pl.multiple_of(core * tokens, tokens), tokens)]
    fa, fb, fc = look(freq_look, own_ids, 3)
    own_length = r.lengths[chip]
    row_pos = core * tokens + iota_of((1, tokens), 1)
    is_cand = (row_pos >= 1) & (row_pos < own_length)
    own_corr = jnp.where(is_cand, fa + fb + fc, -big_negative)
    r.corr[chip] = own_corr
    r.corr_pair[core] = own_corr
    spread_corr.start()
    pair_corr.start()

    def turned(row):
        return jnp.transpose(jnp.broadcast_to(row, (128, tokens)))[:, 0:1]

    corr_col = turned(own_corr)
    r.corr_col[...] = jnp.broadcast_to(corr_col, (tokens, 128))

    total_events = jnp.float32(0.0)
    for d in range(chips):
        total_events = total_events + wide(r.lengths[d] - 1)
    col_pos = core * tokens + iota_of((tokens, 1), 0)
    is_event = col_pos + 1 < own_length

    gather_a.advance(3)
    gather_b.start()
    rows_there.arrived()
    embedded = low(dot_tn(r.spread[...], r.row_in[...].reshape(asked, width)))
    cand_buf[chip] = embedded
    r.emb_pair[core] = embedded
    gather_c.start()
    pair_emb.start()
    gather_a.complete()
    pair_a.start()
    gather_b.advance(3)
    pair_a.wait_recv()
    qkv_w, pos_w, gain_w = r.qkv_w, r.pos_w, r.gain_w

    def unpack_a(index, carry):
        one, two = wide(wa[0, index]), wide(wa[1, index])
        qkv_w[pl.ds(pl.multiple_of(index * 48, 16), 48), :] = low(jnp.concatenate([one[0:24], two[0:24]], axis=0))
        gain_w[pl.ds(pl.multiple_of(index * 16, 16), 16), :] = jnp.concatenate([one[24:32], two[24:32]], axis=0)[:, 0:128]
        early = jnp.concatenate([one[32:40], two[32:40]], axis=0)
        late = jnp.concatenate([one[40:48], two[40:48]], axis=0)
        pos_w[pl.ds(pl.multiple_of(index * 16, 16), 16), :] = jnp.where(core == 0, early, late)
        return carry

    lax.fori_loop(0, chips, unpack_a, 0)
    gain_rows = jnp.transpose(gain_w[...])[0:8, :]
    r.gain_rows[...] = gain_rows
    gain_one, gain_two, gain_three = (r.gain_rows[i : i + 1, :] for i in range(3))

    resid_zero = wide(cand_buf[chip]) + jnp.transpose(pos_w[...])
    r.resid_zero[...] = resid_zero
    normed, _ = rms_apply(resid_zero, gain_one)
    r.input_one[...] = low(normed)
    qkv_own = low(dot_nt(r.input_one[...], qkv_w[...]))
    kv = r.kv
    kv[0] = qkv_own[:, width : 3 * width]
    kv_copy = remote(kv.at[0], kv.at[1], r.kv_send, r.kv_recv, chip, 1 - core)
    kv_copy.start()

    kv_copy.wait_recv()

    head_dim = width // HEADS
    scaling = head_dim ** (-0.5)
    causal = iota_of((tokens, tokens), 1) <= iota_of((tokens, tokens), 0)
    other_bias = jnp.where(core == 0, big_negative, 0.0)
    head_lane = lax.div(iota_of((1, width), 1), head_dim)
    prob = r.prob
    zero_low = jnp.zeros((), jnp.bfloat16)
    both = 2 * tokens

    def of_head(values, head):
        return jnp.where(head_lane == head, values, zero_low)

    def rows_of(head, size=tokens):
        return slice(head * size, (head + 1) * size)

    def stack(to, values):
        for head in range(HEADS):
            to[rows_of(head), :] = of_head(values, head)

    def stack_pair(to, pair, lanes):
        for head in range(HEADS):
            to[rows_of(2 * head), :] = of_head(pair[0, :, lanes], head)
            to[rows_of(2 * head + 1), :] = of_head(pair[1, :, lanes], head)

    stack(r.query_rows, qkv_own[:, 0:width])
    stack_pair(r.value_rows, kv, slice(width, 2 * width))

    def attend(head):
        query = r.query_rows[rows_of(head), :]
        own = dot_nt(query, kv[0, :, 0:width]) * scaling
        own = jnp.where(causal, own, big_negative)
        other = dot_nt(query, kv[1, :, 0:width]) * scaling + other_bias
        peak = jnp.max(jnp.maximum(own, other), axis=-1, keepdims=True)
        own = jnp.exp(own - peak)
        other = jnp.exp(other - peak)
        share = 1.0 / jnp.sum(own + other, axis=-1, keepdims=True)
        own = own * share
        other = other * share
        prob[head, :, 0:tokens] = own
        prob[head, :, tokens:both] = other
        own, other = low(own), low(other)
        r.prob_own[rows_of(head), :] = own
        r.prob_other[rows_of(head), :] = other
        r.prob_lanes[:, rows_of(2 * head)] = own
        r.prob_lanes[:, rows_of(2 * head + 1)] = other

    gather_c.advance(1)
    for head in range(HEADS):
        attend(head)
    gather_b.complete()
    pair_b.start()
    gather_c.advance(2)
    pair_b.wait_recv()
    merge_w, widen_w, narrow_w = r.merge_w, r.widen_w, r.narrow_w

    def unpack_b(index, carry):
        one, two = wide(wb[0, index]), wide(wb[1, index])
        at16 = pl.ds(pl.multiple_of(index * 16, 16), 16)
        merge_w[at16, :] = low(jnp.concatenate([one[0:8], two[0:8]], axis=0))
        widen_w[pl.ds(pl.multiple_of(index * 64, 16), 64), :] = low(jnp.concatenate([one[8:40], two[8:40]], axis=0))
        for i in range(hidden // width):
            top = 40 + 8 * i
            narrow_w[at16, pl.ds(i * width, width)] = low(
                jnp.concatenate([one[top : top + 8], two[top : top + 8]], axis=0)
            )
        return carry

    lax.fori_loop(0, chips, unpack_b, 0)
    r.attended[...] = low(dot_nn(r.prob_lanes[...], r.value_rows[...]))
    resid_one = r.resid_zero[...] + dot_nt(r.attended[...], merge_w[...])
    r.resid_one[...] = resid_one
    normed, _ = rms_apply(resid_one, gain_two)
    r.input_two[...] = low(normed)
    r.resid_two[...] = resid_one
    for i in range(hidden // FF_CHUNK):
        part = slice(i * FF_CHUNK, (i + 1) * FF_CHUNK)
        act, slope = gelu_both(dot_nt(r.input_two[...], widen_w[part, :]))
        r.act[:, part] = low(act)
        r.slope[:, part] = slope
    r.resid_two[...] += dot_nt(r.act[...], narrow_w[...])
    normed, _ = rms_apply(r.resid_two[...], gain_three)
    user_buf[chip] = low(normed)
    r.user_pair[core] = user_buf[chip]
    gather_u.start()
    pair_user.start()

    gather_c.advance(2)
    spread_corr.arrived()
    pair_emb.wait_recv()
    pair_corr.wait_recv()
    shifted = jnp.concatenate([wide(cand_buf[chip])[1:, :], wide(r.emb_pair[1, pl.ds(0, 16), :])[0:1, :]], axis=0)
    target_corr = jnp.concatenate([corr_col[1:, :], r.corr_pair[1][:, 0:1]], axis=0)
    target_logit = jnp.sum(wide(user_buf[chip]) * shifted, axis=-1, keepdims=True) - target_corr
    target_logit = jnp.where(is_event, target_logit, 0.0)
    pair_user.wait_recv()
    users = r.user_pair[...].reshape(2 * tokens, width)
    logit_buf, peaks, totals, acc = r.logit, r.peaks, r.totals, r.acc
    totals[...] = jnp.zeros_like(totals)
    acc[...] = jnp.zeros_like(acc)
    group = chips // CHUNKS
    pair_row = iota_of((both, tokens), 0)
    pair_col = core * tokens + iota_of((both, tokens), 1)

    def fold(values, how):
        parts = [values[:, i : i + 128] for i in range(0, values.shape[1], 128)]
        return functools.reduce(how, parts)

    peak = jnp.full((both, 1), big_negative, jnp.float32)
    for chunk in range(CHUNKS):
        gather_c.advance(1)
        gather_c.need(range(group * chunk, group * (chunk + 1)))
        peaks[...] = jnp.broadcast_to(peak, peaks.shape)

        steps = range(chunk * group, (chunk + 1) * group)
        for index, step in enumerate(steps):
            there = place.relative(step)
            logits = dot_nt(users, cand_buf[there]) - r.corr[there]
            logit_buf[index] = logits
            peaks[...] = jnp.maximum(peaks[...], fold(logits, jnp.maximum))
        before, peak = peak, jnp.max(peaks[...], axis=-1, keepdims=True)
        scale = jnp.exp(before - peak)
        totals[...] *= scale
        acc[...] *= scale
        gather_u.advance((1, 2, 2, 1)[chunk])

        for index, step in enumerate(steps):
            expo = jnp.exp(logit_buf[index] - peak)
            totals[...] += fold(expo, jnp.add)
            if step == 0:
                expo = jnp.where(pair_col == pair_row + 1, 0.0, expo)
            acc[...] += dot_nn(low(expo), cand_buf[place.relative(step)])
    total = jnp.sum(totals[...], axis=-1, keepdims=True)
    peaks[...] = jnp.broadcast_to(peak, peaks.shape)
    totals[...] = jnp.broadcast_to(total, totals.shape)
    own_rows = pl.ds(pl.multiple_of(core * tokens, tokens), tokens)
    other_rows = pl.ds(pl.multiple_of((1 - core) * tokens, tokens), tokens)
    soft_out, soft_in = r.soft_out, r.soft_in
    soft_out[:, 0:width] = acc[other_rows, :]
    soft_out[:, width : width + 128] = peaks[other_rows, :]
    soft_out[:, width + 128 : width + 256] = totals[other_rows, :]
    pair_soft.start()
    pair_soft.wait_recv()
    own_peak, own_total = peaks[own_rows, :][:, 0:1], totals[own_rows, :][:, 0:1]
    other_peak = soft_in[:, width : width + 1]
    peak = jnp.maximum(own_peak, other_peak)
    own_scale, other_scale = jnp.exp(own_peak - peak), jnp.exp(other_peak - peak)
    total = own_total * own_scale + soft_in[:, width + 128 : width + 129] * other_scale
    soft = acc[own_rows, :] * own_scale + soft_in[:, 0:width] * other_scale
    log_total = peak + jnp.log(total)
    loss_own = jnp.sum(jnp.where(is_event, log_total - target_logit, 0.0), axis=0, keepdims=True)
    weight = jnp.where(is_event, 1.0 / total_events, 0.0)
    target_coef = wide(low(weight * (jnp.exp(target_logit - log_total) - 1.0)))
    user_grad = soft * (weight / total) + target_coef * shifted
    shift_col = jnp.where(is_event, log_total + jnp.log(total_events), -big_negative)
    norm_buf = r.norm
    norm_buf[chip] = jnp.transpose(jnp.broadcast_to(shift_col, (tokens, 128)))[0:1, :]
    spread_norm.start()
    grad_two, gain_grad_three = rms_back(
        user_grad, r.resid_two[...],
        lax.rsqrt(jnp.mean(r.resid_two[...] * r.resid_two[...], axis=-1, keepdims=True) + norm_eps),
        gain_three,
    )
    branch_two = low(grad_two)
    narrow_grad = dot_tn(branch_two, r.act[...])
    r.pre[...] = low(dot_nn(branch_two, narrow_w[...]) * r.slope[...])
    widen_grad = dot_tn(r.pre[...], r.input_two[...])
    resid_one = r.resid_one[...]
    inverse_two = lax.rsqrt(jnp.mean(resid_one * resid_one, axis=-1, keepdims=True) + norm_eps)
    from_two, gain_grad_two = rms_back(dot_nn(r.pre[...], widen_w[...]), resid_one, inverse_two, gain_two)
    grad_one = grad_two + from_two
    r.grad_one[...] = grad_one
    branch_one = low(grad_one)
    merge_grad = dot_tn(branch_one, r.attended[...])
    r.mixed[...] = low(dot_nn(branch_one, merge_w[...]))

    tail, head_pack = r.tail_pack, r.head_pack
    for d in range(2 * chips):
        at = (d % 2, d // 2 % 4, d // 8)
        tail[*at, pl.ds(0, 32), :] = low(widen_grad[32 * d : 32 * d + 32])
        tail[*at, pl.ds(32, 32), :] = low(
            jnp.concatenate(
                [
                    narrow_grad[8 * d : 8 * d + 8, i * width : (i + 1) * width]
                    for i in range(hidden // width)
                ],
                axis=0,
            )
        )
    reduce_tail = Reduce(place, tail, r.tail_pair, r.tail_sum, r.tail_plane, r.tail_part, r.tail_line, r.tail_sems)
    reduce_head = Reduce(place, head_pack, r.head_pair, r.head_sum, r.head_plane, r.head_part, r.head_line, r.head_sems)
    reduce_tail.to_pair()
    gather_u.advance(1)
    stack(r.mixed_rows, r.mixed[...])
    stack_pair(r.key_rows, kv, slice(0, width))

    def attend_back(head):
        mixed = r.mixed_rows[rows_of(head), :]
        own, other = prob[head, :, 0:tokens], prob[head, :, tokens:both]
        own_grad = dot_nt(mixed, kv[0, :, width : 2 * width])
        other_grad = dot_nt(mixed, kv[1, :, width : 2 * width])
        inner = jnp.sum(own * own_grad + other * other_grad, axis=-1, keepdims=True)
        own_score = low(own * (own_grad - inner))
        other_score = low(other * (other_grad - inner))
        r.score_own[rows_of(head), :] = own_score
        r.score_other[rows_of(head), :] = other_score
        r.score_lanes[:, rows_of(2 * head)] = own_score
        r.score_lanes[:, rows_of(2 * head + 1)] = other_score

    for head in range(HEADS):
        attend_back(head)
        if head == 1:
            gather_u.advance(1)
        if head == 3:
            reduce_tail.to_plane()
            gather_u.advance(1)
        if head == 5:
            gather_u.advance(1)
    back = r.back
    back[0, :, 0:width] = low(dot_tn(r.score_other[...], r.query_rows[...]) * scaling)
    back[0, :, width : 2 * width] = low(dot_tn(r.prob_other[...], r.mixed_rows[...]))
    back_copy = remote(back.at[0], back.at[1], r.back_send, r.back_recv, chip, 1 - core)
    back_copy.start()
    qkv_grad = r.qkv_grad
    qkv_grad[:, 0:width] = low(dot_nn(r.score_lanes[...], r.key_rows[...]) * scaling)
    key_own = dot_tn(r.score_own[...], r.query_rows[...]) * scaling
    value_own = dot_tn(r.prob_own[...], r.mixed_rows[...])
    back_copy.wait_recv()
    qkv_grad[:, width : 2 * width] = low(key_own + wide(back[1, :, 0:width]))
    qkv_grad[:, 2 * width : 3 * width] = low(value_own + wide(back[1, :, width : 2 * width]))
    qkv_wgrad = dot_tn(qkv_grad[...], r.input_one[...])
    resid_zero = r.resid_zero[...]
    inverse_one = lax.rsqrt(jnp.mean(resid_zero * resid_zero, axis=-1, keepdims=True) + norm_eps)
    from_one, gain_grad_one = rms_back(dot_nn(qkv_grad[...], qkv_w[...]), resid_zero, inverse_one, gain_one)
    resid_grad = r.grad_one[...] + from_one
    r.resid_grad[...] = resid_grad
    pos_grad = jnp.transpose(resid_grad)
    nothing = jnp.zeros((8, width), jnp.float32)
    for d in range(2 * chips):
        at = (d % 2, d // 2 % 4, d // 8)
        head_pack[*at, pl.ds(0, 32), :] = low(
            jnp.concatenate([qkv_wgrad[24 * d : 24 * d + 24], merge_grad[8 * d : 8 * d + 8]], axis=0)
        )
        pos_piece = pos_grad[8 * d : 8 * d + 8]
        head_pack[*at, pl.ds(32, 16), :] = low(
            jnp.concatenate(
                [jnp.where(core == 0, pos_piece, nothing), jnp.where(core == 0, nothing, pos_piece)], axis=0
            )
        )
    reduce_head.to_pair()
    gain_buf = r.gain_buf
    gain_buf[chip] = jnp.concatenate([gain_grad_one, gain_grad_two, gain_grad_three], axis=1)
    gain_there = Scatter(place, None, gain_buf, r.gain_send, r.gain_recv)
    gain_there.start()
    gather_u.complete()
    spread_norm.arrived()
    both_corr = jnp.concatenate([turned(r.corr_pair[0]), turned(r.corr_pair[1])], axis=0)
    event_row = jnp.where(row_pos + 1 < own_length, 1.0 / total_events, 0.0)

    r.corr_both[...] = jnp.broadcast_to(both_corr, r.corr_both.shape)

    def give_blocks(half, sums):
        rows = r.emb_pair[half]
        corr = r.corr_both[pl.ds(pl.multiple_of(half * tokens, tokens), tokens), :][:, 0:1]
        row = half * tokens + iota_of((tokens, tokens), 0)
        col = core * tokens + iota_of((tokens, tokens), 1)
        for step in range(chips):
            block_rows = user_buf[place.relative(step)]
            coef = jnp.exp((dot_nt(rows, block_rows) - corr) - norm_buf[place.relative(step)])
            if step == 0:
                coef = coef - jnp.where((row == col + 1) & (corr < 1e29), event_row, 0.0)
                sums[...] = dot_nn(low(coef), block_rows)
            else:
                sums[...] += dot_nn(low(coef), block_rows)

    give_blocks(1 - core, r.cand_out)
    pair_cand.start()
    give_blocks(core, r.cand_own)
    reduce_head.to_plane()
    pair_cand.wait_recv()

    emb_grad = low(r.resid_grad[...] + (r.cand_own[...] + r.cand_in[...]))
    back_out, back_in = r.back_out, r.back_in
    back_out[...] = low(dot_nn(r.spread[...], emb_grad)).reshape(chips, capacity, width)
    back_in[core, chip] = back_out[chip]
    rows_back = Scatter(place, back_out, back_in.at[core], r.rows_send, r.rows_recv)
    rows_back.start()
    reduce_tail.to_line()
    asked_copy.wait_recv()
    asked_all = jnp.concatenate([r.asked[0], r.asked[1]], axis=1).astype(jnp.int32)
    part_rows = TABLE_PART if rows_dev % TABLE_PART == 0 else 8
    parts = [pl.ds(first, part_rows) for first in range(0, rows_dev, part_rows)]
    for part in parts:
        r.hot[part, :] = low(wide(iota_of((part_rows, 2 * asked), 0) + part.start == asked_all))

    reduce_head.to_line()
    shard = r.shard_grad
    shard[0:64] = reduce_tail.total()
    shard[64:112] = reduce_head.total()
    total = shard[...]
    gain_there.arrived()
    gain_total = gain_buf[0]
    for step in range(1, chips):
        gain_total = gain_total + gain_buf[step]
    gain_pair = r.gain_pair
    gain_pair[core] = gain_total
    gain_copy = remote(gain_pair.at[core], gain_pair.at[core], r.gp_send, r.gp_recv, chip, 1 - core)
    gain_copy.start()
    gain_copy.wait_recv()
    gain_total = gain_pair[0] + gain_pair[1]
    gain_three_rows = [gain_total[:, i * width : (i + 1) * width] for i in range(3)]
    gain_w[:, 0:8] = jnp.transpose(jnp.concatenate(gain_three_rows + [jnp.zeros((5, width), jnp.float32)], axis=0))
    r.gain_grad[...] = gain_w[pl.ds(pl.multiple_of(me * 8, 8), 8), :]
    gain_lane = iota_of((1, 3 * width), 1)
    gain_mine = lax.div(lax.rem(gain_lane, width), 8) == me
    square = jnp.sum(total * total, axis=0, keepdims=True)
    square = jnp.sum(square, axis=1, keepdims=True)
    square = square + jnp.sum(jnp.where(gain_mine, gain_total * gain_total, 0.0), axis=1, keepdims=True)
    lane = iota_of((1, 128), 1)
    r.scalar_pair[core] = jnp.where(lane == 0, square, jnp.where(lane == 1, loss_own, 0.0))
    pair_sums.start()

    rows_back.arrived()
    rows_pair = remote(back_in.at[core], back_in.at[core], r.rp_send, r.rp_recv, chip, 1 - core)
    rows_pair.start()
    rows_pair.wait_recv()
    table_grad = r.table_grad
    incoming = back_in[...].reshape(2 * asked, width)
    table_square = jnp.zeros((1, width), jnp.float32)
    for part in parts:
        grads = dot_nn(r.hot[part, :], incoming)
        table_grad[part, :] = grads
        table_square = table_square + jnp.sum(grads * grads, axis=0, keepdims=True)
    square = jnp.sum(table_square, axis=1, keepdims=True)

    scalar_buf = r.scalar_buf
    pair_sums.wait_recv()
    scalar_buf[chip] = r.scalar_pair[0] + r.scalar_pair[1] + jnp.where(lane == 0, square, 0.0)
    spread_sums.start()
    gather_a.sent()
    gather_b.sent()
    gather_c.sent()
    gather_u.sent()
    rows_there.sent()
    rows_back.sent()
    gain_there.sent()
    spread_corr.sent()
    spread_norm.sent()
    reduce_tail.sent()
    reduce_head.sent()
    pairs = (pair_a, pair_b, pair_emb, pair_corr, pair_user, pair_soft, pair_cand, pair_sums)
    for copy in (asked_copy, kv_copy, back_copy, gain_copy, rows_pair, *pairs):
        copy.wait_send()
    spread_sums.arrived()
    sums = scalar_buf[0]
    for d in range(1, chips):
        sums = sums + scalar_buf[d]
    r.sums[...] = jnp.where(lane == 2, total_events, sums)
    spread_sums.sent()


TABLE_PART = 224
CHUNKS = 4
ENDS = dict(
    ids=0, lengths=0, home=0, freq=0, table=0, pos=0, qkv=0, merge=0, widen=0, narrow=0, gains=0,
    table_grad=1, shard_grad=1, gain_grad=1, sums=1,
)


def scratch_of(sizes):
    (chips, rows_dev, seq_len, width, hidden, capacity, tokens, key_rows) = sizes
    f32, b16 = jnp.float32, jnp.bfloat16
    devices, levels = 2 * chips, chips // 4
    dma = pltpu.SemaphoreType.DMA
    lanes = -(-rows_dev // 128) * 128
    if lanes == rows_dev:
        lanes += 128
    sends = Gather.sends(chips)
    shapes = dict(
        table_here=pltpu.VMEM((rows_dev, width), f32),
        table_sem=dma,
        wa=pltpu.VMEM((2, chips, 48, width), b16),
        wb=pltpu.VMEM((2, chips, 80, width), b16),
        cand=pltpu.VMEM((chips, tokens, width), b16),
        corr=pltpu.VMEM((chips, 1, tokens), f32),
        logit=pltpu.VMEM((chips // CHUNKS, 2 * tokens, tokens), f32),
        user=pltpu.VMEM((chips, tokens, width), b16),
        emb_pair=pltpu.VMEM((2, tokens, width), b16),
        corr_pair=pltpu.VMEM((2, 1, tokens), f32),
        user_pair=pltpu.VMEM((2, tokens, width), b16),
        soft_out=pltpu.VMEM((tokens, width + 256), f32),
        soft_in=pltpu.VMEM((tokens, width + 256), f32),
        cand_out=pltpu.VMEM((tokens, width), f32),
        cand_in=pltpu.VMEM((tokens, width), f32),
        cand_own=pltpu.VMEM((tokens, width), f32),
        corr_both=pltpu.VMEM((2 * tokens, 128), f32),
        wa_pair=dma((2,)), wb_pair=dma((2,)), emb_sems=dma((2,)), corr_sems=dma((2,)),
        user_sems=dma((2,)), soft_sems=dma((2,)), cand_sems=dma((2,)),
        low_table=pltpu.VMEM((lanes, width), b16),
        keys=pltpu.VMEM((key_rows, 384), f32),
        home_all=pltpu.VMEM((chips, tokens), f32),
        row_out=pltpu.VMEM((chips, capacity, width), b16),
        row_in=pltpu.VMEM((chips, capacity, width), b16),
        asked=pltpu.VMEM((2, 1, chips * capacity), f32),
        spread=pltpu.VMEM((chips * capacity, tokens), b16),
        corr_col=pltpu.VMEM((tokens, 128), f32),
        qkv_w=pltpu.VMEM((3 * width, width), b16),
        pos_w=pltpu.VMEM((width, tokens), f32),
        gain_w=pltpu.VMEM((width, 128), f32),
        turn=pltpu.VMEM((128, 128), f32),
        gain_rows=pltpu.VMEM((8, width), f32),
        merge_w=pltpu.VMEM((width, width), b16),
        widen_w=pltpu.VMEM((hidden, width), b16),
        narrow_w=pltpu.VMEM((width, hidden), b16),
        resid_zero=pltpu.VMEM((tokens, width), f32),
        resid_one=pltpu.VMEM((tokens, width), f32),
        resid_two=pltpu.VMEM((tokens, width), f32),
        input_one=pltpu.VMEM((tokens, width), b16),
        input_two=pltpu.VMEM((tokens, width), b16),
        query_rows=pltpu.VMEM((HEADS * tokens, width), b16),
        mixed_rows=pltpu.VMEM((HEADS * tokens, width), b16),
        key_rows=pltpu.VMEM((2 * HEADS * tokens, width), b16),
        value_rows=pltpu.VMEM((2 * HEADS * tokens, width), b16),
        prob_own=pltpu.VMEM((HEADS * tokens, tokens), b16),
        prob_other=pltpu.VMEM((HEADS * tokens, tokens), b16),
        prob_lanes=pltpu.VMEM((tokens, 2 * HEADS * tokens), b16),
        score_own=pltpu.VMEM((HEADS * tokens, tokens), b16),
        score_other=pltpu.VMEM((HEADS * tokens, tokens), b16),
        score_lanes=pltpu.VMEM((tokens, 2 * HEADS * tokens), b16),
        kv=pltpu.VMEM((2, tokens, 2 * width), b16),
        prob=pltpu.VMEM((HEADS, tokens, 2 * tokens), f32),
        acc=pltpu.VMEM((2 * tokens, width), f32),
        attended=pltpu.VMEM((tokens, width), b16),
        act=pltpu.VMEM((tokens, hidden), b16),
        slope=pltpu.VMEM((tokens, hidden), f32),
        pre=pltpu.VMEM((tokens, hidden), b16),
        peaks=pltpu.VMEM((2 * tokens, 128), f32),
        totals=pltpu.VMEM((2 * tokens, 128), f32),
        norm=pltpu.VMEM((chips, 1, tokens), f32),
        grad_one=pltpu.VMEM((tokens, width), f32),
        mixed=pltpu.VMEM((tokens, width), b16),
        tail_pack=pltpu.VMEM((2, 4, levels, 64, width), b16),
        tail_pair=pltpu.VMEM((4, levels, 64, width), b16),
        tail_sum=pltpu.VMEM((4, levels, 64, width), b16),
        tail_plane=pltpu.VMEM((4, levels, 64, width), b16),
        tail_part=pltpu.VMEM((levels, 64, width), b16),
        tail_line=pltpu.VMEM((levels, 64, width), b16),
        tail_sems=dma((10 + 2 * levels,)),
        head_pack=pltpu.VMEM((2, 4, levels, 48, width), b16),
        head_pair=pltpu.VMEM((4, levels, 48, width), b16),
        head_sum=pltpu.VMEM((4, levels, 48, width), b16),
        head_plane=pltpu.VMEM((4, levels, 48, width), b16),
        head_part=pltpu.VMEM((levels, 48, width), b16),
        head_line=pltpu.VMEM((levels, 48, width), b16),
        head_sems=dma((10 + 2 * levels,)),
        back=pltpu.VMEM((2, tokens, 2 * width), b16),
        qkv_grad=pltpu.VMEM((tokens, 3 * width), b16),
        resid_grad=pltpu.VMEM((tokens, width), f32),
        gain_buf=pltpu.VMEM((chips, 1, 3 * width), f32),
        gain_pair=pltpu.VMEM((2, 1, 3 * width), f32),
        back_out=pltpu.VMEM((chips, capacity, width), b16),
        back_in=pltpu.VMEM((2, chips, capacity, width), b16),
        hot=pltpu.VMEM((rows_dev, 2 * chips * capacity), b16),
        scalar_buf=pltpu.VMEM((chips, 1, 128), f32),
        scalar_pair=pltpu.VMEM((2, 1, 128), f32),
        sums_sems=dma((2,)),
        wa_send=dma((sends,)), wa_recv=dma((chips,)),
        wb_send=dma((sends,)), wb_recv=dma((chips,)),
        cand_send=dma((sends,)), cand_recv=dma((chips,)),
        user_send=dma((sends,)), user_recv=dma((chips,)),
        row_send=dma((chips,)), row_recv=dma((chips,)),
        rows_send=dma((chips,)), rows_recv=dma((chips,)),
        gain_send=dma((chips,)), gain_recv=dma((chips,)),
        norm_send=dma((chips,)), norm_recv=dma((chips,)),
        corr_send=dma((chips,)), corr_recv=dma((chips,)),
        scalar_send=dma((chips,)), scalar_recv=dma((chips,)),
        asked_send=dma, asked_recv=dma,
        kv_send=dma, kv_recv=dma,
        back_send=dma, back_recv=dma,
        gp_send=dma, gp_recv=dma,
        rp_send=dma, rp_recv=dma,
    )
    return shapes


def adam(weight, first, second, grad, rate):
    first = beta_one * first + (1.0 - beta_one) * grad
    second = beta_two * second + (1.0 - beta_two) * grad * grad
    fix_one = 1.0 - beta_one**STEP
    fix_two = 1.0 - beta_two**STEP
    update = first / fix_one / (jnp.sqrt(second / fix_two) + adam_eps) + decay_rate * weight
    return weight - rate * update, first, second


def update_kernel(*refs):
    (table_grad, shard, gain_grad, sums), refs = refs[:4], refs[4:]
    ins, outs, turn = refs[:21], refs[21:-1], refs[-1]
    square = sums[0:1, 0:1]
    norm = jnp.sqrt(square)
    factor = jnp.minimum(1.0, clip_limit / norm)

    def update(index, grad, rate):
        new = adam(*(ref[...] for ref in ins[3 * index : 3 * index + 3]), grad * factor, rate)
        for ref, value in zip(outs[3 + 3 * index : 6 + 3 * index], new):
            ref[...] = value

    update(0, table_grad[...], learn_rate)

    @pl.when(pl.program_id(0) == 0)
    def _():
        outs[0][...] = sums[0:1, 1:2]
        outs[1][...] = sums[0:1, 2:3]
        outs[2][...] = norm
        update(1, jnp.concatenate([shard[96:104, :], shard[104:112, :]], axis=1), learn_rate)
        update(2, shard[64:88, :], learn_rate)
        update(3, shard[88:96, :], learn_rate)
        update(4, shard[0:32, :], learn_rate)
        update(5, jnp.concatenate([shard[32 + 8 * i : 40 + 8 * i, :] for i in range(4)], axis=1), learn_rate)
        turn[0:8, :] = gain_grad[...]
        update(6, jnp.transpose(turn[...])[0:3, 0:8], gain_rate)


def fused_body(*args):
    (item_ids, lengths, home_row, log_freq) = args[:4]
    weights = args[4:]
    item_table = weights[0]
    rows_dev, width = item_table.shape
    chips = lax.axis_size("dp")
    seq_len = item_ids.shape[1]
    tokens = seq_len // 2
    hidden = weights[12].shape[1] * 2 * chips
    capacity = 2 * tokens // chips
    key_rows = -(-home_row.shape[0] // (128 * 128)) * 128
    sizes = (chips, rows_dev, seq_len, width, hidden, capacity, tokens, key_rows)
    dense = [w.T for w in weights[3:18]]
    shapes = scratch_of(sizes)
    vmem = pl.BlockSpec(memory_space=pltpu.VMEM)
    smem = pl.BlockSpec(memory_space=pltpu.SMEM)
    f32 = jnp.float32
    table_grad, shard, gain_grad, sums = pl.pallas_call(
        functools.partial(step_kernel, sizes),
        out_shape=[
            jax.ShapeDtypeStruct((rows_dev, width), f32),
            jax.ShapeDtypeStruct((112, width), f32),
            jax.ShapeDtypeStruct((8, 128), f32),
            jax.ShapeDtypeStruct((1, 128), f32),
        ],
        in_specs=[vmem, smem, vmem, vmem, pl.BlockSpec(memory_space=pl.ANY)] + [vmem] * 6,
        out_specs=[vmem] * 4,
        scratch_shapes=list(shapes.values()),
        compiler_params=pltpu.CompilerParams(
            collective_id=0, has_side_effects=True, vmem_limit_bytes=60 * 2**20
        ),
    )(
        item_ids, lengths, home_row.reshape(-1, 128), log_freq.reshape(-1, 128), item_table,
        dense[0], dense[3], dense[6], dense[9], dense[12], weights[18],
    )
    part = rows_dev // 2 if rows_dev % 16 == 0 else rows_dev
    table_spec = pl.BlockSpec((part, width), lambda i: (i, 0))

    def whole(x):
        return pl.BlockSpec(x.shape, lambda i: (0,) * len(x.shape))

    small = dense + [weights[18], weights[19], weights[20]]
    one = jax.ShapeDtypeStruct((1, 1), f32)
    outs = pl.pallas_call(
        update_kernel,
        grid=(rows_dev // part,),
        out_shape=[one] * 3 + [jax.ShapeDtypeStruct(x.shape, f32) for x in list(weights[:3]) + small],
        in_specs=[table_spec, whole(shard), whole(gain_grad), whole(sums)] + [table_spec] * 3 + [whole(x) for x in small],
        out_specs=[whole(one)] * 3 + [table_spec] * 3 + [whole(x) for x in small],
        scratch_shapes=[pltpu.VMEM((128, 128), f32)],
        compiler_params=pltpu.CompilerParams(vmem_limit_bytes=60 * 2**20),
    )(table_grad, shard, gain_grad, sums, *weights[:3], *small)
    outs = list(outs)
    return tuple(
        [x.reshape(()) for x in outs[:3]] + outs[3:6] + [x.T for x in outs[6:21]] + outs[21:]
    )


def solution(mesh):
    placed = (
        P(),
        P(),
        P(),
        P(),
        P("dp", None),
        P("dp", None),
        P("dp", None),
        P(None, ("dp", "sub")),
        P(None, ("dp", "sub")),
        P(None, ("dp", "sub")),
        P(None, ("dp", "sub")),
        P(None, ("dp", "sub")),
        P(None, ("dp", "sub")),
        P(None, ("dp", "sub")),
        P(None, ("dp", "sub")),
        P(None, ("dp", "sub")),
        P(None, ("dp", "sub")),
        P(None, ("dp", "sub")),
        P(None, ("dp", "sub")),
        P(None, ("dp", "sub")),
        P(None, ("dp", "sub")),
        P(None, ("dp", "sub")),
        P(None, ("dp", "sub")),
        P(None, ("dp", "sub")),
        P(None, ("dp", "sub")),
    )
    fits = mesh.shape["sub"] == 2 and mesh.shape["dp"] == 16
    return jax.shard_map(
        fused_body if fits else body,
        mesh=mesh,
        in_specs=placed,
        out_specs=(
            P(),
            P(),
            P(),
            P("dp", None),
            P("dp", None),
            P("dp", None),
            P(None, ("dp", "sub")),
            P(None, ("dp", "sub")),
            P(None, ("dp", "sub")),
            P(None, ("dp", "sub")),
            P(None, ("dp", "sub")),
            P(None, ("dp", "sub")),
            P(None, ("dp", "sub")),
            P(None, ("dp", "sub")),
            P(None, ("dp", "sub")),
            P(None, ("dp", "sub")),
            P(None, ("dp", "sub")),
            P(None, ("dp", "sub")),
            P(None, ("dp", "sub")),
            P(None, ("dp", "sub")),
            P(None, ("dp", "sub")),
            P(None, ("dp", "sub")),
            P(None, ("dp", "sub")),
            P(None, ("dp", "sub")),
        ),
        check_vma=False,
    )
```
